32 devices in a mesh: seq: 8 (over z, x), chan: 4 (over y, core).
Axes of the slice: x: 2, y: 2, z: 4, core: 2. Of those that a mesh axis runs over, the one named last changes fastest.
Arguments:
- tokens: bfloat16 [2048, 4096], P('seq', 'chan'), may hold values from -6 to 6
- in_weight: bfloat16 [4096, 3, 4096], P('seq', None, 'chan'), may hold values from -0.09375 to 0.09375
- short_taps: float32 [3, 3, 4096], P(None, None, 'chan'), may hold values from -3 to 3
- skip_gain: float32 [4096], P('chan'), may hold values from 0.5 to 1.5
- long_filter: bfloat16 [2048, 4096], P('seq', 'chan'), may hold values from -1.1 to 1.1
- out_weight: bfloat16 [4096, 4096], P('chan'), may hold values from -0.125 to 0.125
Outputs:
- mixed_out: bfloat16 [2048, 4096], P('seq', 'chan')
The draws below stay inside these ranges and needn't reach their ends.
All inputs are finite; a program needn't handle non-finite values.
Results may differ from the reference program's by a relative error of at most 0.023.
Values may be sent and summed in bfloat16 or wider, within the bound.
No kernel may reach another device: no remote copies, remote signals or barrier semaphores. Data moves between devices by JAX's collectives and lax.ppermute only.
A program may use at most 128 MiB of HBM per device.

```python
import jax
import jax.numpy as jnp

D = 4096
TAPS = 3
CONTEXT_SPAN = 2048


def draw_long_filter(key, part):
    key = jax.random.fold_in(key, 11)
    prng_seeds = jax.random.split(key, 5)
    lag_indices = jnp.arange(CONTEXT_SPAN, dtype=jnp.float32)[:, None]
    slow_flag = jax.random.uniform(prng_seeds[0], (D,)) < 0.5
    slow_rates = jnp.exp(jax.random.uniform(prng_seeds[1], (D,), jnp.float32, jnp.log(0.3 / CONTEXT_SPAN), jnp.log(2.3 / CONTEXT_SPAN)))
    fast_rates = jnp.exp(jax.random.uniform(prng_seeds[3], (D,), jnp.float32, jnp.log(2.3 / CONTEXT_SPAN), jnp.log(1.0 / 30.0)))
    fading_speeds = jnp.where(slow_flag, slow_rates, fast_rates)
    noise = jnp.clip(jax.random.normal(prng_seeds[2], (CONTEXT_SPAN, D), jnp.float32), -4.0, 4.0)
    spike_offset = jax.random.randint(prng_seeds[4], (3,), 0, CONTEXT_SPAN).astype(jnp.float32)
    spike_number = jnp.sum((lag_indices[:, :, None] >= spike_offset[None, None, :]).astype(jnp.float32), axis=2)
    fading_profile = jnp.exp(-fading_speeds[None, :] * lag_indices) * jnp.power(0.6, spike_number)
    scaling = jnp.sqrt(1.0 - jnp.exp(-2.0 * fading_speeds))[None, :]
    return (noise * fading_profile * scaling).astype(jnp.bfloat16)


def raised(values, own_key, source, target, parts, factor):
    owner, partner = [(jnp.arange(values.shape[position]) // (values.shape[position] // parts)).reshape([-1 if axis == position else 1 for axis in range(values.ndim)]) for position in (source, target)]
    chosen = jax.random.permutation(own_key, parts)[partner]
    strong = (owner == chosen) | (owner == (partner + parts // 2) % parts)
    return jnp.where(strong, factor * values, values)


def block_levels(own_key, shape, cuts, least, top_value):
    def one(position, parts):
        steps = jax.random.uniform(jax.random.fold_in(jax.random.fold_in(own_key, 6), position), (parts,), jnp.float32, least / len(cuts), top_value / len(cuts))
        return jnp.repeat(jnp.exp(steps), shape[position] // parts).reshape((-1,) + (1,) * (len(shape) - position - 1))

    factor_of = one(*cuts[0])
    for cut in cuts[1:]:
        factor_of = factor_of * one(*cut)
    return factor_of


def normal_values(stream_key, extent, width, limit, pieces=(), kind=jnp.bfloat16):
    array = jax.random.normal(stream_key, extent, jnp.float32) * width
    if len(pieces) > 0:
        array = block_levels(stream_key, extent, pieces, -0.22, 0.18) * array
    return jnp.clip(array, min=-limit, max=limit).astype(kind)


def heavy_noise(stream_key, extent, spread, bound, cuts, heavy, kind=jnp.bfloat16):
    result = spread * jax.random.normal(stream_key, extent, jnp.float32)
    if cuts:
        result = result * block_levels(stream_key, extent, cuts, -0.22, 0.18)
    return jnp.clip(raised(result, jax.random.fold_in(stream_key, 3), *heavy), -bound, bound).astype(kind)


def setup_inputs(seed: int = 0) -> dict:
    arg_keys = jax.random.split(jax.random.key(seed), 7)
    tokens = normal_values(arg_keys[0], (CONTEXT_SPAN, D), 1.0, 6.0, ((0, 8), (1, 4)))
    in_weight = normal_values(arg_keys[1], (D, 3, D), D ** -0.5, 0.09375, ((0, 8), (2, 4)))
    short_taps = normal_values(arg_keys[2], (3, TAPS, D), 0.6, 3.0, ((2, 4),), jnp.float32)
    skip_gain = jnp.clip(0.5 + 1.0 * jax.random.uniform(arg_keys[3], (D,), jnp.float32) ** block_levels(arg_keys[3], (D,), ((0, 4),), -0.2, 0.2), 0.5, 1.5)
    long_filter = draw_long_filter(jax.random.fold_in(arg_keys[6], 71), 0)
    out_weight = heavy_noise(arg_keys[5], (D, D), D ** -0.5, 0.125, ((0, 4),), (0, 1, 4, 2.0))
    return dict(tokens=tokens, in_weight=in_weight, short_taps=short_taps, skip_gain=skip_gain, long_filter=long_filter, out_weight=out_weight)


def reference(tokens, in_weight, short_taps, skip_gain, long_filter, out_weight):
    flat_weight = in_weight.reshape(D, 3 * D)
    projected = jnp.dot(tokens, flat_weight, preferred_element_type=jnp.float32).astype(jnp.bfloat16)
    values = projected.astype(jnp.float32).reshape(CONTEXT_SPAN, 3, D)
    padded = jnp.pad(values, ((TAPS - 1, 0), (0, 0), (0, 0)))
    smoothed = jnp.zeros_like(values)
    for tap_index in range(TAPS):
        lag_start = TAPS - 1 - tap_index
        smoothed = smoothed + short_taps[:, tap_index, :][None] * padded[lag_start:lag_start + CONTEXT_SPAN]
    gated = smoothed[:, 1, :] * smoothed[:, 2, :]
    spectrum = jnp.fft.rfft(gated, n=2 * CONTEXT_SPAN, axis=0) * jnp.fft.rfft(long_filter.astype(jnp.float32), n=2 * CONTEXT_SPAN, axis=0)
    mixed_seq = jnp.fft.irfft(spectrum, n=2 * CONTEXT_SPAN, axis=0)[:CONTEXT_SPAN] + skip_gain[None, :] * gated
    product = (mixed_seq * smoothed[:, 0, :]).astype(jnp.bfloat16)
    return jnp.dot(product, out_weight, preferred_element_type=jnp.float32).astype(jnp.bfloat16)
```

```python
import functools
import math

import jax
import jax.numpy as jnp
import numpy as np
from jax import lax
from jax.experimental import pallas as pl
from jax.experimental.pallas import tpu as pltpu
from jax.sharding import PartitionSpec as P

exact_prec = lax.Precision.HIGHEST
inner_len = 64


def dft_tables(half_len, blocks):
    full_len = 2 * half_len
    full_size = full_len * blocks
    half_index = jnp.arange(half_len, dtype=jnp.int32)
    full_index = jnp.arange(full_len, dtype=jnp.int32)
    block_index = jnp.arange(blocks, dtype=jnp.int32)
    outer_angle = (half_index[:, None] * full_index[None, :] % full_len).astype(jnp.float32) * (
        2.0 * math.pi / full_len
    )
    inner_angle = (block_index[:, None] * block_index[None, :] % blocks).astype(jnp.float32) * (
        2.0 * math.pi / blocks
    )
    twist_angle = (full_index[:, None] * block_index[None, :] % full_size).astype(jnp.float32) * (
        2.0 * math.pi / full_size
    )
    return (
        jnp.cos(outer_angle),
        jnp.sin(outer_angle),
        jnp.cos(inner_angle),
        jnp.sin(inner_angle),
        jnp.cos(twist_angle),
        jnp.sin(twist_angle),
    )


def forward_dft(signal, tables):
    outer_cos, outer_sin, inner_cos, inner_sin, twist_cos, twist_sin = tables
    real_section = jnp.einsum("cmn,mk->ckn", signal, outer_cos, precision=exact_prec)
    imag_section = -jnp.einsum("cmn,mk->ckn", signal, outer_sin, precision=exact_prec)
    real_twist = real_section * twist_cos + imag_section * twist_sin
    imag_twist = imag_section * twist_cos - real_section * twist_sin
    real_freq = jnp.einsum("ckn,nj->ckj", real_twist, inner_cos, precision=exact_prec) + jnp.einsum(
        "ckn,nj->ckj", imag_twist, inner_sin, precision=exact_prec
    )
    imag_freq = jnp.einsum("ckn,nj->ckj", imag_twist, inner_cos, precision=exact_prec) - jnp.einsum(
        "ckn,nj->ckj", real_twist, inner_sin, precision=exact_prec
    )
    return (real_freq, imag_freq)


def inverse_real(spectrum_real, spectrum_imag, tables):
    outer_cos, outer_sin, inner_cos, inner_sin, twist_cos, twist_sin = tables
    full_size = outer_cos.shape[1] * inner_cos.shape[0]
    back_real = jnp.einsum(
        "ckj,jn->ckn", spectrum_real, inner_cos, precision=exact_prec
    ) - jnp.einsum("ckj,jn->ckn", spectrum_imag, inner_sin, precision=exact_prec)
    back_imag = jnp.einsum(
        "ckj,jn->ckn", spectrum_imag, inner_cos, precision=exact_prec
    ) + jnp.einsum("ckj,jn->ckn", spectrum_real, inner_sin, precision=exact_prec)
    turn_real = back_real * twist_cos - back_imag * twist_sin
    turn_imag = back_imag * twist_cos + back_real * twist_sin
    summed_real = jnp.einsum(
        "ckn,mk->cmn", turn_real, outer_cos, precision=exact_prec
    ) - jnp.einsum("ckn,mk->cmn", turn_imag, outer_sin, precision=exact_prec)
    return summed_real / full_size


def causal_conv(signal, kernel, blocks):
    channels, length = signal.shape
    half_len = length // blocks
    tables = dft_tables(half_len, blocks)
    stacked = jnp.concatenate([signal, kernel], 0).reshape(2 * channels, half_len, blocks)
    real_freq, imag_freq = forward_dft(stacked, tables)
    data_real, filter_real = (real_freq[:channels], real_freq[channels:])
    data_imag, filter_imag = (imag_freq[:channels], imag_freq[channels:])
    spectrum_real = data_real * filter_real - data_imag * filter_imag
    spectrum_imag = data_real * filter_imag + data_imag * filter_real
    return inverse_real(spectrum_real, spectrum_imag, tables).reshape(channels, length)


def body(tokens, in_weight, short_taps, skip_gain, long_filter, out_weight):
    row_count, chan_width = tokens.shape
    blocks = lax.axis_size("seq")
    part_width = chan_width // blocks
    flat_weight = in_weight.reshape(in_weight.shape[0], 3 * chan_width)
    whole = lax.all_gather(tokens, "chan", axis=1, tiled=True)
    projected = jnp.dot(
        whole,
        lax.all_gather(flat_weight, "seq", axis=0, tiled=True),
        preferred_element_type=jnp.float32,
    )
    projected = projected.astype(jnp.bfloat16).reshape(row_count, 3, chan_width)
    outgoing = jnp.transpose(projected, (1, 2, 0))
    filter_rows = jnp.transpose(long_filter)[None]
    channel_major, filter_major = (
        lax.all_to_all(outgoing, "seq", split_axis=1, concat_axis=2, tiled=True),
        lax.all_to_all(filter_rows, "seq", split_axis=1, concat_axis=2, tiled=True),
    )
    offset = lax.axis_index("seq") * part_width
    local_taps = lax.dynamic_slice_in_dim(short_taps, offset, part_width, 2)
    local_skip = lax.dynamic_slice_in_dim(skip_gain, offset, part_width, 0)
    values = channel_major.astype(jnp.float32)
    tap_count = short_taps.shape[1]
    length = values.shape[2]
    padded = jnp.pad(values, ((0, 0), (0, 0), (tap_count - 1, 0)))
    smoothed = jnp.zeros_like(values)
    for tap_index in range(tap_count):
        lag_start = tap_count - 1 - tap_index
        smoothed = (
            smoothed
            + local_taps[:, tap_index, :, None] * padded[:, :, lag_start : lag_start + length]
        )
    gate_query = smoothed[0]
    gated = smoothed[1] * smoothed[2]
    mixed_seq = (
        causal_conv(gated, filter_major[0].astype(jnp.float32), blocks)
        + local_skip[:, None] * gated
    )
    product = (mixed_seq * gate_query).astype(jnp.bfloat16)
    returned = lax.all_to_all(product, "seq", split_axis=1, concat_axis=0, tiled=True)
    summed = lax.psum_scatter(
        lax.dot_general(
            out_weight, returned, (((0,), (0,)), ((), ())), preferred_element_type=jnp.float32
        ).astype(jnp.bfloat16),
        "chan",
        scatter_dimension=0,
        tiled=True,
    ).astype(jnp.float32)
    return jnp.transpose(summed).astype(jnp.bfloat16)


def wave_tables(length):
    span = 2 * length
    outer = span // inner_len
    used, rows = outer // 2, outer // 2 + 1
    padded_rows = -(-rows // 8) * 8
    m, k = np.arange(used), np.arange(rows)
    n, j = np.arange(inner_len), np.arange(inner_len)
    angle = (2.0 * math.pi / outer) * (np.outer(k, m) % outer)
    ahead = np.zeros((2, padded_rows, used))
    ahead[0, :rows], ahead[1, :rows] = np.cos(angle), -np.sin(angle)
    weight = np.where((k == 0) | (k == used), 1.0, 2.0) / span
    back = np.zeros((used, 2, padded_rows))
    back[:, 0, :rows] = (np.cos(angle) * weight[:, None]).T
    back[:, 1, :rows] = (-np.sin(angle) * weight[:, None]).T
    turn = n[None, None, :] * (k[:, None, None] + outer * j[None, :, None]) % span
    cos, sin = np.cos(turn * (2.0 * math.pi / span)), np.sin(turn * (2.0 * math.pi / span))
    middle = np.concatenate(
        [np.concatenate([cos, sin], 2), np.concatenate([-sin, cos], 2)], 1
    )
    return tuple(
        jnp.asarray(table, jnp.bfloat16)
        for table in (
            ahead.reshape(2 * padded_rows, used),
            middle,
            np.swapaxes(middle, 1, 2),
            back.reshape(used, 2 * padded_rows),
        )
    )


def project_kernel(where_ref, *refs):
    groups, parts = refs[:16], refs[16:20]
    own_ref, send_ref, held, weights, sems = refs[20:]
    place, chan = where_ref[0], where_ref[1]
    depth, side = place // 2, place % 2
    weight_copies = [
        pltpu.make_async_copy(parts[i], weights.at[i], sems.at[i]) for i in range(4)
    ]
    token_copies = [
        pltpu.make_async_copy(groups[i], held.at[i], sems.at[4 + i]) for i in range(16)
    ]
    for copy in weight_copies + token_copies:
        copy.start()
    for copy in weight_copies:
        copy.wait()
    block = own_ref.shape[0] // 8
    half = own_ref.shape[1]
    for step in range(4):
        total = None
        for turn in range(4):
            token_copies[4 * step + turn].wait()
            slot = jnp.bitwise_xor(depth, jnp.bitwise_xor(chan, turn))
            term = jnp.dot(
                held[4 * step + turn], weights[slot], preferred_element_type=jnp.float32
            )
            total = term if total is None else total + term
        low, high = total[:, :half], total[:, half:]
        own = jnp.where(side == 0, low, high)
        send = jnp.where(side == 0, high, low).astype(jnp.bfloat16)
        for pair in range(2):
            start = pl.multiple_of(jnp.bitwise_xor(place, 2 * step + pair) * block, block)
            own_ref[pl.ds(start, block), :] = own[pair * block : (pair + 1) * block]
            send_ref[pl.ds(start, block), :] = send[pair * block : (pair + 1) * block]


def project(where, groups, parts, length):
    width = parts[0].shape[1] // 2
    depth = parts[0].shape[0]
    return pl.pallas_call(
        project_kernel,
        out_shape=(
            jax.ShapeDtypeStruct((length, width), jnp.float32),
            jax.ShapeDtypeStruct((length, width), jnp.bfloat16),
        ),
        in_specs=[pl.BlockSpec(memory_space=pltpu.SMEM)]
        + [pl.BlockSpec(memory_space=pl.ANY)] * 20,
        out_specs=(
            pl.BlockSpec(memory_space=pltpu.VMEM),
            pl.BlockSpec(memory_space=pltpu.VMEM),
        ),
        scratch_shapes=[
            pltpu.VMEM((16,) + groups[0].shape, jnp.bfloat16),
            pltpu.VMEM((4,) + parts[0].shape, jnp.bfloat16),
            pltpu.SemaphoreType.DMA((20,)),
        ],
        compiler_params=pltpu.CompilerParams(vmem_limit_bytes=24 * 2**20),
        cost_estimate=pl.CostEstimate(
            flops=2 * length * 4 * depth * 2 * width,
            bytes_accessed=2 * length * 4 * depth,
            transcendentals=0,
        ),
        name="project",
    )(where, *groups, *parts)


def smooth_into(padded, own_ref, recv_ref, taps_ref, branch, store):
    length = own_ref.shape[0]
    tap_count = taps_ref.shape[1]
    block = length // 8
    padded[0:8, :] = jnp.zeros((8, padded.shape[1]), jnp.float32)
    for i in range(8):
        rows = slice(i * block, (i + 1) * block)
        padded[8 + i * block : 8 + (i + 1) * block, :] = own_ref[rows, :] + recv_ref[
            rows, :
        ].astype(jnp.float32)
    for i in range(8):
        total = None
        for tap in range(tap_count):
            start = 8 + i * block - tap
            term = taps_ref[branch, tap : tap + 1, :] * padded[start : start + block, :]
            total = term if total is None else total + term
        store(slice(i * block, (i + 1) * block), total)


def mix_kernel(
    where_ref, own1, recv1, own2, recv2, taps_ref, skip_ref, ahead, middle, middle_back, back, *refs
):
    filters, mixed_ref = refs[:8], refs[8]
    padded, gated, lags, waves, filter_waves, sums = refs[9:]
    place = where_ref[0]
    length, width = own1.shape
    block = length // 8
    rows, two = middle.shape[0], middle.shape[1]
    padded_rows = ahead.shape[0] // 2
    used = ahead.shape[1]
    for i in range(8):
        start = pl.multiple_of(jnp.bitwise_xor(place, i) * block, block)
        lags[pl.ds(start, block), :] = filters[i][...].astype(jnp.float32)

    def first(at, value):
        gated[at, :] = value

    def second(at, value):
        gated[at, :] = gated[at, :] * value

    smooth_into(padded, own1, recv1, taps_ref, 1, first)
    smooth_into(padded, own2, recv2, taps_ref, 2, second)
    for n in range(inner_len):
        both = jnp.concatenate(
            [gated[pl.ds(n, used, stride=inner_len), :], lags[pl.ds(n, used, stride=inner_len), :]],
            1,
        ).astype(jnp.bfloat16)
        wave = jnp.dot(ahead[...], both, preferred_element_type=jnp.float32)
        for i in range(2):
            at = pl.ds(i * inner_len + n, padded_rows, stride=two)
            part = wave[i * padded_rows : (i + 1) * padded_rows]
            waves[at, :] = part[:, :width]
            filter_waves[at, :] = part[:, width:]
    if padded_rows > rows:
        sums[rows * two :, :] = jnp.zeros(((padded_rows - rows) * two, width), jnp.float32)

    def one(k, _):
        at = pl.ds(pl.multiple_of(k * two, two), two)
        both = jnp.concatenate([waves[at, :], filter_waves[at, :]], 1).astype(jnp.bfloat16)
        freq = jnp.dot(middle[k], both, preferred_element_type=jnp.float32)
        data_real, filter_real = freq[:inner_len, :width], freq[:inner_len, width:]
        data_imag, filter_imag = freq[inner_len:, :width], freq[inner_len:, width:]
        spectrum = jnp.concatenate(
            [
                data_real * filter_real - data_imag * filter_imag,
                data_real * filter_imag + data_imag * filter_real,
            ],
            0,
        ).astype(jnp.bfloat16)
        sums[at, :] = jnp.dot(middle_back[k], spectrum, preferred_element_type=jnp.float32)
        return 0

    lax.fori_loop(0, rows, one, 0, unroll=11 if rows % 11 == 0 else 1)
    for n in range(0, inner_len, 2):
        pieces = [
            jnp.concatenate(
                [
                    sums[pl.ds(n + i, padded_rows, stride=two), :],
                    sums[pl.ds(inner_len + n + i, padded_rows, stride=two), :],
                ],
                0,
            )
            for i in range(2)
        ]
        wave = jnp.dot(
            back[...],
            jnp.concatenate(pieces, 1).astype(jnp.bfloat16),
            preferred_element_type=jnp.float32,
        )
        for i in range(2):
            at = pl.ds(n + i, used, stride=inner_len)
            mixed_ref[at, :] = wave[:, i * width : (i + 1) * width] + skip_ref[...] * gated[at, :]


def mix(where, own1, recv1, own2, recv2, taps, skip, tables, filters):
    length, width = own1.shape
    rows, two = tables[1].shape[:2]
    padded_rows = tables[0].shape[0] // 2
    vmem = pl.BlockSpec(memory_space=pltpu.VMEM)
    return pl.pallas_call(
        mix_kernel,
        out_shape=jax.ShapeDtypeStruct((length, width), jnp.float32),
        in_specs=[pl.BlockSpec(memory_space=pltpu.SMEM)] + [vmem] * 18,
        out_specs=vmem,
        scratch_shapes=[
            pltpu.VMEM((length + 8, width), jnp.float32),
            pltpu.VMEM((length, width), jnp.float32),
            pltpu.VMEM((length, width), jnp.float32),
            pltpu.VMEM((padded_rows * two, width), jnp.float32),
            pltpu.VMEM((padded_rows * two, width), jnp.float32),
            pltpu.VMEM((padded_rows * two, width), jnp.float32),
        ],
        compiler_params=pltpu.CompilerParams(vmem_limit_bytes=40 * 2**20),
        cost_estimate=pl.CostEstimate(
            flops=2 * 8 * length * inner_len * width, bytes_accessed=6 * 2**20, transcendentals=0
        ),
        name="mix",
    )(where, own1, recv1, own2, recv2, taps, skip, *tables, *filters)


def gate_kernel(where_ref, own0, recv0, mixed_ref, taps_ref, *refs):
    outs, padded, product = refs[:8], refs[8], refs[9]
    place = where_ref[0]
    block = own0.shape[0] // 8

    def store(at, value):
        product[at, :] = (mixed_ref[at, :] * value).astype(jnp.bfloat16)

    smooth_into(padded, own0, recv0, taps_ref, 0, store)
    for i in range(8):
        start = pl.multiple_of(jnp.bitwise_xor(place, i) * block, block)
        outs[i][...] = product[pl.ds(start, block), :]


def gate(where, own0, recv0, mixed, taps):
    length, width = own0.shape
    vmem = pl.BlockSpec(memory_space=pltpu.VMEM)
    return pl.pallas_call(
        gate_kernel,
        out_shape=(jax.ShapeDtypeStruct((length // 8, width), jnp.bfloat16),) * 8,
        in_specs=[pl.BlockSpec(memory_space=pltpu.SMEM)] + [vmem] * 4,
        out_specs=(vmem,) * 8,
        scratch_shapes=[
            pltpu.VMEM((length + 8, width), jnp.float32),
            pltpu.VMEM((length, width), jnp.bfloat16),
        ],
        compiler_params=pltpu.CompilerParams(vmem_limit_bytes=16 * 2**20),
        cost_estimate=pl.CostEstimate(
            flops=8 * length * width, bytes_accessed=12 * length * width, transcendentals=0
        ),
        name="gate",
    )(where, own0, recv0, mixed, taps)


def emit_kernel(where_ref, *refs, added):
    parts, weight_ref = refs[:8], refs[8]
    extra = refs[9 : 9 + added]
    out_ref, joined = refs[9 + added :]
    place = where_ref[0]
    width = parts[0].shape[1]

    @pl.when(pl.program_id(0) == 0)
    def _():
        for i in range(8):
            start = pl.multiple_of(jnp.bitwise_xor(place, i) * width, width)
            joined[:, pl.ds(start, width)] = parts[i][...]

    total = jnp.dot(joined[...], weight_ref[...], preferred_element_type=jnp.float32)
    for term in extra:
        total = total + term[...].astype(jnp.float32)
    out_ref[...] = total.astype(out_ref.dtype)


def emit(where, parts, weight, extra, out_dtype):
    rows, width = parts[0].shape
    columns = weight.shape[1] // 4
    tile = columns // 4
    whole = pl.BlockSpec((rows, width), lambda i, at: (0, 0))
    tiled = pl.BlockSpec((rows, tile), lambda i, at: (0, i))
    return pl.pallas_call(
        functools.partial(emit_kernel, added=len(extra)),
        out_shape=jax.ShapeDtypeStruct((rows, columns), out_dtype),
        grid_spec=pltpu.PrefetchScalarGridSpec(
            num_scalar_prefetch=1,
            grid=(4,),
            in_specs=[whole] * 8
            + [pl.BlockSpec((weight.shape[0], tile), lambda i, at: (0, 4 * at[1] + i))]
            + [tiled] * len(extra),
            out_specs=tiled,
            scratch_shapes=[pltpu.VMEM((rows, 8 * width), jnp.bfloat16)],
        ),
        compiler_params=pltpu.CompilerParams(vmem_limit_bytes=16 * 2**20),
        cost_estimate=pl.CostEstimate(
            flops=2 * rows * weight.shape[0] * columns,
            bytes_accessed=2 * weight.shape[0] * columns,
            transcendentals=0,
        ),
        name="emit",
    )(where, *parts, weight, *extra)


def swap(value, axis, count, turn):
    return lax.ppermute(value, axis, [(i, i ^ turn) for i in range(count)])


def fast_body(tokens, in_weight, short_taps, skip_gain, long_filter, out_weight):
    seq, chans = lax.axis_size("seq"), lax.axis_size("chan")
    place, chan = lax.axis_index("seq"), lax.axis_index("chan")
    depth, side = place // 2, place % 2
    rows, width = tokens.shape
    length = rows * seq
    part = width // seq
    half = width // 2
    where = jnp.stack([place, chan]).astype(jnp.int32)

    ours = lax.dynamic_slice_in_dim(tokens, side * half, half, 1)
    theirs = lax.dynamic_slice_in_dim(tokens, (1 - side) * half, half, 1)
    pair = jnp.concatenate([ours, swap(theirs, "seq", seq, 1)], 0)
    far = swap(pair, "seq", seq, 4)
    line = [pair, swap(pair, "seq", seq, 2), far, swap(far, "seq", seq, 2)]
    across = [swap(value, "chan", chans, 2) for value in line]
    groups = []
    for i in range(4):
        groups += [
            line[i],
            swap(line[i], "chan", chans, 1),
            across[i],
            swap(across[i], "chan", chans, 1),
        ]

    filters = []
    for turn in range(seq):
        piece = lax.dynamic_slice_in_dim(long_filter, (place ^ turn) * part, part, 1)
        filters.append(piece if turn == 0 else swap(piece, "seq", seq, turn))

    def branch(index):
        parts = []
        for turn in range(4):
            piece = lax.dynamic_slice_in_dim(
                in_weight[:, index, :], (depth ^ turn) * 2 * part, 2 * part, 1
            )
            parts.append(piece if turn == 0 else swap(piece, "seq", seq, 2 * turn))
        own, send = project(where, groups, parts, length)
        return own, swap(send, "seq", seq, 1)

    taps = lax.dynamic_slice_in_dim(short_taps, place * part, part, 2)
    skip = lax.dynamic_slice_in_dim(skip_gain, place * part, part, 0)[None]
    own1, recv1 = branch(1)
    own2, recv2 = branch(2)
    own0, recv0 = branch(0)
    mixed = mix(where, own1, recv1, own2, recv2, taps, skip, wave_tables(length), filters)
    pieces = gate(where, own0, recv0, mixed, taps)
    joined = [
        piece if turn == 0 else swap(piece, "seq", seq, turn) for turn, piece in enumerate(pieces)
    ]

    def share(turn, extra, dtype):
        return emit(jnp.stack([place, chan ^ turn]).astype(jnp.int32), joined, out_weight, extra, dtype)

    from_core = swap(share(3, [], jnp.bfloat16), "chan", chans, 1)
    near = swap(share(1, [], jnp.bfloat16), "chan", chans, 1)
    from_chip = swap(share(2, [from_core], jnp.bfloat16), "chan", chans, 2)
    own = share(0, [near], jnp.float32)
    return (own + from_chip.astype(jnp.float32)).astype(jnp.bfloat16)


def solution(mesh):
    in_specs = (
        P("seq", "chan"),
        P("seq", None, "chan"),
        P(None, None, "chan"),
        P("chan"),
        P("seq", "chan"),
        P("chan", None),
    )
    out_specs = P("seq", "chan")
    seq, chans = mesh.shape["seq"], mesh.shape["chan"]
    chosen = fast_body if seq == 8 and chans == 4 else body
    return jax.shard_map(chosen, mesh=mesh, in_specs=in_specs, out_specs=out_specs, check_vma=False)
```

```python
import functools
import math

import jax
import jax.numpy as jnp
import numpy as np
from jax import lax
from jax.experimental import pallas as pl
from jax.experimental.pallas import tpu as pltpu
from jax.sharding import PartitionSpec as P

exact_prec = lax.Precision.HIGHEST
inner_len = 64


def dft_tables(half_len, blocks):
    full_len = 2 * half_len
    full_size = full_len * blocks
    half_index = jnp.arange(half_len, dtype=jnp.int32)
    full_index = jnp.arange(full_len, dtype=jnp.int32)
    block_index = jnp.arange(blocks, dtype=jnp.int32)
    outer_angle = (half_index[:, None] * full_index[None, :] % full_len).astype(jnp.float32) * (
        2.0 * math.pi / full_len
    )
    inner_angle = (block_index[:, None] * block_index[None, :] % blocks).astype(jnp.float32) * (
        2.0 * math.pi / blocks
    )
    twist_angle = (full_index[:, None] * block_index[None, :] % full_size).astype(jnp.float32) * (
        2.0 * math.pi / full_size
    )
    return (
        jnp.cos(outer_angle),
        jnp.sin(outer_angle),
        jnp.cos(inner_angle),
        jnp.sin(inner_angle),
        jnp.cos(twist_angle),
        jnp.sin(twist_angle),
    )


def forward_dft(signal, tables):
    outer_cos, outer_sin, inner_cos, inner_sin, twist_cos, twist_sin = tables
    real_section = jnp.einsum("cmn,mk->ckn", signal, outer_cos, precision=exact_prec)
    imag_section = -jnp.einsum("cmn,mk->ckn", signal, outer_sin, precision=exact_prec)
    real_twist = real_section * twist_cos + imag_section * twist_sin
    imag_twist = imag_section * twist_cos - real_section * twist_sin
    real_freq = jnp.einsum("ckn,nj->ckj", real_twist, inner_cos, precision=exact_prec) + jnp.einsum(
        "ckn,nj->ckj", imag_twist, inner_sin, precision=exact_prec
    )
    imag_freq = jnp.einsum("ckn,nj->ckj", imag_twist, inner_cos, precision=exact_prec) - jnp.einsum(
        "ckn,nj->ckj", real_twist, inner_sin, precision=exact_prec
    )
    return (real_freq, imag_freq)


def inverse_real(spectrum_real, spectrum_imag, tables):
    outer_cos, outer_sin, inner_cos, inner_sin, twist_cos, twist_sin = tables
    full_size = outer_cos.shape[1] * inner_cos.shape[0]
    back_real = jnp.einsum(
        "ckj,jn->ckn", spectrum_real, inner_cos, precision=exact_prec
    ) - jnp.einsum("ckj,jn->ckn", spectrum_imag, inner_sin, precision=exact_prec)
    back_imag = jnp.einsum(
        "ckj,jn->ckn", spectrum_imag, inner_cos, precision=exact_prec
    ) + jnp.einsum("ckj,jn->ckn", spectrum_real, inner_sin, precision=exact_prec)
    turn_real = back_real * twist_cos - back_imag * twist_sin
    turn_imag = back_imag * twist_cos + back_real * twist_sin
    summed_real = jnp.einsum(
        "ckn,mk->cmn", turn_real, outer_cos, precision=exact_prec
    ) - jnp.einsum("ckn,mk->cmn", turn_imag, outer_sin, precision=exact_prec)
    return summed_real / full_size


def causal_conv(signal, kernel, blocks):
    channels, length = signal.shape
    half_len = length // blocks
    tables = dft_tables(half_len, blocks)
    stacked = jnp.concatenate([signal, kernel], 0).reshape(2 * channels, half_len, blocks)
    real_freq, imag_freq = forward_dft(stacked, tables)
    data_real, filter_real = (real_freq[:channels], real_freq[channels:])
    data_imag, filter_imag = (imag_freq[:channels], imag_freq[channels:])
    spectrum_real = data_real * filter_real - data_imag * filter_imag
    spectrum_imag = data_real * filter_imag + data_imag * filter_real
    return inverse_real(spectrum_real, spectrum_imag, tables).reshape(channels, length)


def body(tokens, in_weight, short_taps, skip_gain, long_filter, out_weight):
    row_count, chan_width = tokens.shape
    blocks = lax.axis_size("seq")
    part_width = chan_width // blocks
    flat_weight = in_weight.reshape(in_weight.shape[0], 3 * chan_width)
    whole = lax.all_gather(tokens, "chan", axis=1, tiled=True)
    projected = jnp.dot(
        whole,
        lax.all_gather(flat_weight, "seq", axis=0, tiled=True),
        preferred_element_type=jnp.float32,
    )
    projected = projected.astype(jnp.bfloat16).reshape(row_count, 3, chan_width)
    outgoing = jnp.transpose(projected, (1, 2, 0))
    filter_rows = jnp.transpose(long_filter)[None]
    channel_major, filter_major = (
        lax.all_to_all(outgoing, "seq", split_axis=1, concat_axis=2, tiled=True),
        lax.all_to_all(filter_rows, "seq", split_axis=1, concat_axis=2, tiled=True),
    )
    offset = lax.axis_index("seq") * part_width
    local_taps = lax.dynamic_slice_in_dim(short_taps, offset, part_width, 2)
    local_skip = lax.dynamic_slice_in_dim(skip_gain, offset, part_width, 0)
    values = channel_major.astype(jnp.float32)
    tap_count = short_taps.shape[1]
    length = values.shape[2]
    padded = jnp.pad(values, ((0, 0), (0, 0), (tap_count - 1, 0)))
    smoothed = jnp.zeros_like(values)
    for tap_index in range(tap_count):
        lag_start = tap_count - 1 - tap_index
        smoothed = (
            smoothed
            + local_taps[:, tap_index, :, None] * padded[:, :, lag_start : lag_start + length]
        )
    gate_query = smoothed[0]
    gated = smoothed[1] * smoothed[2]
    mixed_seq = (
        causal_conv(gated, filter_major[0].astype(jnp.float32), blocks)
        + local_skip[:, None] * gated
    )
    product = (mixed_seq * gate_query).astype(jnp.bfloat16)
    returned = lax.all_to_all(product, "seq", split_axis=1, concat_axis=0, tiled=True)
    summed = lax.psum_scatter(
        lax.dot_general(
            out_weight, returned, (((0,), (0,)), ((), ())), preferred_element_type=jnp.float32
        ).astype(jnp.bfloat16),
        "chan",
        scatter_dimension=0,
        tiled=True,
    ).astype(jnp.float32)
    return jnp.transpose(summed).astype(jnp.bfloat16)


def wave_tables(length):
    span = 2 * length
    outer = span // inner_len
    used, rows = outer // 2, outer // 2 + 1
    padded_rows = -(-rows // 8) * 8
    m, k = np.arange(used), np.arange(rows)
    n, j = np.arange(inner_len), np.arange(inner_len)
    angle = (2.0 * math.pi / outer) * (np.outer(k, m) % outer)
    ahead = np.zeros((2, padded_rows, used))
    ahead[0, :rows], ahead[1, :rows] = np.cos(angle), -np.sin(angle)
    weight = np.where((k == 0) | (k == used), 1.0, 2.0) / span
    back = np.zeros((used, 2, padded_rows))
    back[:, 0, :rows] = (np.cos(angle) * weight[:, None]).T
    back[:, 1, :rows] = (-np.sin(angle) * weight[:, None]).T
    turn = n[None, None, :] * (k[:, None, None] + outer * j[None, :, None]) % span
    cos, sin = np.cos(turn * (2.0 * math.pi / span)), np.sin(turn * (2.0 * math.pi / span))
    middle = np.concatenate(
        [np.concatenate([cos, sin], 2), np.concatenate([-sin, cos], 2)], 1
    )
    return tuple(
        jnp.asarray(table, jnp.bfloat16)
        for table in (
            ahead.reshape(2 * padded_rows, used),
            middle,
            np.swapaxes(middle, 1, 2),
            back.reshape(used, 2 * padded_rows),
        )
    )


def cut_kernel(where_ref, *refs, index, counts, after):
    place = where_ref[0]
    depth, side = place // 2, place % 2
    tokens, weight, filters = [
        refs[sum(counts[:i]) : sum(counts[: i + 1])] for i in range(3)
    ]
    outs, sems = list(refs[sum(counts) + after : -1]), refs[-1]
    copies = []

    def copy(source, target):
        copies.append(pltpu.make_async_copy(source, target, sems.at[len(copies)]))

    for source in tokens:
        half = outs[0].shape[1]
        for which in (1 - side, side):
            columns = pl.ds(pl.multiple_of(which * half, half), half)
            copy(source.at[:, columns], outs.pop(0))
    rows, width = weight[0].shape[1], outs[0].shape[1]
    for turn in (2, 1, 3, 0):
        start = pl.multiple_of(jnp.bitwise_xor(depth, turn) * width, width)
        columns = pl.ds(start, width)
        copy(weight[0].at[index, :, columns], outs[turn].at[pl.ds(0, rows), :])
        for source in filters:
            copy(source.at[:, columns], outs[turn].at[pl.ds(rows, source.shape[0]), :])
    for one in copies:
        one.start()
    for one in copies:
        one.wait()


def cut(where, tokens, weight, index, filters, after):
    rows = weight.shape[1] + sum(value.shape[0] for value in filters)
    shapes = []
    for value in tokens:
        shapes += [jax.ShapeDtypeStruct((value.shape[0], value.shape[1] // 2), value.dtype)] * 2
    shapes += [jax.ShapeDtypeStruct((rows, weight.shape[2] // 4), weight.dtype)] * 4
    counts = (len(tokens), 1, len(filters))
    return pl.pallas_call(
        functools.partial(cut_kernel, index=index, counts=counts, after=len(after)),
        out_shape=tuple(shapes),
        in_specs=[pl.BlockSpec(memory_space=pltpu.SMEM)]
        + [pl.BlockSpec(memory_space=pltpu.HBM)] * sum(counts)
        + [pl.BlockSpec(memory_space=pl.ANY)] * len(after),
        out_specs=(pl.BlockSpec(memory_space=pltpu.VMEM),) * len(shapes),
        scratch_shapes=[pltpu.SemaphoreType.DMA((10,))],
        compiler_params=pltpu.CompilerParams(vmem_limit_bytes=8 * 2**20),
        name="cut",
    )(where, *tokens, weight, *filters, *after)


def join_kernel(*refs, count):
    out_ref = refs[-1]
    start = 0
    for source in refs[:count]:
        out_ref[start : start + source.shape[0], :] = source[...]
        start += source.shape[0]


def join(values, after):
    rows = sum(value.shape[0] for value in values)
    vmem = pl.BlockSpec(memory_space=pltpu.VMEM)
    return pl.pallas_call(
        functools.partial(join_kernel, count=len(values)),
        out_shape=jax.ShapeDtypeStruct((rows, values[0].shape[1]), values[0].dtype),
        in_specs=[vmem] * len(values) + [pl.BlockSpec(memory_space=pl.ANY)] * len(after),
        out_specs=vmem,
        compiler_params=pltpu.CompilerParams(vmem_limit_bytes=8 * 2**20),
        name="join",
    )(*values, *after)


def project_kernel(where_ref, *refs, filter_rows, after):
    line, across, cores, parts = refs[:4], refs[4:8], refs[8:10], refs[10:14]
    if filter_rows:
        own_ref, send_ref, lags_ref, weights = refs[14 + after :]
    else:
        own_ref, send_ref, weights = refs[14 + after :]
    place, chan = where_ref[0], where_ref[1]
    depth, side = place // 2, place % 2
    rows = line[0].shape[1]
    for i in range(4):
        slot = jnp.bitwise_xor(depth, jnp.bitwise_xor(chan, i))
        start = pl.multiple_of(slot * rows, rows)
        weights[pl.ds(start, rows), :] = parts[i][0:rows, :]
    length, half = own_ref.shape
    block = length // 8
    for step in range(4):
        low = 4 * block * (step % 2)
        both = cores[step // 2]
        joined = jnp.concatenate(
            [
                line[step][...],
                both[low : low + 2 * block, :],
                across[step][...],
                both[low + 2 * block : low + 4 * block, :],
            ],
            1,
        )
        total = jnp.dot(joined, weights[...], preferred_element_type=jnp.float32)
        left, right = total[:, :half], total[:, half:]
        own = jnp.where(side == 0, left, right)
        send = jnp.where(side == 0, right, left).astype(jnp.bfloat16)
        for pair in range(2):
            start = pl.multiple_of(jnp.bitwise_xor(place, 2 * step + pair) * block, block)
            own_ref[pl.ds(start, block), :] = own[pair * block : (pair + 1) * block]
            send_ref[pl.ds(start, block), :] = send[pair * block : (pair + 1) * block]
    if filter_rows:
        for i in range(4):
            piece = parts[i][rows:, :].astype(jnp.float32)
            left, right = piece[:, :half], piece[:, half:]
            at = slice(i * filter_rows, (i + 1) * filter_rows)
            lags_ref[at, :] = jnp.where(side == 0, left, right).astype(jnp.bfloat16)
            at = slice(length + i * filter_rows, length + (i + 1) * filter_rows)
            send_ref[at, :] = jnp.where(side == 0, right, left).astype(jnp.bfloat16)


def project(where, line, across, cores, parts, length, after):
    depth, width = line[0].shape[1], parts[0].shape[1]
    filter_rows = parts[0].shape[0] - depth
    vmem = pl.BlockSpec(memory_space=pltpu.VMEM)
    shapes = [
        jax.ShapeDtypeStruct((length, width // 2), jnp.float32),
        jax.ShapeDtypeStruct((length + 4 * filter_rows, width // 2), jnp.bfloat16),
    ]
    if filter_rows:
        shapes.append(jax.ShapeDtypeStruct((4 * filter_rows, width // 2), jnp.bfloat16))
    return pl.pallas_call(
        functools.partial(project_kernel, filter_rows=filter_rows, after=len(after)),
        out_shape=tuple(shapes),
        in_specs=[pl.BlockSpec(memory_space=pltpu.SMEM)]
        + [vmem] * 14
        + [pl.BlockSpec(memory_space=pl.ANY)] * len(after),
        out_specs=(vmem,) * len(shapes),
        scratch_shapes=[pltpu.VMEM((4 * depth, width), jnp.bfloat16)],
        compiler_params=pltpu.CompilerParams(vmem_limit_bytes=24 * 2**20),
        cost_estimate=pl.CostEstimate(
            flops=2 * length * 4 * depth * width,
            bytes_accessed=2 * length * 4 * depth,
            transcendentals=0,
        ),
        name="project",
    )(where, *line, *across, *cores, *parts, *after)


def smooth_into(padded, own_ref, recv_ref, taps_ref, branch, store):
    length = own_ref.shape[0]
    tap_count = taps_ref.shape[1]
    block = length // 8
    padded[0:8, :] = jnp.zeros((8, padded.shape[1]), jnp.float32)
    for i in range(8):
        rows = slice(i * block, (i + 1) * block)
        padded[8 + i * block : 8 + (i + 1) * block, :] = own_ref[rows, :] + recv_ref[
            rows, :
        ].astype(jnp.float32)
    for i in range(8):
        total = None
        for tap in range(tap_count):
            start = 8 + i * block - tap
            term = taps_ref[branch, tap : tap + 1, :] * padded[start : start + block, :]
            total = term if total is None else total + term
        store(slice(i * block, (i + 1) * block), total)


def mix_kernel(
    where_ref, own1, recv1, own2, recv2, taps_ref, skip_ref, ahead, middle, middle_back, back, *refs
):
    lags_here, lags_there, mixed_ref = refs[:3]
    padded, gated, lags, waves, filter_waves, sums = refs[3:]
    place = where_ref[0]
    length, width = own1.shape
    block = length // 8
    rows, two = middle.shape[0], middle.shape[1]
    padded_rows = ahead.shape[0] // 2
    used = ahead.shape[1]
    for i in range(4):
        at = slice(i * block, (i + 1) * block)
        for side, source in enumerate((lags_here, lags_there)):
            start = pl.multiple_of(jnp.bitwise_xor(place, 2 * i + side) * block, block)
            lags[pl.ds(start, block), :] = source[at, :].astype(jnp.float32)

    def first(at, value):
        gated[at, :] = value

    def second(at, value):
        gated[at, :] = gated[at, :] * value

    smooth_into(padded, own1, recv1, taps_ref, 1, first)
    smooth_into(padded, own2, recv2, taps_ref, 2, second)
    for n in range(inner_len):
        both = jnp.concatenate(
            [gated[pl.ds(n, used, stride=inner_len), :], lags[pl.ds(n, used, stride=inner_len), :]],
            1,
        ).astype(jnp.bfloat16)
        wave = jnp.dot(ahead[...], both, preferred_element_type=jnp.float32)
        for i in range(2):
            at = pl.ds(i * inner_len + n, padded_rows, stride=two)
            part = wave[i * padded_rows : (i + 1) * padded_rows]
            waves[at, :] = part[:, :width]
            filter_waves[at, :] = part[:, width:]
    if padded_rows > rows:
        sums[rows * two :, :] = jnp.zeros(((padded_rows - rows) * two, width), jnp.float32)

    def one(k, _):
        at = pl.ds(pl.multiple_of(k * two, two), two)
        both = jnp.concatenate([waves[at, :], filter_waves[at, :]], 1).astype(jnp.bfloat16)
        freq = jnp.dot(middle[k], both, preferred_element_type=jnp.float32)
        data_real, filter_real = freq[:inner_len, :width], freq[:inner_len, width:]
        data_imag, filter_imag = freq[inner_len:, :width], freq[inner_len:, width:]
        spectrum = jnp.concatenate(
            [
                data_real * filter_real - data_imag * filter_imag,
                data_real * filter_imag + data_imag * filter_real,
            ],
            0,
        ).astype(jnp.bfloat16)
        sums[at, :] = jnp.dot(middle_back[k], spectrum, preferred_element_type=jnp.float32)
        return 0

    lax.fori_loop(0, rows, one, 0, unroll=11 if rows % 11 == 0 else 1)
    for n in range(0, inner_len, 2):
        pieces = [
            jnp.concatenate(
                [
                    sums[pl.ds(n + i, padded_rows, stride=two), :],
                    sums[pl.ds(inner_len + n + i, padded_rows, stride=two), :],
                ],
                0,
            )
            for i in range(2)
        ]
        wave = jnp.dot(
            back[...],
            jnp.concatenate(pieces, 1).astype(jnp.bfloat16),
            preferred_element_type=jnp.float32,
        )
        for i in range(2):
            at = pl.ds(n + i, used, stride=inner_len)
            mixed_ref[at, :] = wave[:, i * width : (i + 1) * width] + skip_ref[...] * gated[at, :]


def mix(where, own1, recv1, own2, recv2, taps, skip, tables, lags_here, lags_there):
    length, width = own1.shape
    rows, two = tables[1].shape[:2]
    padded_rows = tables[0].shape[0] // 2
    vmem = pl.BlockSpec(memory_space=pltpu.VMEM)
    return pl.pallas_call(
        mix_kernel,
        out_shape=jax.ShapeDtypeStruct((length, width), jnp.float32),
        in_specs=[pl.BlockSpec(memory_space=pltpu.SMEM)] + [vmem] * 12,
        out_specs=vmem,
        scratch_shapes=[
            pltpu.VMEM((length + 8, width), jnp.float32),
            pltpu.VMEM((length, width), jnp.float32),
            pltpu.VMEM((length, width), jnp.float32),
            pltpu.VMEM((padded_rows * two, width), jnp.float32),
            pltpu.VMEM((padded_rows * two, width), jnp.float32),
            pltpu.VMEM((padded_rows * two, width), jnp.float32),
        ],
        compiler_params=pltpu.CompilerParams(vmem_limit_bytes=40 * 2**20),
        cost_estimate=pl.CostEstimate(
            flops=2 * 8 * length * inner_len * width, bytes_accessed=6 * 2**20, transcendentals=0
        ),
        name="mix",
    )(where, own1, recv1, own2, recv2, taps, skip, *tables, lags_here, lags_there)


def gate_kernel(where_ref, own0, recv0, mixed_ref, taps_ref, *refs):
    outs, padded, product = refs[:8], refs[8], refs[9]
    place = where_ref[0]
    block = own0.shape[0] // 8

    def store(at, value):
        product[at, :] = (mixed_ref[at, :] * value).astype(jnp.bfloat16)

    smooth_into(padded, own0, recv0, taps_ref, 0, store)
    for i in range(8):
        start = pl.multiple_of(jnp.bitwise_xor(place, i) * block, block)
        outs[i][...] = product[pl.ds(start, block), :]


def gate(where, own0, recv0, mixed, taps):
    length, width = own0.shape
    vmem = pl.BlockSpec(memory_space=pltpu.VMEM)
    return pl.pallas_call(
        gate_kernel,
        out_shape=(jax.ShapeDtypeStruct((length // 8, width), jnp.bfloat16),) * 8,
        in_specs=[pl.BlockSpec(memory_space=pltpu.SMEM)] + [vmem] * 4,
        out_specs=(vmem,) * 8,
        scratch_shapes=[
            pltpu.VMEM((length + 8, width), jnp.float32),
            pltpu.VMEM((length, width), jnp.bfloat16),
        ],
        compiler_params=pltpu.CompilerParams(vmem_limit_bytes=16 * 2**20),
        cost_estimate=pl.CostEstimate(
            flops=8 * length * width, bytes_accessed=12 * length * width, transcendentals=0
        ),
        name="gate",
    )(where, own0, recv0, mixed, taps)


def emit_kernel(where_ref, weight, *refs, added):
    parts, extra = refs[:8], refs[8 : 8 + added]
    out_ref, joined, tiles, sems = refs[8 + added :]
    place, column = where_ref[0], where_ref[1]
    width = parts[0].shape[1]
    count, _, tile = tiles.shape
    copies = []
    for i in range(count):
        start = pl.multiple_of((column * count + i) * tile, tile)
        copies.append(
            pltpu.make_async_copy(weight.at[:, pl.ds(start, tile)], tiles.at[i], sems.at[i])
        )
        copies[i].start()
    for i in range(8):
        start = pl.multiple_of(jnp.bitwise_xor(place, i) * width, width)
        joined[:, pl.ds(start, width)] = parts[i][...]
    for i in range(count):
        copies[i].wait()
        total = jnp.dot(joined[...], tiles[i], preferred_element_type=jnp.float32)
        at = slice(i * tile, (i + 1) * tile)
        for term in extra:
            total = total + term[:, at].astype(jnp.float32)
        out_ref[:, at] = total.astype(out_ref.dtype)


def emit(where, parts, weight, extra, out_dtype):
    rows, width = parts[0].shape
    columns = weight.shape[1] // 4
    count = 4
    vmem = pl.BlockSpec(memory_space=pltpu.VMEM)
    return pl.pallas_call(
        functools.partial(emit_kernel, added=len(extra)),
        out_shape=jax.ShapeDtypeStruct((rows, columns), out_dtype),
        in_specs=[
            pl.BlockSpec(memory_space=pltpu.SMEM),
            pl.BlockSpec(memory_space=pltpu.HBM),
        ]
        + [vmem] * (8 + len(extra)),
        out_specs=vmem,
        scratch_shapes=[
            pltpu.VMEM((rows, 8 * width), jnp.bfloat16),
            pltpu.VMEM((count, weight.shape[0], columns // count), jnp.bfloat16),
            pltpu.SemaphoreType.DMA((count,)),
        ],
        compiler_params=pltpu.CompilerParams(vmem_limit_bytes=16 * 2**20),
        cost_estimate=pl.CostEstimate(
            flops=2 * rows * weight.shape[0] * columns,
            bytes_accessed=2 * weight.shape[0] * columns,
            transcendentals=0,
        ),
        name="emit",
    )(where, weight, *parts, *extra)


def swap(value, axis, count, turn):
    return lax.ppermute(value, axis, [(i, i ^ turn) for i in range(count)])


def fast_body(tokens, in_weight, short_taps, skip_gain, long_filter, out_weight):
    seq, chans = lax.axis_size("seq"), lax.axis_size("chan")
    place, chan = lax.axis_index("seq"), lax.axis_index("chan")
    rows, width = tokens.shape
    length = rows * seq
    part = width // seq
    where = jnp.stack([place, chan]).astype(jnp.int32)

    weight = jnp.transpose(in_weight, (1, 0, 2))

    def far_part(parts, turn):
        return swap(parts[turn], "seq", seq, 2 * turn)

    theirs, ours, *cut1 = cut(where, [tokens], weight, 1, [long_filter], [])
    w1_2, w1_1 = far_part(cut1, 2), far_part(cut1, 1)
    far_ours = swap(ours, "seq", seq, 4)
    beside = swap(theirs, "seq", seq, 1)
    pair = join([ours, beside], [])
    far_beside = swap(beside, "seq", seq, 4)
    near = swap(pair, "seq", seq, 2)
    pair_across = swap(pair, "chan", chans, 2)
    far = join([far_ours, far_beside], [w1_2, w1_1])
    cut2 = cut(where, [], weight, 2, [], [far])
    w1_3 = far_part(cut1, 3)
    far_near = swap(far, "seq", seq, 2)
    w2_2 = far_part(cut2, 2)
    far_across = swap(far, "chan", chans, 2)
    near_across = swap(near, "chan", chans, 2)
    core_a = swap(join([pair, pair_across, near, near_across], [w1_3]), "chan", chans, 1)
    far_near_across = swap(far_near, "chan", chans, 2)
    cut0 = cut(where, [], weight, 0, [], [far_near])
    w2_1 = far_part(cut2, 1)
    w2_3 = far_part(cut2, 3)
    core_b = swap(
        join([far, far_across, far_near, far_near_across], [w2_2, w2_1]), "chan", chans, 1
    )
    w0_2, w0_1, w0_3 = far_part(cut0, 2), far_part(cut0, 1), far_part(cut0, 3)
    line, across = [pair, near, far, far_near], [
        pair_across,
        near_across,
        far_across,
        far_near_across,
    ]
    cores = [core_a, core_b]
    parts1 = [cut1[0], w1_1, w1_2, w1_3]
    parts2 = [cut2[0], w2_1, w2_2, w2_3]
    parts0 = [cut0[0], w0_1, w0_2, w0_3]

    taps = lax.dynamic_slice_in_dim(short_taps, place * part, part, 2)
    skip = lax.dynamic_slice_in_dim(skip_gain, place * part, part, 0)[None]
    own1, send1, lags_here = project(where, line, across, cores, parts1, length, [])
    recv1 = swap(send1, "seq", seq, 1)
    own2, send2 = project(where, line, across, cores, parts2, length, [w0_2, w0_1])
    recv2 = swap(send2, "seq", seq, 1)
    own0, send0 = project(where, line, across, cores, parts0, length, [])
    recv0 = swap(send0, "seq", seq, 1)
    mixed = mix(
        where, own1, recv1, own2, recv2, taps, skip, wave_tables(length), lags_here, recv1[length:]
    )
    pieces = gate(where, own0, recv0, mixed, taps)
    joined = [
        piece if turn == 0 else swap(piece, "seq", seq, turn) for turn, piece in enumerate(pieces)
    ]

    def share(turn, extra, dtype):
        return emit(jnp.stack([place, chan ^ turn]).astype(jnp.int32), joined, out_weight, extra, dtype)

    from_core = swap(share(3, [], jnp.bfloat16), "chan", chans, 1)
    near = swap(share(1, [], jnp.bfloat16), "chan", chans, 1)
    from_chip = swap(share(2, [from_core], jnp.bfloat16), "chan", chans, 2)
    own = share(0, [near], jnp.float32)
    return (own + from_chip.astype(jnp.float32)).astype(jnp.bfloat16)


def solution(mesh):
    in_specs = (
        P("seq", "chan"),
        P("seq", None, "chan"),
        P(None, None, "chan"),
        P("chan"),
        P("seq", "chan"),
        P("chan", None),
    )
    out_specs = P("seq", "chan")
    seq, chans = mesh.shape["seq"], mesh.shape["chan"]
    chosen = fast_body if seq == 8 and chans == 4 else body
    return jax.shard_map(chosen, mesh=mesh, in_specs=in_specs, out_specs=out_specs, check_vma=False)
```

```python
import functools
import math

import jax
import jax.numpy as jnp
import numpy as np
from jax import lax
from jax.experimental import pallas as pl
from jax.experimental.pallas import tpu as pltpu
from jax.sharding import PartitionSpec as P

exact_prec = lax.Precision.HIGHEST
inner_len = 64


def dft_tables(half_len, blocks):
    full_len = 2 * half_len
    full_size = full_len * blocks
    half_index = jnp.arange(half_len, dtype=jnp.int32)
    full_index = jnp.arange(full_len, dtype=jnp.int32)
    block_index = jnp.arange(blocks, dtype=jnp.int32)
    outer_angle = (half_index[:, None] * full_index[None, :] % full_len).astype(jnp.float32) * (
        2.0 * math.pi / full_len
    )
    inner_angle = (block_index[:, None] * block_index[None, :] % blocks).astype(jnp.float32) * (
        2.0 * math.pi / blocks
    )
    twist_angle = (full_index[:, None] * block_index[None, :] % full_size).astype(jnp.float32) * (
        2.0 * math.pi / full_size
    )
    return (
        jnp.cos(outer_angle),
        jnp.sin(outer_angle),
        jnp.cos(inner_angle),
        jnp.sin(inner_angle),
        jnp.cos(twist_angle),
        jnp.sin(twist_angle),
    )


def forward_dft(signal, tables):
    outer_cos, outer_sin, inner_cos, inner_sin, twist_cos, twist_sin = tables
    real_section = jnp.einsum("cmn,mk->ckn", signal, outer_cos, precision=exact_prec)
    imag_section = -jnp.einsum("cmn,mk->ckn", signal, outer_sin, precision=exact_prec)
    real_twist = real_section * twist_cos + imag_section * twist_sin
    imag_twist = imag_section * twist_cos - real_section * twist_sin
    real_freq = jnp.einsum("ckn,nj->ckj", real_twist, inner_cos, precision=exact_prec) + jnp.einsum(
        "ckn,nj->ckj", imag_twist, inner_sin, precision=exact_prec
    )
    imag_freq = jnp.einsum("ckn,nj->ckj", imag_twist, inner_cos, precision=exact_prec) - jnp.einsum(
        "ckn,nj->ckj", real_twist, inner_sin, precision=exact_prec
    )
    return (real_freq, imag_freq)


def inverse_real(spectrum_real, spectrum_imag, tables):
    outer_cos, outer_sin, inner_cos, inner_sin, twist_cos, twist_sin = tables
    full_size = outer_cos.shape[1] * inner_cos.shape[0]
    back_real = jnp.einsum(
        "ckj,jn->ckn", spectrum_real, inner_cos, precision=exact_prec
    ) - jnp.einsum("ckj,jn->ckn", spectrum_imag, inner_sin, precision=exact_prec)
    back_imag = jnp.einsum(
        "ckj,jn->ckn", spectrum_imag, inner_cos, precision=exact_prec
    ) + jnp.einsum("ckj,jn->ckn", spectrum_real, inner_sin, precision=exact_prec)
    turn_real = back_real * twist_cos - back_imag * twist_sin
    turn_imag = back_imag * twist_cos + back_real * twist_sin
    summed_real = jnp.einsum(
        "ckn,mk->cmn", turn_real, outer_cos, precision=exact_prec
    ) - jnp.einsum("ckn,mk->cmn", turn_imag, outer_sin, precision=exact_prec)
    return summed_real / full_size


def causal_conv(signal, kernel, blocks):
    channels, length = signal.shape
    half_len = length // blocks
    tables = dft_tables(half_len, blocks)
    stacked = jnp.concatenate([signal, kernel], 0).reshape(2 * channels, half_len, blocks)
    real_freq, imag_freq = forward_dft(stacked, tables)
    data_real, filter_real = (real_freq[:channels], real_freq[channels:])
    data_imag, filter_imag = (imag_freq[:channels], imag_freq[channels:])
    spectrum_real = data_real * filter_real - data_imag * filter_imag
    spectrum_imag = data_real * filter_imag + data_imag * filter_real
    return inverse_real(spectrum_real, spectrum_imag, tables).reshape(channels, length)


def body(tokens, in_weight, short_taps, skip_gain, long_filter, out_weight):
    row_count, chan_width = tokens.shape
    blocks = lax.axis_size("seq")
    part_width = chan_width // blocks
    flat_weight = in_weight.reshape(in_weight.shape[0], 3 * chan_width)
    whole = lax.all_gather(tokens, "chan", axis=1, tiled=True)
    projected = jnp.dot(
        whole,
        lax.all_gather(flat_weight, "seq", axis=0, tiled=True),
        preferred_element_type=jnp.float32,
    )
    projected = projected.astype(jnp.bfloat16).reshape(row_count, 3, chan_width)
    outgoing = jnp.transpose(projected, (1, 2, 0))
    filter_rows = jnp.transpose(long_filter)[None]
    channel_major, filter_major = (
        lax.all_to_all(outgoing, "seq", split_axis=1, concat_axis=2, tiled=True),
        lax.all_to_all(filter_rows, "seq", split_axis=1, concat_axis=2, tiled=True),
    )
    offset = lax.axis_index("seq") * part_width
    local_taps = lax.dynamic_slice_in_dim(short_taps, offset, part_width, 2)
    local_skip = lax.dynamic_slice_in_dim(skip_gain, offset, part_width, 0)
    values = channel_major.astype(jnp.float32)
    tap_count = short_taps.shape[1]
    length = values.shape[2]
    padded = jnp.pad(values, ((0, 0), (0, 0), (tap_count - 1, 0)))
    smoothed = jnp.zeros_like(values)
    for tap_index in range(tap_count):
        lag_start = tap_count - 1 - tap_index
        smoothed = (
            smoothed
            + local_taps[:, tap_index, :, None] * padded[:, :, lag_start : lag_start + length]
        )
    gate_query = smoothed[0]
    gated = smoothed[1] * smoothed[2]
    mixed_seq = (
        causal_conv(gated, filter_major[0].astype(jnp.float32), blocks)
        + local_skip[:, None] * gated
    )
    product = (mixed_seq * gate_query).astype(jnp.bfloat16)
    returned = lax.all_to_all(product, "seq", split_axis=1, concat_axis=0, tiled=True)
    summed = lax.psum_scatter(
        lax.dot_general(
            out_weight, returned, (((0,), (0,)), ((), ())), preferred_element_type=jnp.float32
        ).astype(jnp.bfloat16),
        "chan",
        scatter_dimension=0,
        tiled=True,
    ).astype(jnp.float32)
    return jnp.transpose(summed).astype(jnp.bfloat16)


def wave_tables(length):
    span = 2 * length
    outer = span // inner_len
    used, rows = outer // 2, outer // 2 + 1
    padded_rows = -(-rows // 8) * 8
    m, k = np.arange(used), np.arange(rows)
    n, j = np.arange(inner_len), np.arange(inner_len)
    angle = (2.0 * math.pi / outer) * (np.outer(k, m) % outer)
    ahead = np.zeros((2, padded_rows, used))
    ahead[0, :rows], ahead[1, :rows] = np.cos(angle), -np.sin(angle)
    weight = np.where((k == 0) | (k == used), 1.0, 2.0) / span
    back = np.zeros((used, 2, padded_rows))
    back[:, 0, :rows] = (np.cos(angle) * weight[:, None]).T
    back[:, 1, :rows] = (-np.sin(angle) * weight[:, None]).T
    turn = n[None, None, :] * (k[:, None, None] + outer * j[None, :, None]) % span
    cos, sin = np.cos(turn * (2.0 * math.pi / span)), np.sin(turn * (2.0 * math.pi / span))
    middle = np.concatenate(
        [np.concatenate([cos, sin], 2), np.concatenate([-sin, cos], 2)], 1
    )
    return tuple(
        jnp.asarray(table, jnp.bfloat16)
        for table in (
            ahead.reshape(2 * padded_rows, used),
            middle,
            np.swapaxes(middle, 1, 2),
            back.reshape(used, 2 * padded_rows),
        )
    )


def cut_kernel(where_ref, *refs, index, counts, after):
    place = where_ref[0]
    depth, side = place // 2, place % 2
    tokens, weight, filters = [
        refs[sum(counts[:i]) : sum(counts[: i + 1])] for i in range(3)
    ]
    outs, sems = list(refs[sum(counts) + after : -1]), refs[-1]
    copies = []

    def copy(source, target):
        copies.append(pltpu.make_async_copy(source, target, sems.at[len(copies)]))

    for source in tokens:
        half = outs[0].shape[1]
        for which in (1 - side, side):
            columns = pl.ds(pl.multiple_of(which * half, half), half)
            copy(source.at[:, columns], outs.pop(0))
    rows, width = weight[0].shape[1], outs[0].shape[1]
    for turn in (2, 1, 3, 0):
        start = pl.multiple_of(jnp.bitwise_xor(depth, turn) * width, width)
        columns = pl.ds(start, width)
        copy(weight[0].at[index, :, columns], outs[turn].at[pl.ds(0, rows), :])
        for source in filters:
            copy(source.at[:, columns], outs[turn].at[pl.ds(rows, source.shape[0]), :])
    for one in copies:
        one.start()
    for one in copies:
        one.wait()


def cut(where, tokens, weight, index, filters, after, limit):
    rows = weight.shape[1] + sum(value.shape[0] for value in filters)
    shapes = []
    for value in tokens:
        shapes += [jax.ShapeDtypeStruct((value.shape[0], value.shape[1] // 2), value.dtype)] * 2
    shapes += [jax.ShapeDtypeStruct((rows, weight.shape[2] // 4), weight.dtype)] * 4
    counts = (len(tokens), 1, len(filters))
    return pl.pallas_call(
        functools.partial(cut_kernel, index=index, counts=counts, after=len(after)),
        out_shape=tuple(shapes),
        in_specs=[pl.BlockSpec(memory_space=pltpu.SMEM)]
        + [pl.BlockSpec(memory_space=pltpu.HBM)] * sum(counts)
        + [pl.BlockSpec(memory_space=pl.ANY)] * len(after),
        out_specs=(pl.BlockSpec(memory_space=pltpu.VMEM),) * len(shapes),
        scratch_shapes=[pltpu.SemaphoreType.DMA((10,))],
        compiler_params=pltpu.CompilerParams(vmem_limit_bytes=limit),
        name="cut",
    )(where, *tokens, weight, *filters, *after)


def join_kernel(*refs, count):
    out_ref = refs[-1]
    start = 0
    for source in refs[:count]:
        out_ref[start : start + source.shape[0], :] = source[...]
        start += source.shape[0]


def join(values, after):
    rows = sum(value.shape[0] for value in values)
    vmem = pl.BlockSpec(memory_space=pltpu.VMEM)
    return pl.pallas_call(
        functools.partial(join_kernel, count=len(values)),
        out_shape=jax.ShapeDtypeStruct((rows, values[0].shape[1]), values[0].dtype),
        in_specs=[vmem] * len(values) + [pl.BlockSpec(memory_space=pl.ANY)] * len(after),
        out_specs=vmem,
        compiler_params=pltpu.CompilerParams(vmem_limit_bytes=8 * 2**20),
        name="join",
    )(*values, *after)


def project_kernel(where_ref, *refs, filter_rows, after):
    line, across, cores, parts = refs[:4], refs[4:8], refs[8:10], refs[10:14]
    if filter_rows:
        own_ref, send_ref, lags_ref, weights = refs[14 + after :]
    else:
        own_ref, send_ref, weights = refs[14 + after :]
    place, chan = where_ref[0], where_ref[1]
    depth, side = place // 2, place % 2
    rows = line[0].shape[1]
    for i in range(4):
        slot = jnp.bitwise_xor(depth, jnp.bitwise_xor(chan, i))
        start = pl.multiple_of(slot * rows, rows)
        weights[pl.ds(start, rows), :] = parts[i][0:rows, :]
    length, half = own_ref.shape
    block = length // 8
    for step in range(4):
        low = 4 * block * (step % 2)
        both = cores[step // 2]
        joined = jnp.concatenate(
            [
                line[step][...],
                both[low : low + 2 * block, :],
                across[step][...],
                both[low + 2 * block : low + 4 * block, :],
            ],
            1,
        )
        total = jnp.dot(joined, weights[...], preferred_element_type=jnp.float32)
        left, right = total[:, :half], total[:, half:]
        own = jnp.where(side == 0, left, right)
        send = jnp.where(side == 0, right, left).astype(jnp.bfloat16)
        for pair in range(2):
            start = pl.multiple_of(jnp.bitwise_xor(place, 2 * step + pair) * block, block)
            own_ref[pl.ds(start, block), :] = own[pair * block : (pair + 1) * block]
            send_ref[pl.ds(start, block), :] = send[pair * block : (pair + 1) * block]
    if filter_rows:
        for i in range(4):
            piece = parts[i][rows:, :].astype(jnp.float32)
            left, right = piece[:, :half], piece[:, half:]
            at = slice(i * filter_rows, (i + 1) * filter_rows)
            lags_ref[at, :] = jnp.where(side == 0, left, right).astype(jnp.bfloat16)
            at = slice(length + i * filter_rows, length + (i + 1) * filter_rows)
            send_ref[at, :] = jnp.where(side == 0, right, left).astype(jnp.bfloat16)


def project(where, line, across, cores, parts, length, after):
    depth, width = line[0].shape[1], parts[0].shape[1]
    filter_rows = parts[0].shape[0] - depth
    vmem = pl.BlockSpec(memory_space=pltpu.VMEM)
    shapes = [
        jax.ShapeDtypeStruct((length, width // 2), jnp.float32),
        jax.ShapeDtypeStruct((length + 4 * filter_rows, width // 2), jnp.bfloat16),
    ]
    if filter_rows:
        shapes.append(jax.ShapeDtypeStruct((4 * filter_rows, width // 2), jnp.bfloat16))
    return pl.pallas_call(
        functools.partial(project_kernel, filter_rows=filter_rows, after=len(after)),
        out_shape=tuple(shapes),
        in_specs=[pl.BlockSpec(memory_space=pltpu.SMEM)]
        + [vmem] * 14
        + [pl.BlockSpec(memory_space=pl.ANY)] * len(after),
        out_specs=(vmem,) * len(shapes),
        scratch_shapes=[pltpu.VMEM((4 * depth, width), jnp.bfloat16)],
        compiler_params=pltpu.CompilerParams(vmem_limit_bytes=12 * 2**20),
        cost_estimate=pl.CostEstimate(
            flops=2 * length * 4 * depth * width,
            bytes_accessed=2 * length * 4 * depth,
            transcendentals=0,
        ),
        name="project",
    )(where, *line, *across, *cores, *parts, *after)


def smooth_into(padded, own_ref, recv_ref, taps_ref, branch, store):
    length = own_ref.shape[0]
    tap_count = taps_ref.shape[1]
    block = length // 8
    padded[0:8, :] = jnp.zeros((8, padded.shape[1]), jnp.float32)
    for i in range(8):
        rows = slice(i * block, (i + 1) * block)
        padded[8 + i * block : 8 + (i + 1) * block, :] = own_ref[rows, :] + recv_ref[
            rows, :
        ].astype(jnp.float32)
    for i in range(8):
        total = None
        for tap in range(tap_count):
            start = 8 + i * block - tap
            term = taps_ref[branch, tap : tap + 1, :] * padded[start : start + block, :]
            total = term if total is None else total + term
        store(slice(i * block, (i + 1) * block), total)


def mix_kernel(
    where_ref,
    own1,
    recv1,
    own2,
    recv2,
    taps_ref,
    skip_ref,
    ahead,
    middle,
    middle_back,
    back,
    *refs,
    after,
):
    lags_here, lags_there = refs[:2]
    mixed_ref, padded, gated, lags, waves, filter_waves, sums = refs[2 + after :]
    place = where_ref[0]
    length, width = own1.shape
    block = length // 8
    rows, two = middle.shape[0], middle.shape[1]
    padded_rows = ahead.shape[0] // 2
    used = ahead.shape[1]
    for i in range(4):
        at = slice(i * block, (i + 1) * block)
        for side, source in enumerate((lags_here, lags_there)):
            start = pl.multiple_of(jnp.bitwise_xor(place, 2 * i + side) * block, block)
            lags[pl.ds(start, block), :] = source[at, :].astype(jnp.float32)

    def first(at, value):
        gated[at, :] = value

    def second(at, value):
        gated[at, :] = gated[at, :] * value

    smooth_into(padded, own1, recv1, taps_ref, 1, first)
    smooth_into(padded, own2, recv2, taps_ref, 2, second)
    for n in range(inner_len):
        both = jnp.concatenate(
            [gated[pl.ds(n, used, stride=inner_len), :], lags[pl.ds(n, used, stride=inner_len), :]],
            1,
        ).astype(jnp.bfloat16)
        wave = jnp.dot(ahead[...], both, preferred_element_type=jnp.float32)
        for i in range(2):
            at = pl.ds(i * inner_len + n, padded_rows, stride=two)
            part = wave[i * padded_rows : (i + 1) * padded_rows]
            waves[at, :] = part[:, :width]
            filter_waves[at, :] = part[:, width:]
    if padded_rows > rows:
        sums[rows * two :, :] = jnp.zeros(((padded_rows - rows) * two, width), jnp.float32)

    def one(k, _):
        at = pl.ds(pl.multiple_of(k * two, two), two)
        both = jnp.concatenate([waves[at, :], filter_waves[at, :]], 1).astype(jnp.bfloat16)
        freq = jnp.dot(middle[k], both, preferred_element_type=jnp.float32)
        data_real, filter_real = freq[:inner_len, :width], freq[:inner_len, width:]
        data_imag, filter_imag = freq[inner_len:, :width], freq[inner_len:, width:]
        spectrum = jnp.concatenate(
            [
                data_real * filter_real - data_imag * filter_imag,
                data_real * filter_imag + data_imag * filter_real,
            ],
            0,
        ).astype(jnp.bfloat16)
        sums[at, :] = jnp.dot(middle_back[k], spectrum, preferred_element_type=jnp.float32)
        return 0

    lax.fori_loop(0, rows, one, 0, unroll=11 if rows % 11 == 0 else 1)
    for n in range(0, inner_len, 2):
        pieces = [
            jnp.concatenate(
                [
                    sums[pl.ds(n + i, padded_rows, stride=two), :],
                    sums[pl.ds(inner_len + n + i, padded_rows, stride=two), :],
                ],
                0,
            )
            for i in range(2)
        ]
        wave = jnp.dot(
            back[...],
            jnp.concatenate(pieces, 1).astype(jnp.bfloat16),
            preferred_element_type=jnp.float32,
        )
        for i in range(2):
            at = pl.ds(n + i, used, stride=inner_len)
            mixed_ref[at, :] = wave[:, i * width : (i + 1) * width] + skip_ref[...] * gated[at, :]


def mix(where, own1, recv1, own2, recv2, taps, skip, tables, lags_here, lags_there, after):
    length, width = own1.shape
    rows, two = tables[1].shape[:2]
    padded_rows = tables[0].shape[0] // 2
    vmem = pl.BlockSpec(memory_space=pltpu.VMEM)
    return pl.pallas_call(
        functools.partial(mix_kernel, after=len(after)),
        out_shape=jax.ShapeDtypeStruct((length, width), jnp.float32),
        in_specs=[pl.BlockSpec(memory_space=pltpu.SMEM)]
        + [vmem] * 12
        + [pl.BlockSpec(memory_space=pl.ANY)] * len(after),
        out_specs=vmem,
        scratch_shapes=[
            pltpu.VMEM((length + 8, width), jnp.float32),
            pltpu.VMEM((length, width), jnp.float32),
            pltpu.VMEM((length, width), jnp.float32),
            pltpu.VMEM((padded_rows * two, width), jnp.float32),
            pltpu.VMEM((padded_rows * two, width), jnp.float32),
            pltpu.VMEM((padded_rows * two, width), jnp.float32),
        ],
        compiler_params=pltpu.CompilerParams(vmem_limit_bytes=20 * 2**20),
        cost_estimate=pl.CostEstimate(
            flops=2 * 8 * length * inner_len * width, bytes_accessed=6 * 2**20, transcendentals=0
        ),
        name="mix",
    )(where, own1, recv1, own2, recv2, taps, skip, *tables, lags_here, lags_there, *after)


def gate_kernel(where_ref, own0, recv0, mixed_ref, taps_ref, *refs):
    outs, padded, product = refs[:8], refs[8], refs[9]
    place = where_ref[0]
    block = own0.shape[0] // 8

    def store(at, value):
        product[at, :] = (mixed_ref[at, :] * value).astype(jnp.bfloat16)

    smooth_into(padded, own0, recv0, taps_ref, 0, store)
    for i in range(8):
        start = pl.multiple_of(jnp.bitwise_xor(place, i) * block, block)
        outs[i][...] = product[pl.ds(start, block), :]


def gate(where, own0, recv0, mixed, taps):
    length, width = own0.shape
    vmem = pl.BlockSpec(memory_space=pltpu.VMEM)
    return pl.pallas_call(
        gate_kernel,
        out_shape=(jax.ShapeDtypeStruct((length // 8, width), jnp.bfloat16),) * 8,
        in_specs=[pl.BlockSpec(memory_space=pltpu.SMEM)] + [vmem] * 4,
        out_specs=(vmem,) * 8,
        scratch_shapes=[
            pltpu.VMEM((length + 8, width), jnp.float32),
            pltpu.VMEM((length, width), jnp.bfloat16),
        ],
        compiler_params=pltpu.CompilerParams(vmem_limit_bytes=8 * 2**20),
        cost_estimate=pl.CostEstimate(
            flops=8 * length * width, bytes_accessed=12 * length * width, transcendentals=0
        ),
        name="gate",
    )(where, own0, recv0, mixed, taps)


def emit_kernel(where_ref, weight, *refs, turns, added):
    parts, extra = refs[:8], refs[8 : 8 + added]
    outs = refs[8 + added : 8 + added + len(turns)]
    joined, tiles, sems = refs[8 + added + len(turns) :]
    place, chan = where_ref[0], where_ref[1]
    width = parts[0].shape[1]
    columns = outs[0].shape[1]
    count, depth, _ = tiles.shape
    copies = []
    for i, turn in enumerate(turns):
        start = pl.multiple_of(jnp.bitwise_xor(chan, turn) * columns, columns)
        for step in range(count // len(turns)):
            slot = i * (count // len(turns)) + step
            source = weight.at[pl.ds(step * depth, depth), pl.ds(start, columns)]
            copies.append(pltpu.make_async_copy(source, tiles.at[slot], sems.at[slot]))
            copies[slot].start()
    for i in range(8):
        start = pl.multiple_of(jnp.bitwise_xor(place, i) * width, width)
        joined[:, pl.ds(start, width)] = parts[i][...]
    for i in range(len(turns)):
        total = None
        for step in range(count // len(turns)):
            slot = i * (count // len(turns)) + step
            copies[slot].wait()
            term = jnp.dot(
                joined[:, step * depth : (step + 1) * depth],
                tiles[slot],
                preferred_element_type=jnp.float32,
            )
            total = term if total is None else total + term
        if added:
            total = total + extra[i][...].astype(jnp.float32)
        outs[i][...] = total.astype(outs[i].dtype)


def emit(where, parts, weight, turns, extra, out_dtype):
    rows, width = parts[0].shape
    columns = weight.shape[1] // 4
    steps = 4
    vmem = pl.BlockSpec(memory_space=pltpu.VMEM)
    shape = jax.ShapeDtypeStruct((rows, columns), out_dtype)
    return pl.pallas_call(
        functools.partial(emit_kernel, turns=turns, added=len(extra)),
        out_shape=(shape,) * len(turns),
        in_specs=[
            pl.BlockSpec(memory_space=pltpu.SMEM),
            pl.BlockSpec(memory_space=pl.ANY),
        ]
        + [vmem] * (8 + len(extra)),
        out_specs=(vmem,) * len(turns),
        scratch_shapes=[
            pltpu.VMEM((rows, 8 * width), jnp.bfloat16),
            pltpu.VMEM((steps * len(turns), weight.shape[0] // steps, columns), jnp.bfloat16),
            pltpu.SemaphoreType.DMA((steps * len(turns),)),
        ],
        compiler_params=pltpu.CompilerParams(vmem_limit_bytes=57 * 2**20),
        cost_estimate=pl.CostEstimate(
            flops=2 * rows * weight.shape[0] * columns * len(turns),
            bytes_accessed=2 * weight.shape[0] * columns * len(turns),
            transcendentals=0,
        ),
        name="emit",
    )(where, weight, *parts, *extra)


def swap(value, axis, count, turn):
    return lax.ppermute(value, axis, [(i, i ^ turn) for i in range(count)])


def fast_body(tokens, in_weight, short_taps, skip_gain, long_filter, out_weight):
    seq, chans = lax.axis_size("seq"), lax.axis_size("chan")
    place, chan = lax.axis_index("seq"), lax.axis_index("chan")
    rows, width = tokens.shape
    length = rows * seq
    part = width // seq
    where = jnp.stack([place, chan]).astype(jnp.int32)

    weight = jnp.transpose(in_weight, (1, 0, 2))

    def far_part(parts, turn):
        return swap(parts[turn], "seq", seq, 2 * turn)

    theirs, ours, *cut1 = cut(where, [tokens], weight, 1, [long_filter], [], 56 * 2**20)
    w1_2, w1_1 = far_part(cut1, 2), far_part(cut1, 1)
    far_ours = swap(ours, "seq", seq, 4)
    beside = swap(theirs, "seq", seq, 1)
    pair = join([ours, beside], [])
    far_beside = swap(beside, "seq", seq, 4)
    near = swap(pair, "seq", seq, 2)
    pair_across = swap(pair, "chan", chans, 2)
    far = join([far_ours, far_beside], [w1_2, w1_1])
    cut2 = cut(where, [], weight, 2, [], [near], 8 * 2**20)
    w1_3 = far_part(cut1, 3)
    far_near = swap(far, "seq", seq, 2)
    w2_2 = far_part(cut2, 2)
    far_across = swap(far, "chan", chans, 2)
    near_across = swap(near, "chan", chans, 2)
    core_a = swap(join([pair, pair_across, near, near_across], [w1_3]), "chan", chans, 1)
    far_near_across = swap(far_near, "chan", chans, 2)
    cut0 = cut(where, [], weight, 0, [], [far_near], 8 * 2**20)
    w2_1 = far_part(cut2, 1)
    w2_3 = far_part(cut2, 3)
    core_b = swap(
        join([far, far_across, far_near, far_near_across], [w2_2, w2_1]), "chan", chans, 1
    )
    w0_2, w0_1, w0_3 = far_part(cut0, 2), far_part(cut0, 1), far_part(cut0, 3)
    line, across = [pair, near, far, far_near], [
        pair_across,
        near_across,
        far_across,
        far_near_across,
    ]
    cores = [core_a, core_b]
    parts1 = [cut1[0], w1_1, w1_2, w1_3]
    parts2 = [cut2[0], w2_1, w2_2, w2_3]
    parts0 = [cut0[0], w0_1, w0_2, w0_3]

    taps = lax.dynamic_slice_in_dim(short_taps, place * part, part, 2)
    skip = lax.dynamic_slice_in_dim(skip_gain, place * part, part, 0)[None]
    own1, send1, lags_here = project(where, line, across, cores, parts1, length, [])
    recv1 = swap(send1, "seq", seq, 1)
    own2, send2 = project(where, line, across, cores, parts2, length, [])
    recv2 = swap(send2, "seq", seq, 1)
    own0, send0 = project(where, line, across, cores, parts0, length, [])
    recv0 = swap(send0, "seq", seq, 1)
    mixed = mix(
        where, own1, recv1, own2, recv2, taps, skip, wave_tables(length), lags_here, recv1[length:], [send0]
    )
    pieces = gate(where, own0, recv0, mixed, taps)
    joined = [
        piece if turn == 0 else swap(piece, "seq", seq, turn) for turn, piece in enumerate(pieces)
    ]

    across_out, beside_out = emit(where, joined, out_weight, (3, 1), [], jnp.bfloat16)
    from_core = swap(across_out, "chan", chans, 1)
    near_sum = swap(beside_out, "chan", chans, 1)
    (chip_out,) = emit(where, joined, out_weight, (2,), [from_core], jnp.bfloat16)
    from_chip = swap(chip_out, "chan", chans, 2)
    (own,) = emit(where, joined, out_weight, (0,), [near_sum], jnp.float32)
    return (own + from_chip.astype(jnp.float32)).astype(jnp.bfloat16)


def solution(mesh):
    in_specs = (
        P("seq", "chan"),
        P("seq", None, "chan"),
        P(None, None, "chan"),
        P("chan"),
        P("seq", "chan"),
        P("chan", None),
    )
    out_specs = P("seq", "chan")
    seq, chans = mesh.shape["seq"], mesh.shape["chan"]
    chosen = fast_body if seq == 8 and chans == 4 else body
    return jax.shard_map(chosen, mesh=mesh, in_specs=in_specs, out_specs=out_specs, check_vma=False)
```

```python
import functools
import math

import jax
import jax.numpy as jnp
import numpy as np
from jax import lax
from jax.experimental import pallas as pl
from jax.experimental.pallas import tpu as pltpu
from jax.sharding import PartitionSpec as P

exact_prec = lax.Precision.HIGHEST
inner_len = 64


def dft_tables(half_len, blocks):
    full_len = 2 * half_len
    full_size = full_len * blocks
    half_index = jnp.arange(half_len, dtype=jnp.int32)
    full_index = jnp.arange(full_len, dtype=jnp.int32)
    block_index = jnp.arange(blocks, dtype=jnp.int32)
    outer_angle = (half_index[:, None] * full_index[None, :] % full_len).astype(jnp.float32) * (
        2.0 * math.pi / full_len
    )
    inner_angle = (block_index[:, None] * block_index[None, :] % blocks).astype(jnp.float32) * (
        2.0 * math.pi / blocks
    )
    twist_angle = (full_index[:, None] * block_index[None, :] % full_size).astype(jnp.float32) * (
        2.0 * math.pi / full_size
    )
    return (
        jnp.cos(outer_angle),
        jnp.sin(outer_angle),
        jnp.cos(inner_angle),
        jnp.sin(inner_angle),
        jnp.cos(twist_angle),
        jnp.sin(twist_angle),
    )


def forward_dft(signal, tables):
    outer_cos, outer_sin, inner_cos, inner_sin, twist_cos, twist_sin = tables
    real_section = jnp.einsum("cmn,mk->ckn", signal, outer_cos, precision=exact_prec)
    imag_section = -jnp.einsum("cmn,mk->ckn", signal, outer_sin, precision=exact_prec)
    real_twist = real_section * twist_cos + imag_section * twist_sin
    imag_twist = imag_section * twist_cos - real_section * twist_sin
    real_freq = jnp.einsum("ckn,nj->ckj", real_twist, inner_cos, precision=exact_prec) + jnp.einsum(
        "ckn,nj->ckj", imag_twist, inner_sin, precision=exact_prec
    )
    imag_freq = jnp.einsum("ckn,nj->ckj", imag_twist, inner_cos, precision=exact_prec) - jnp.einsum(
        "ckn,nj->ckj", real_twist, inner_sin, precision=exact_prec
    )
    return (real_freq, imag_freq)


def inverse_real(spectrum_real, spectrum_imag, tables):
    outer_cos, outer_sin, inner_cos, inner_sin, twist_cos, twist_sin = tables
    full_size = outer_cos.shape[1] * inner_cos.shape[0]
    back_real = jnp.einsum(
        "ckj,jn->ckn", spectrum_real, inner_cos, precision=exact_prec
    ) - jnp.einsum("ckj,jn->ckn", spectrum_imag, inner_sin, precision=exact_prec)
    back_imag = jnp.einsum(
        "ckj,jn->ckn", spectrum_imag, inner_cos, precision=exact_prec
    ) + jnp.einsum("ckj,jn->ckn", spectrum_real, inner_sin, precision=exact_prec)
    turn_real = back_real * twist_cos - back_imag * twist_sin
    turn_imag = back_imag * twist_cos + back_real * twist_sin
    summed_real = jnp.einsum(
        "ckn,mk->cmn", turn_real, outer_cos, precision=exact_prec
    ) - jnp.einsum("ckn,mk->cmn", turn_imag, outer_sin, precision=exact_prec)
    return summed_real / full_size


def causal_conv(signal, kernel, blocks):
    channels, length = signal.shape
    half_len = length // blocks
    tables = dft_tables(half_len, blocks)
    stacked = jnp.concatenate([signal, kernel], 0).reshape(2 * channels, half_len, blocks)
    real_freq, imag_freq = forward_dft(stacked, tables)
    data_real, filter_real = (real_freq[:channels], real_freq[channels:])
    data_imag, filter_imag = (imag_freq[:channels], imag_freq[channels:])
    spectrum_real = data_real * filter_real - data_imag * filter_imag
    spectrum_imag = data_real * filter_imag + data_imag * filter_real
    return inverse_real(spectrum_real, spectrum_imag, tables).reshape(channels, length)


def body(tokens, in_weight, short_taps, skip_gain, long_filter, out_weight):
    row_count, chan_width = tokens.shape
    blocks = lax.axis_size("seq")
    part_width = chan_width // blocks
    flat_weight = in_weight.reshape(in_weight.shape[0], 3 * chan_width)
    whole = lax.all_gather(tokens, "chan", axis=1, tiled=True)
    projected = jnp.dot(
        whole,
        lax.all_gather(flat_weight, "seq", axis=0, tiled=True),
        preferred_element_type=jnp.float32,
    )
    projected = projected.astype(jnp.bfloat16).reshape(row_count, 3, chan_width)
    outgoing = jnp.transpose(projected, (1, 2, 0))
    filter_rows = jnp.transpose(long_filter)[None]
    channel_major, filter_major = (
        lax.all_to_all(outgoing, "seq", split_axis=1, concat_axis=2, tiled=True),
        lax.all_to_all(filter_rows, "seq", split_axis=1, concat_axis=2, tiled=True),
    )
    offset = lax.axis_index("seq") * part_width
    local_taps = lax.dynamic_slice_in_dim(short_taps, offset, part_width, 2)
    local_skip = lax.dynamic_slice_in_dim(skip_gain, offset, part_width, 0)
    values = channel_major.astype(jnp.float32)
    tap_count = short_taps.shape[1]
    length = values.shape[2]
    padded = jnp.pad(values, ((0, 0), (0, 0), (tap_count - 1, 0)))
    smoothed = jnp.zeros_like(values)
    for tap_index in range(tap_count):
        lag_start = tap_count - 1 - tap_index
        smoothed = (
            smoothed
            + local_taps[:, tap_index, :, None] * padded[:, :, lag_start : lag_start + length]
        )
    gate_query = smoothed[0]
    gated = smoothed[1] * smoothed[2]
    mixed_seq = (
        causal_conv(gated, filter_major[0].astype(jnp.float32), blocks)
        + local_skip[:, None] * gated
    )
    product = (mixed_seq * gate_query).astype(jnp.bfloat16)
    returned = lax.all_to_all(product, "seq", split_axis=1, concat_axis=0, tiled=True)
    summed = lax.psum_scatter(
        lax.dot_general(
            out_weight, returned, (((0,), (0,)), ((), ())), preferred_element_type=jnp.float32
        ).astype(jnp.bfloat16),
        "chan",
        scatter_dimension=0,
        tiled=True,
    ).astype(jnp.float32)
    return jnp.transpose(summed).astype(jnp.bfloat16)


def wave_tables(length):
    span = 2 * length
    outer = span // inner_len
    used, rows = outer // 2, outer // 2 + 1
    padded_rows = -(-rows // 8) * 8
    m, k = np.arange(used), np.arange(rows)
    n, j = np.arange(inner_len), np.arange(inner_len)
    angle = (2.0 * math.pi / outer) * (np.outer(k, m) % outer)
    ahead = np.zeros((2, padded_rows, used))
    ahead[0, :rows], ahead[1, :rows] = np.cos(angle), -np.sin(angle)
    weight = np.where((k == 0) | (k == used), 1.0, 2.0) / span
    back = np.zeros((used, 2, padded_rows))
    back[:, 0, :rows] = (np.cos(angle) * weight[:, None]).T
    back[:, 1, :rows] = (-np.sin(angle) * weight[:, None]).T
    turn = n[None, None, :] * (k[:, None, None] + outer * j[None, :, None]) % span
    cos, sin = np.cos(turn * (2.0 * math.pi / span)), np.sin(turn * (2.0 * math.pi / span))
    middle = np.concatenate(
        [np.concatenate([cos, sin], 2), np.concatenate([-sin, cos], 2)], 1
    )
    return tuple(
        jnp.asarray(table, jnp.bfloat16)
        for table in (
            ahead.reshape(2 * padded_rows, used),
            middle,
            np.swapaxes(middle, 1, 2),
            back.reshape(used, 2 * padded_rows),
        )
    )


def halve_kernel(
    where_ref, tokens, filters, weight, theirs, ours, filter_theirs, *refs, turns, index
):
    pieces, sems = refs[:-1], refs[-1]
    depth, side = where_ref[0] // 2, where_ref[0] % 2
    half = ours.shape[1]
    part = half // 4
    copies = []

    def copy(source, block, width, target):
        columns = pl.ds(pl.multiple_of(block * width, width), width)
        copies.append(
            pltpu.make_async_copy(source.at[:, columns], target, sems.at[len(copies)])
        )

    copy(tokens, side, half, ours)
    copy(tokens, 1 - side, half, theirs)
    for i in range(4):
        copy(filters, 2 * i + 1 - side, part, filter_theirs.at[:, pl.ds(i * part, part)])
    for turn, piece in zip(turns, pieces, strict=True):
        copy(weight.at[index], jnp.bitwise_xor(depth, turn), piece.shape[1], piece)
    for one in copies:
        one.start()
    for one in copies:
        one.wait()


def halve(where, tokens, filters, weight, turns, index):
    shapes = []
    for value in (tokens, tokens, filters):
        shapes.append(jax.ShapeDtypeStruct((value.shape[0], value.shape[1] // 2), value.dtype))
    shapes += [jax.ShapeDtypeStruct((weight.shape[1], weight.shape[2] // 4), weight.dtype)] * len(
        turns
    )
    return pl.pallas_call(
        functools.partial(halve_kernel, turns=turns, index=index),
        out_shape=tuple(shapes),
        in_specs=[pl.BlockSpec(memory_space=pltpu.SMEM)]
        + [pl.BlockSpec(memory_space=pl.ANY)] * 3,
        out_specs=(pl.BlockSpec(memory_space=pltpu.VMEM),) * len(shapes),
        scratch_shapes=[pltpu.SemaphoreType.DMA((6 + len(turns),))],
        compiler_params=pltpu.CompilerParams(vmem_limit_bytes=61 * 2**20),
        name="halve",
    )(where, tokens, filters, weight)


def cut_kernel(where_ref, weight, filters, filter_beside, *refs, plan, after):
    place = where_ref[0]
    depth, side = place // 2, place % 2
    outs, sems = refs[after:-1], refs[-1]
    copies = []

    def copy(source, target):
        copies.append(pltpu.make_async_copy(source, target, sems.at[len(copies)]))

    def columns_of(block, width):
        return pl.ds(pl.multiple_of(block * width, width), width)

    rows, width = weight.shape[1], outs[0].shape[1]
    half = width // 2
    for out, (turn, names) in zip(outs, plan, strict=True):
        block = jnp.bitwise_xor(depth, turn)
        low = 0
        for name in names:
            if name == "f":
                at = pl.ds(low, filters.shape[0])
                here = columns_of(2 * block + side, half)
                copy(filters.at[:, here], out.at[at, pl.ds(0, half)])
                there = columns_of(block, half)
                copy(filter_beside.at[:, there], out.at[at, pl.ds(half, half)])
                low += filters.shape[0]
            else:
                source = weight.at[name, :, columns_of(block, width)]
                copy(source, out.at[pl.ds(low, rows), :])
                low += rows
    for one in copies:
        one.start()
    for one in copies:
        one.wait()


def cut(where, weight, filters, filter_beside, plan, after):
    count_of = {"f": filters.shape[0]}
    shapes = []
    for _, names in plan:
        rows = sum(count_of.get(name, weight.shape[1]) for name in names)
        shapes.append(jax.ShapeDtypeStruct((rows, weight.shape[2] // 4), weight.dtype))
    return pl.pallas_call(
        functools.partial(cut_kernel, plan=plan, after=len(after)),
        out_shape=tuple(shapes),
        in_specs=[pl.BlockSpec(memory_space=pltpu.SMEM)]
        + [pl.BlockSpec(memory_space=pl.ANY)] * (3 + len(after)),
        out_specs=(pl.BlockSpec(memory_space=pltpu.VMEM),) * len(shapes),
        scratch_shapes=[pltpu.SemaphoreType.DMA((24,))],
        compiler_params=pltpu.CompilerParams(vmem_limit_bytes=8 * 2**20),
        name="cut",
    )(where, weight, filters, filter_beside, *after)


def join_kernel(*refs, pieces, outs):
    for out_ref, group in zip(refs[len(refs) - outs :], pieces, strict=True):
        start = 0
        for at, low, count in group:
            out_ref[start : start + count, :] = refs[at][low : low + count, :]
            start += count


def join(values, pieces, after):
    shapes = []
    for group in pieces:
        rows = sum(count for _, _, count in group)
        shapes.append(jax.ShapeDtypeStruct((rows, values[0].shape[1]), values[0].dtype))
    vmem = pl.BlockSpec(memory_space=pltpu.VMEM)
    return pl.pallas_call(
        functools.partial(join_kernel, pieces=pieces, outs=len(pieces)),
        out_shape=tuple(shapes),
        in_specs=[vmem] * len(values) + [pl.BlockSpec(memory_space=pl.ANY)] * len(after),
        out_specs=(vmem,) * len(shapes),
        compiler_params=pltpu.CompilerParams(vmem_limit_bytes=8 * 2**20),
        name="join",
    )(*values, *after)


def project_kernel(where_ref, *refs, lows, after):
    line, across, cores, parts = refs[:4], refs[4:7], refs[7:9], refs[9:13]
    own_ref, send_ref, weights = refs[13 + after :]
    place, chan = where_ref[0], where_ref[1]
    depth, side = place // 2, place % 2
    rows = line[0].shape[1]
    for i in range(4):
        slot = jnp.bitwise_xor(depth, jnp.bitwise_xor(chan, i))
        start = pl.multiple_of(slot * rows, rows)
        weights[pl.ds(start, rows), :] = parts[i][lows[i] : lows[i] + rows, :]
    length, half = own_ref.shape
    block = length // 8
    for step in range(4):
        low = 4 * block * (step % 2)
        both = cores[step // 2]
        beside = across[(0, 1, 1, 2)[step]]
        at = 2 * block if step == 1 else 0
        joined = jnp.concatenate(
            [
                line[step][...],
                both[low : low + 2 * block, :],
                beside[at : at + 2 * block, :],
                both[low + 2 * block : low + 4 * block, :],
            ],
            1,
        )
        total = jnp.dot(joined, weights[...], preferred_element_type=jnp.float32)
        left, right = total[:, :half], total[:, half:]
        own = jnp.where(side == 0, left, right)
        send = jnp.where(side == 0, right, left).astype(jnp.bfloat16)
        for pair in range(2):
            start = pl.multiple_of(jnp.bitwise_xor(place, 2 * step + pair) * block, block)
            own_ref[pl.ds(start, block), :] = own[pair * block : (pair + 1) * block]
            send_ref[pl.ds(start, block), :] = send[pair * block : (pair + 1) * block]


def project(where, line, across, cores, parts, lows, length, after):
    depth, width = line[0].shape[1], parts[0].shape[1]
    vmem = pl.BlockSpec(memory_space=pltpu.VMEM)
    return pl.pallas_call(
        functools.partial(project_kernel, lows=lows, after=len(after)),
        out_shape=(
            jax.ShapeDtypeStruct((length, width // 2), jnp.float32),
            jax.ShapeDtypeStruct((length, width // 2), jnp.bfloat16),
        ),
        in_specs=[pl.BlockSpec(memory_space=pltpu.SMEM)]
        + [vmem] * 13
        + [pl.BlockSpec(memory_space=pl.ANY)] * len(after),
        out_specs=(vmem, vmem),
        scratch_shapes=[pltpu.VMEM((4 * depth, width), jnp.bfloat16)],
        compiler_params=pltpu.CompilerParams(vmem_limit_bytes=12 * 2**20),
        cost_estimate=pl.CostEstimate(
            flops=2 * length * 4 * depth * 2 * width,
            bytes_accessed=2 * length * 4 * depth,
            transcendentals=0,
        ),
        name="project",
    )(where, *line, *across, *cores, *parts, *after)


def smooth_into(padded, own_ref, recv_ref, taps, branch, store):
    length = own_ref.shape[0]
    tap_count = taps.shape[1]
    block = length // 8
    padded[0:8, :] = jnp.zeros((8, padded.shape[1]), jnp.float32)
    for i in range(8):
        rows = slice(i * block, (i + 1) * block)
        padded[8 + i * block : 8 + (i + 1) * block, :] = own_ref[rows, :] + recv_ref[
            rows, :
        ].astype(jnp.float32)
    for i in range(8):
        total = None
        for tap in range(tap_count):
            start = 8 + i * block - tap
            term = taps[branch, tap : tap + 1, :] * padded[start : start + block, :]
            total = term if total is None else total + term
        store(slice(i * block, (i + 1) * block), total)


def ahead_into(signal, table, waves):
    padded_rows, used = table.shape[0] // 2, table.shape[1]
    two = 2 * inner_len
    for n in range(0, inner_len, 2):
        both = jnp.concatenate(
            [signal[pl.ds(n + i, used, stride=inner_len), :] for i in range(2)], 1
        ).astype(jnp.bfloat16)
        wave = jnp.dot(table[...], both, preferred_element_type=jnp.float32)
        width = wave.shape[1] // 2
        for i in range(2):
            part = wave[:, i * width : (i + 1) * width]
            for half in range(2):
                at = pl.ds(half * inner_len + n + i, padded_rows, stride=two)
                waves[at, :] = part[half * padded_rows : (half + 1) * padded_rows]


def unroll_of(rows):
    return 11 if rows % 11 == 0 else 1


def spectrum_kernel(where_ref, ahead, middle, *refs, lows):
    filters, freq_ref, lags, waves = refs[:4], refs[4], refs[5], refs[6]
    place = where_ref[0]
    length, width = lags.shape
    block = length // 8
    rows, two = middle.shape[:2]
    for i in range(4):
        at = slice(lows[i], lows[i] + block)
        for pair in range(2):
            start = pl.multiple_of(jnp.bitwise_xor(place, 2 * i + pair) * block, block)
            piece = filters[i][at, pair * width : (pair + 1) * width]
            lags[pl.ds(start, block), :] = piece.astype(jnp.float32)
    ahead_into(lags, ahead, waves)

    def one(k, _):
        at = pl.ds(pl.multiple_of(k * two, two), two)
        wave = waves[at, :].astype(jnp.bfloat16)
        freq_ref[at, :] = jnp.dot(middle[k], wave, preferred_element_type=jnp.float32)
        return 0

    lax.fori_loop(0, rows, one, 0, unroll=unroll_of(rows))


def spectrum(where, tables, filters, lows, length):
    ahead, middle = tables[:2]
    rows, two = middle.shape[:2]
    width = filters[0].shape[1] // 2
    vmem = pl.BlockSpec(memory_space=pltpu.VMEM)
    return pl.pallas_call(
        functools.partial(spectrum_kernel, lows=lows),
        out_shape=jax.ShapeDtypeStruct((rows * two, width), jnp.float32),
        in_specs=[pl.BlockSpec(memory_space=pltpu.SMEM)] + [vmem] * 6,
        out_specs=vmem,
        scratch_shapes=[
            pltpu.VMEM((length, width), jnp.float32),
            pltpu.VMEM((ahead.shape[0] // 2 * two, width), jnp.float32),
        ],
        compiler_params=pltpu.CompilerParams(vmem_limit_bytes=8 * 2**20),
        cost_estimate=pl.CostEstimate(
            flops=2 * 2 * length * inner_len * width, bytes_accessed=2**20, transcendentals=0
        ),
        name="spectrum",
    )(where, ahead, middle, *filters)


def mix_kernel(
    where_ref,
    own1,
    recv1,
    own2,
    recv2,
    taps_ref,
    skip_ref,
    ahead,
    middle,
    middle_back,
    back,
    freq_ref,
    weight,
    *refs,
    after,
):
    mixed_ref, held_ref, padded, gated, waves, sums, sem = refs[after:]
    loading = pltpu.make_async_copy(weight, held_ref, sem)
    loading.start()
    place = where_ref[0]
    width = own1.shape[1]
    ours = pl.ds(pl.multiple_of(place * width, width), width)
    taps, skip = taps_ref[:, :, ours], skip_ref[:, ours]
    rows, two = middle.shape[0], middle.shape[1]
    padded_rows = ahead.shape[0] // 2
    used = ahead.shape[1]

    def first(at, value):
        gated[at, :] = value

    def second(at, value):
        gated[at, :] = gated[at, :] * value

    smooth_into(padded, own1, recv1, taps, 1, first)
    smooth_into(padded, own2, recv2, taps, 2, second)
    ahead_into(gated, ahead, waves)
    if padded_rows > rows:
        sums[rows * two :, :] = jnp.zeros(((padded_rows - rows) * two, width), jnp.float32)

    def one(k, _):
        at = pl.ds(pl.multiple_of(k * two, two), two)
        wave = waves[at, :].astype(jnp.bfloat16)
        data = jnp.dot(middle[k], wave, preferred_element_type=jnp.float32)
        filters = freq_ref[at, :]
        data_real, filter_real = data[:inner_len], filters[:inner_len]
        data_imag, filter_imag = data[inner_len:], filters[inner_len:]
        product = jnp.concatenate(
            [
                data_real * filter_real - data_imag * filter_imag,
                data_real * filter_imag + data_imag * filter_real,
            ],
            0,
        ).astype(jnp.bfloat16)
        sums[at, :] = jnp.dot(middle_back[k], product, preferred_element_type=jnp.float32)
        return 0

    lax.fori_loop(0, rows, one, 0, unroll=unroll_of(rows))
    for n in range(0, inner_len, 2):
        pieces = [
            jnp.concatenate(
                [
                    sums[pl.ds(n + i, padded_rows, stride=two), :],
                    sums[pl.ds(inner_len + n + i, padded_rows, stride=two), :],
                ],
                0,
            )
            for i in range(2)
        ]
        wave = jnp.dot(
            back[...],
            jnp.concatenate(pieces, 1).astype(jnp.bfloat16),
            preferred_element_type=jnp.float32,
        )
        for i in range(2):
            at = pl.ds(n + i, used, stride=inner_len)
            mixed_ref[at, :] = wave[:, i * width : (i + 1) * width] + skip * gated[at, :]
    loading.wait()


def mix(where, own1, recv1, own2, recv2, taps, skip, tables, freq, weight, after):
    length, width = own1.shape
    two = tables[1].shape[1]
    padded_rows = tables[0].shape[0] // 2
    vmem = pl.BlockSpec(memory_space=pltpu.VMEM)
    return pl.pallas_call(
        functools.partial(mix_kernel, after=len(after)),
        out_shape=(
            jax.ShapeDtypeStruct((length, width), jnp.float32),
            jax.ShapeDtypeStruct(weight.shape, weight.dtype),
        ),
        in_specs=[pl.BlockSpec(memory_space=pltpu.SMEM)]
        + [vmem] * 11
        + [pl.BlockSpec(memory_space=pl.ANY)] * (1 + len(after)),
        out_specs=(vmem, vmem),
        scratch_shapes=[
            pltpu.VMEM((length + 8, width), jnp.float32),
            pltpu.VMEM((length, width), jnp.float32),
            pltpu.VMEM((padded_rows * two, width), jnp.float32),
            pltpu.VMEM((padded_rows * two, width), jnp.float32),
            pltpu.SemaphoreType.DMA,
        ],
        compiler_params=pltpu.CompilerParams(vmem_limit_bytes=16 * 2**20),
        cost_estimate=pl.CostEstimate(
            flops=2 * 6 * length * inner_len * width, bytes_accessed=6 * 2**20, transcendentals=0
        ),
        name="mix",
    )(where, own1, recv1, own2, recv2, taps, skip, *tables, freq, weight, *after)


def gate_kernel(where_ref, own0, recv0, mixed_ref, taps_ref, *refs):
    outs, padded, product = refs[:8], refs[8], refs[9]
    place = where_ref[0]
    block, width = own0.shape[0] // 8, own0.shape[1]
    taps = taps_ref[:, :, pl.ds(pl.multiple_of(place * width, width), width)]

    def store(at, value):
        product[at, :] = (mixed_ref[at, :] * value).astype(jnp.bfloat16)

    smooth_into(padded, own0, recv0, taps, 0, store)
    for i in range(8):
        start = pl.multiple_of(jnp.bitwise_xor(place, i) * block, block)
        outs[i][...] = product[pl.ds(start, block), :]


def gate(where, own0, recv0, mixed, taps):
    length, width = own0.shape
    vmem = pl.BlockSpec(memory_space=pltpu.VMEM)
    return pl.pallas_call(
        gate_kernel,
        out_shape=(jax.ShapeDtypeStruct((length // 8, width), jnp.bfloat16),) * 8,
        in_specs=[pl.BlockSpec(memory_space=pltpu.SMEM)] + [vmem] * 4,
        out_specs=(vmem,) * 8,
        scratch_shapes=[
            pltpu.VMEM((length + 8, width), jnp.float32),
            pltpu.VMEM((length, width), jnp.bfloat16),
        ],
        compiler_params=pltpu.CompilerParams(vmem_limit_bytes=8 * 2**20),
        cost_estimate=pl.CostEstimate(
            flops=8 * length * width, bytes_accessed=12 * length * width, transcendentals=0
        ),
        name="gate",
    )(where, own0, recv0, mixed, taps)


def emit_kernel(where_ref, weight, *refs, turns, added):
    parts, extra = refs[:8], refs[8 : 8 + added]
    outs, joined = refs[8 + added : -1], refs[-1]
    place, chan = where_ref[0], where_ref[1]
    width = parts[0].shape[1]
    columns = outs[0].shape[1]
    tile = 256
    for i in range(8):
        start = pl.multiple_of(jnp.bitwise_xor(place, i) * width, width)
        joined[:, pl.ds(start, width)] = parts[i][...]
    for i, turn in enumerate(turns):
        for low in range(0, columns, tile):
            start = pl.multiple_of(jnp.bitwise_xor(chan, turn) * columns + low, tile)
            total = jnp.dot(
                joined[...], weight[:, pl.ds(start, tile)], preferred_element_type=jnp.float32
            )
            if added:
                total = total + extra[i][:, low : low + tile].astype(jnp.float32)
            outs[i][:, low : low + tile] = total.astype(outs[i].dtype)


def emit(where, parts, weight, turns, extra, out_dtype):
    rows, width = parts[0].shape
    columns = weight.shape[1] // 4
    vmem = pl.BlockSpec(memory_space=pltpu.VMEM)
    shape = jax.ShapeDtypeStruct((rows, columns), out_dtype)
    return pl.pallas_call(
        functools.partial(emit_kernel, turns=turns, added=len(extra)),
        out_shape=(shape,) * len(turns),
        in_specs=[pl.BlockSpec(memory_space=pltpu.SMEM)] + [vmem] * (9 + len(extra)),
        out_specs=(vmem,) * len(turns),
        scratch_shapes=[pltpu.VMEM((rows, 8 * width), jnp.bfloat16)],
        compiler_params=pltpu.CompilerParams(vmem_limit_bytes=8 * 2**20),
        cost_estimate=pl.CostEstimate(
            flops=2 * rows * weight.shape[0] * columns * len(turns),
            bytes_accessed=2 * weight.shape[0] * columns * len(turns),
            transcendentals=0,
        ),
        name="emit",
    )(where, weight, *parts, *extra)


def swap(value, axis, count, turn):
    return lax.ppermute(value, axis, [(i, i ^ turn) for i in range(count)])


def fast_body(tokens, in_weight, short_taps, skip_gain, long_filter, out_weight):
    seq, chans = lax.axis_size("seq"), lax.axis_size("chan")
    place, chan = lax.axis_index("seq"), lax.axis_index("chan")
    rows, width = tokens.shape
    length = rows * seq
    part = width // seq
    where = jnp.stack([place, chan]).astype(jnp.int32)

    weight = jnp.transpose(in_weight, (1, 0, 2))

    lags = tokens.shape[0]
    rows = in_weight.shape[0]

    theirs, ours, filter_theirs, cut1_1, cut1_2 = halve(
        where, tokens, long_filter, weight, (1, 2), 1
    )
    far_ours = swap(ours, "seq", seq, 4)
    beside = swap(theirs, "seq", seq, 1)
    w1_1 = swap(cut1_1, "seq", seq, 2)
    filter_beside = swap(filter_theirs, "seq", seq, 1)
    (pair,) = join([ours, beside], [[(0, 0, lags), (1, 0, lags)]], [far_ours, w1_1])
    far_beside = swap(beside, "seq", seq, 4)
    near = swap(pair, "seq", seq, 2)
    pair_across = swap(pair, "chan", chans, 2)
    w1_2 = swap(cut1_2, "seq", seq, 4)
    plan = [(0, (1, 2, "f", 0)), (3, (1, 2, "f")), (2, (2, "f")), (1, (2, "f"))]
    inputs = (where, weight, long_filter, filter_beside)
    w_0, cut12_3, cut2_2, cut2_1 = cut(*inputs, plan, [pair])
    whole = [(0, 0, lags), (1, 0, lags)]
    far, far_and_near = join(
        [far_ours, far_beside, near],
        [whole, whole + [(2, 0, 2 * lags)]],
        [pair_across, w1_2, cut12_3],
    )
    w12_3 = swap(cut12_3, "seq", seq, 6)
    w2_1 = swap(cut2_1, "seq", seq, 2)
    w2_2 = swap(cut2_2, "seq", seq, 4)
    far_near = swap(far, "seq", seq, 2)
    across = swap(far_and_near, "chan", chans, 2)
    every = [(0, 0, 2 * lags), (1, 0, 2 * lags)]
    (first,) = join(
        [pair, pair_across, near, across],
        [every + [(2, 0, 2 * lags), (3, 2 * lags, 2 * lags)]],
        [],
    )
    core_a = swap(first, "chan", chans, 1)
    far_near_across = swap(far_near, "chan", chans, 2)
    (second,) = join(
        [far, across, far_near, far_near_across],
        [every + [(2, 0, 2 * lags), (3, 0, 2 * lags)]],
        [w12_3, w2_1, w2_2],
    )
    core_b = swap(second, "chan", chans, 1)
    line, across = [pair, near, far, far_near], [pair_across, across, far_near_across]
    cores = [core_a, core_b]
    shared = (where, line, across, cores)
    parts1 = [w_0, w1_1, w1_2, w12_3]
    own1, send1 = project(*shared, parts1, (0, 0, 0, 0), length, [])
    recv1 = swap(send1, "seq", seq, 1)
    cut0_2, cut0_3, cut0_1 = cut(*inputs, [(2, (0,)), (3, (0,)), (1, (0,))], [w2_2])
    w0_2, w0_3 = swap(cut0_2, "seq", seq, 4), swap(cut0_3, "seq", seq, 6)
    w0_1 = swap(cut0_1, "seq", seq, 2)
    parts2 = [w_0, w2_1, w2_2, w12_3]
    tables = wave_tables(length)
    freq = spectrum(where, tables, parts2, (2 * rows, rows, rows, 2 * rows), length)
    own2, send2 = project(*shared, parts2, (rows, 0, 0, rows), length, [freq])
    recv2 = swap(send2, "seq", seq, 1)
    lows = (2 * rows + lags, 0, 0, 0)
    own0, send0 = project(*shared, [w_0, w0_1, w0_2, w0_3], lows, length, [])
    recv0 = swap(send0, "seq", seq, 1)
    mixed, held = mix(
        where,
        own1,
        recv1,
        own2,
        recv2,
        short_taps,
        skip_gain[None],
        tables,
        freq,
        out_weight,
        [send0],
    )
    pieces = gate(where, own0, recv0, mixed, short_taps)
    joined = [
        piece if turn == 0 else swap(piece, "seq", seq, turn) for turn, piece in enumerate(pieces)
    ]

    (across_out,) = emit(where, joined, held, (3,), [], jnp.bfloat16)
    from_core = swap(across_out, "chan", chans, 1)
    (beside_out,) = emit(where, joined, held, (1,), [], jnp.bfloat16)
    near_sum = swap(beside_out, "chan", chans, 1)
    (chip_out,) = emit(where, joined, held, (2,), [from_core], jnp.bfloat16)
    from_chip = swap(chip_out, "chan", chans, 2)
    (own,) = emit(where, joined, held, (0,), [near_sum], jnp.float32)
    return (own + from_chip.astype(jnp.float32)).astype(jnp.bfloat16)


def solution(mesh):
    in_specs = (
        P("seq", "chan"),
        P("seq", None, "chan"),
        P(None, None, "chan"),
        P("chan"),
        P("seq", "chan"),
        P("chan", None),
    )
    out_specs = P("seq", "chan")
    seq, chans = mesh.shape["seq"], mesh.shape["chan"]
    chosen = fast_body if seq == 8 and chans == 4 else body
    return jax.shard_map(chosen, mesh=mesh, in_specs=in_specs, out_specs=out_specs, check_vma=False)
```

```python
import functools
import math

import jax
import jax.numpy as jnp
import numpy as np
from jax import lax
from jax.experimental import pallas as pl
from jax.experimental.pallas import tpu as pltpu
from jax.sharding import PartitionSpec as P

exact_prec = lax.Precision.HIGHEST
inner_len = 64


def dft_tables(half_len, blocks):
    full_len = 2 * half_len
    full_size = full_len * blocks
    half_index = jnp.arange(half_len, dtype=jnp.int32)
    full_index = jnp.arange(full_len, dtype=jnp.int32)
    block_index = jnp.arange(blocks, dtype=jnp.int32)
    outer_angle = (half_index[:, None] * full_index[None, :] % full_len).astype(jnp.float32) * (
        2.0 * math.pi / full_len
    )
    inner_angle = (block_index[:, None] * block_index[None, :] % blocks).astype(jnp.float32) * (
        2.0 * math.pi / blocks
    )
    twist_angle = (full_index[:, None] * block_index[None, :] % full_size).astype(jnp.float32) * (
        2.0 * math.pi / full_size
    )
    return (
        jnp.cos(outer_angle),
        jnp.sin(outer_angle),
        jnp.cos(inner_angle),
        jnp.sin(inner_angle),
        jnp.cos(twist_angle),
        jnp.sin(twist_angle),
    )


def forward_dft(signal, tables):
    outer_cos, outer_sin, inner_cos, inner_sin, twist_cos, twist_sin = tables
    real_section = jnp.einsum("cmn,mk->ckn", signal, outer_cos, precision=exact_prec)
    imag_section = -jnp.einsum("cmn,mk->ckn", signal, outer_sin, precision=exact_prec)
    real_twist = real_section * twist_cos + imag_section * twist_sin
    imag_twist = imag_section * twist_cos - real_section * twist_sin
    real_freq = jnp.einsum("ckn,nj->ckj", real_twist, inner_cos, precision=exact_prec) + jnp.einsum(
        "ckn,nj->ckj", imag_twist, inner_sin, precision=exact_prec
    )
    imag_freq = jnp.einsum("ckn,nj->ckj", imag_twist, inner_cos, precision=exact_prec) - jnp.einsum(
        "ckn,nj->ckj", real_twist, inner_sin, precision=exact_prec
    )
    return (real_freq, imag_freq)


def inverse_real(spectrum_real, spectrum_imag, tables):
    outer_cos, outer_sin, inner_cos, inner_sin, twist_cos, twist_sin = tables
    full_size = outer_cos.shape[1] * inner_cos.shape[0]
    back_real = jnp.einsum(
        "ckj,jn->ckn", spectrum_real, inner_cos, precision=exact_prec
    ) - jnp.einsum("ckj,jn->ckn", spectrum_imag, inner_sin, precision=exact_prec)
    back_imag = jnp.einsum(
        "ckj,jn->ckn", spectrum_imag, inner_cos, precision=exact_prec
    ) + jnp.einsum("ckj,jn->ckn", spectrum_real, inner_sin, precision=exact_prec)
    turn_real = back_real * twist_cos - back_imag * twist_sin
    turn_imag = back_imag * twist_cos + back_real * twist_sin
    summed_real = jnp.einsum(
        "ckn,mk->cmn", turn_real, outer_cos, precision=exact_prec
    ) - jnp.einsum("ckn,mk->cmn", turn_imag, outer_sin, precision=exact_prec)
    return summed_real / full_size


def causal_conv(signal, kernel, blocks):
    channels, length = signal.shape
    half_len = length // blocks
    tables = dft_tables(half_len, blocks)
    stacked = jnp.concatenate([signal, kernel], 0).reshape(2 * channels, half_len, blocks)
    real_freq, imag_freq = forward_dft(stacked, tables)
    data_real, filter_real = (real_freq[:channels], real_freq[channels:])
    data_imag, filter_imag = (imag_freq[:channels], imag_freq[channels:])
    spectrum_real = data_real * filter_real - data_imag * filter_imag
    spectrum_imag = data_real * filter_imag + data_imag * filter_real
    return inverse_real(spectrum_real, spectrum_imag, tables).reshape(channels, length)


def body(tokens, in_weight, short_taps, skip_gain, long_filter, out_weight):
    row_count, chan_width = tokens.shape
    blocks = lax.axis_size("seq")
    part_width = chan_width // blocks
    flat_weight = in_weight.reshape(in_weight.shape[0], 3 * chan_width)
    whole = lax.all_gather(tokens, "chan", axis=1, tiled=True)
    projected = jnp.dot(
        whole,
        lax.all_gather(flat_weight, "seq", axis=0, tiled=True),
        preferred_element_type=jnp.float32,
    )
    projected = projected.astype(jnp.bfloat16).reshape(row_count, 3, chan_width)
    outgoing = jnp.transpose(projected, (1, 2, 0))
    filter_rows = jnp.transpose(long_filter)[None]
    channel_major, filter_major = (
        lax.all_to_all(outgoing, "seq", split_axis=1, concat_axis=2, tiled=True),
        lax.all_to_all(filter_rows, "seq", split_axis=1, concat_axis=2, tiled=True),
    )
    offset = lax.axis_index("seq") * part_width
    local_taps = lax.dynamic_slice_in_dim(short_taps, offset, part_width, 2)
    local_skip = lax.dynamic_slice_in_dim(skip_gain, offset, part_width, 0)
    values = channel_major.astype(jnp.float32)
    tap_count = short_taps.shape[1]
    length = values.shape[2]
    padded = jnp.pad(values, ((0, 0), (0, 0), (tap_count - 1, 0)))
    smoothed = jnp.zeros_like(values)
    for tap_index in range(tap_count):
        lag_start = tap_count - 1 - tap_index
        smoothed = (
            smoothed
            + local_taps[:, tap_index, :, None] * padded[:, :, lag_start : lag_start + length]
        )
    gate_query = smoothed[0]
    gated = smoothed[1] * smoothed[2]
    mixed_seq = (
        causal_conv(gated, filter_major[0].astype(jnp.float32), blocks)
        + local_skip[:, None] * gated
    )
    product = (mixed_seq * gate_query).astype(jnp.bfloat16)
    returned = lax.all_to_all(product, "seq", split_axis=1, concat_axis=0, tiled=True)
    summed = lax.psum_scatter(
        lax.dot_general(
            out_weight, returned, (((0,), (0,)), ((), ())), preferred_element_type=jnp.float32
        ).astype(jnp.bfloat16),
        "chan",
        scatter_dimension=0,
        tiled=True,
    ).astype(jnp.float32)
    return jnp.transpose(summed).astype(jnp.bfloat16)


def wave_tables(length):
    span = 2 * length
    outer = span // inner_len
    used, rows = outer // 2, outer // 2 + 1
    padded_rows = -(-rows // 8) * 8
    m, k = np.arange(used), np.arange(rows)
    n, j = np.arange(inner_len), np.arange(inner_len)
    angle = (2.0 * math.pi / outer) * (np.outer(k, m) % outer)
    ahead = np.zeros((2, padded_rows, used))
    ahead[0, :rows], ahead[1, :rows] = np.cos(angle), -np.sin(angle)
    weight = np.where((k == 0) | (k == used), 1.0, 2.0) / span
    back = np.zeros((used, 2, padded_rows))
    back[:, 0, :rows] = (np.cos(angle) * weight[:, None]).T
    back[:, 1, :rows] = (-np.sin(angle) * weight[:, None]).T
    turn = n[None, None, :] * (k[:, None, None] + outer * j[None, :, None]) % span
    cos, sin = np.cos(turn * (2.0 * math.pi / span)), np.sin(turn * (2.0 * math.pi / span))
    middle = np.concatenate(
        [np.concatenate([cos, sin], 2), np.concatenate([-sin, cos], 2)], 1
    )
    return tuple(
        jnp.asarray(table, jnp.bfloat16)
        for table in (
            ahead.reshape(2 * padded_rows, used),
            middle,
            np.swapaxes(middle, 1, 2),
            back.reshape(used, 2 * padded_rows),
        )
    )


def halve_kernel(where_ref, tokens, filters, weight, ours, theirs, *refs, turns, names):
    pieces, sems = refs[:-1], refs[-1]
    depth, side = where_ref[0] // 2, where_ref[0] % 2
    rows, half = ours.shape
    part = half // 4
    copies = []

    def copy(source, block, width, target):
        columns = pl.ds(pl.multiple_of(block * width, width), width)
        copies.append(
            pltpu.make_async_copy(source.at[:, columns], target, sems.at[len(copies)])
        )

    copy(tokens, side, half, ours)
    copy(tokens, 1 - side, half, theirs.at[pl.ds(0, rows), :])
    for i in range(4):
        target = theirs.at[pl.ds(rows, filters.shape[0]), pl.ds(i * part, part)]
        copy(filters, 2 * i + 1 - side, part, target)
    depth_rows = weight.shape[1]
    for turn, piece in zip(turns, pieces, strict=True):
        for i, name in enumerate(names):
            target = piece.at[pl.ds(i * depth_rows, depth_rows), :]
            copy(weight.at[name], jnp.bitwise_xor(depth, turn), piece.shape[1], target)
    for one in copies:
        one.start()
    for one in copies:
        one.wait()


def halve(where, tokens, filters, weight, turns, names):
    rows, half = tokens.shape[0], tokens.shape[1] // 2
    piece = jax.ShapeDtypeStruct(
        (len(names) * weight.shape[1], weight.shape[2] // 4), weight.dtype
    )
    vmem = pl.BlockSpec(memory_space=pltpu.VMEM)
    return pl.pallas_call(
        functools.partial(halve_kernel, turns=turns, names=names),
        out_shape=(
            jax.ShapeDtypeStruct((rows, half), tokens.dtype),
            jax.ShapeDtypeStruct((rows + filters.shape[0], half), tokens.dtype),
        )
        + (piece,) * len(turns),
        in_specs=[pl.BlockSpec(memory_space=pltpu.SMEM)]
        + [pl.BlockSpec(memory_space=pl.ANY)] * 3,
        out_specs=(vmem,) * (2 + len(turns)),
        scratch_shapes=[pltpu.SemaphoreType.DMA((6 + len(turns) * len(names),))],
        compiler_params=pltpu.CompilerParams(vmem_limit_bytes=61 * 2**20),
        name="halve",
    )(where, tokens, filters, weight)


def cut_kernel(where_ref, weight, filters, filter_beside, *refs, plan, after):
    place = where_ref[0]
    depth, side = place // 2, place % 2
    outs, sems = refs[after:-1], refs[-1]
    copies = []

    def copy(source, target):
        copies.append(pltpu.make_async_copy(source, target, sems.at[len(copies)]))

    def columns_of(block, width):
        return pl.ds(pl.multiple_of(block * width, width), width)

    rows, width = weight.shape[1], outs[0].shape[1]
    half = width // 2
    for out, (turn, names) in zip(outs, plan, strict=True):
        block = jnp.bitwise_xor(depth, turn)
        low = 0
        for name in names:
            if name == "f":
                at = pl.ds(low, filters.shape[0])
                here = columns_of(2 * block + side, half)
                copy(filters.at[:, here], out.at[at, pl.ds(0, half)])
                there = columns_of(block, half)
                below = pl.ds(filter_beside.shape[0] - filters.shape[0], filters.shape[0])
                copy(filter_beside.at[below, there], out.at[at, pl.ds(half, half)])
                low += filters.shape[0]
            else:
                source = weight.at[name, :, columns_of(block, width)]
                copy(source, out.at[pl.ds(low, rows), :])
                low += rows
    for one in copies:
        one.start()
    for one in copies:
        one.wait()


def cut(where, weight, filters, filter_beside, plan, after):
    count_of = {"f": filters.shape[0]}
    shapes = []
    for _, names in plan:
        rows = sum(count_of.get(name, weight.shape[1]) for name in names)
        shapes.append(jax.ShapeDtypeStruct((rows, weight.shape[2] // 4), weight.dtype))
    return pl.pallas_call(
        functools.partial(cut_kernel, plan=plan, after=len(after)),
        out_shape=tuple(shapes),
        in_specs=[pl.BlockSpec(memory_space=pltpu.SMEM)]
        + [pl.BlockSpec(memory_space=pl.ANY)] * (3 + len(after)),
        out_specs=(pl.BlockSpec(memory_space=pltpu.VMEM),) * len(shapes),
        scratch_shapes=[pltpu.SemaphoreType.DMA((24,))],
        compiler_params=pltpu.CompilerParams(vmem_limit_bytes=8 * 2**20),
        name="cut",
    )(where, weight, filters, filter_beside, *after)


def join_kernel(*refs, pieces, outs):
    for out_ref, group in zip(refs[len(refs) - outs :], pieces, strict=True):
        start = 0
        for at, low, count in group:
            out_ref[start : start + count, :] = refs[at][low : low + count, :]
            start += count


def join(values, pieces, after):
    shapes = []
    for group in pieces:
        rows = sum(count for _, _, count in group)
        shapes.append(jax.ShapeDtypeStruct((rows, values[0].shape[1]), values[0].dtype))
    vmem = pl.BlockSpec(memory_space=pltpu.VMEM)
    return pl.pallas_call(
        functools.partial(join_kernel, pieces=pieces, outs=len(pieces)),
        out_shape=tuple(shapes),
        in_specs=[vmem] * len(values) + [pl.BlockSpec(memory_space=pl.ANY)] * len(after),
        out_specs=(vmem,) * len(shapes),
        compiler_params=pltpu.CompilerParams(vmem_limit_bytes=8 * 2**20),
        name="join",
    )(*values, *after)


def project_kernel(where_ref, *refs, lows, after):
    line, across, cores, parts = refs[:4], refs[4:7], refs[7:9], refs[9:13]
    own_ref, send_ref, weights = refs[13 + after :]
    place, chan = where_ref[0], where_ref[1]
    depth, side = place // 2, place % 2
    rows = line[0].shape[1]
    for i in range(4):
        slot = jnp.bitwise_xor(depth, jnp.bitwise_xor(chan, i))
        start = pl.multiple_of(slot * rows, rows)
        weights[pl.ds(start, rows), :] = parts[i][lows[i] : lows[i] + rows, :]
    length, half = own_ref.shape
    block = length // 8
    for step in range(4):
        low = 4 * block * (step % 2)
        both = cores[step // 2]
        beside = across[(0, 1, 1, 2)[step]]
        at = 2 * block if step == 1 else 0
        joined = jnp.concatenate(
            [
                line[step][...],
                both[low : low + 2 * block, :],
                beside[at : at + 2 * block, :],
                both[low + 2 * block : low + 4 * block, :],
            ],
            1,
        )
        total = jnp.dot(joined, weights[...], preferred_element_type=jnp.float32)
        left, right = total[:, :half], total[:, half:]
        own = jnp.where(side == 0, left, right)
        send = jnp.where(side == 0, right, left).astype(jnp.bfloat16)
        for pair in range(2):
            start = pl.multiple_of(jnp.bitwise_xor(place, 2 * step + pair) * block, block)
            own_ref[pl.ds(start, block), :] = own[pair * block : (pair + 1) * block]
            send_ref[pl.ds(start, block), :] = send[pair * block : (pair + 1) * block]


def project(where, line, across, cores, parts, lows, length, after):
    depth, width = line[0].shape[1], parts[0].shape[1]
    vmem = pl.BlockSpec(memory_space=pltpu.VMEM)
    return pl.pallas_call(
        functools.partial(project_kernel, lows=lows, after=len(after)),
        out_shape=(
            jax.ShapeDtypeStruct((length, width // 2), jnp.float32),
            jax.ShapeDtypeStruct((length, width // 2), jnp.bfloat16),
        ),
        in_specs=[pl.BlockSpec(memory_space=pltpu.SMEM)]
        + [vmem] * 13
        + [pl.BlockSpec(memory_space=pl.ANY)] * len(after),
        out_specs=(vmem, vmem),
        scratch_shapes=[pltpu.VMEM((4 * depth, width), jnp.bfloat16)],
        compiler_params=pltpu.CompilerParams(vmem_limit_bytes=12 * 2**20),
        cost_estimate=pl.CostEstimate(
            flops=2 * length * 4 * depth * 2 * width,
            bytes_accessed=2 * length * 4 * depth,
            transcendentals=0,
        ),
        name="project",
    )(where, *line, *across, *cores, *parts, *after)


def smooth_into(padded, own_ref, recv_ref, taps, branch, store):
    length = own_ref.shape[0]
    tap_count = taps.shape[1]
    block = length // 8
    padded[0:8, :] = jnp.zeros((8, padded.shape[1]), jnp.float32)
    for i in range(8):
        rows = slice(i * block, (i + 1) * block)
        padded[8 + i * block : 8 + (i + 1) * block, :] = own_ref[rows, :] + recv_ref[
            rows, :
        ].astype(jnp.float32)
    for i in range(8):
        total = None
        for tap in range(tap_count):
            start = 8 + i * block - tap
            term = taps[branch, tap : tap + 1, :] * padded[start : start + block, :]
            total = term if total is None else total + term
        store(slice(i * block, (i + 1) * block), total)


def ahead_into(signal, table, waves):
    padded_rows, used = table.shape[0] // 2, table.shape[1]
    two = 2 * inner_len
    for n in range(0, inner_len, 2):
        both = jnp.concatenate(
            [signal[pl.ds(n + i, used, stride=inner_len), :] for i in range(2)], 1
        ).astype(jnp.bfloat16)
        wave = jnp.dot(table[...], both, preferred_element_type=jnp.float32)
        width = wave.shape[1] // 2
        for i in range(2):
            part = wave[:, i * width : (i + 1) * width]
            for half in range(2):
                at = pl.ds(half * inner_len + n + i, padded_rows, stride=two)
                waves[at, :] = part[half * padded_rows : (half + 1) * padded_rows]


def unroll_of(rows):
    return 11 if rows % 11 == 0 else 1


def spectrum_kernel(where_ref, ahead, middle, *refs, lows):
    filters, freq_ref, lags, waves = refs[:4], refs[4], refs[5], refs[6]
    place = where_ref[0]
    length, width = lags.shape
    block = length // 8
    rows, two = middle.shape[:2]
    for i in range(4):
        at = slice(lows[i], lows[i] + block)
        for pair in range(2):
            start = pl.multiple_of(jnp.bitwise_xor(place, 2 * i + pair) * block, block)
            piece = filters[i][at, pair * width : (pair + 1) * width]
            lags[pl.ds(start, block), :] = piece.astype(jnp.float32)
    ahead_into(lags, ahead, waves)

    def one(k, _):
        at = pl.ds(pl.multiple_of(k * two, two), two)
        wave = waves[at, :].astype(jnp.bfloat16)
        freq_ref[at, :] = jnp.dot(middle[k], wave, preferred_element_type=jnp.float32)
        return 0

    lax.fori_loop(0, rows, one, 0, unroll=unroll_of(rows))


def spectrum(where, tables, filters, lows, length):
    ahead, middle = tables[:2]
    rows, two = middle.shape[:2]
    width = filters[0].shape[1] // 2
    vmem = pl.BlockSpec(memory_space=pltpu.VMEM)
    return pl.pallas_call(
        functools.partial(spectrum_kernel, lows=lows),
        out_shape=jax.ShapeDtypeStruct((rows * two, width), jnp.float32),
        in_specs=[pl.BlockSpec(memory_space=pltpu.SMEM)] + [vmem] * 6,
        out_specs=vmem,
        scratch_shapes=[
            pltpu.VMEM((length, width), jnp.float32),
            pltpu.VMEM((ahead.shape[0] // 2 * two, width), jnp.float32),
        ],
        compiler_params=pltpu.CompilerParams(vmem_limit_bytes=8 * 2**20),
        cost_estimate=pl.CostEstimate(
            flops=2 * 2 * length * inner_len * width, bytes_accessed=2**20, transcendentals=0
        ),
        name="spectrum",
    )(where, ahead, middle, *filters)


def mix_kernel(
    where_ref,
    own1,
    recv1,
    own2,
    recv2,
    taps_ref,
    skip_ref,
    ahead,
    middle,
    middle_back,
    back,
    freq_ref,
    weight,
    *refs,
    after,
):
    mixed_ref, held_ref, padded, gated, waves, sums, sem = refs[after:]
    loading = pltpu.make_async_copy(weight, held_ref, sem)
    loading.start()
    place = where_ref[0]
    width = own1.shape[1]
    ours = pl.ds(pl.multiple_of(place * width, width), width)
    taps, skip = taps_ref[:, :, ours], skip_ref[:, ours]
    rows, two = middle.shape[0], middle.shape[1]
    padded_rows = ahead.shape[0] // 2
    used = ahead.shape[1]

    def first(at, value):
        gated[at, :] = value

    def second(at, value):
        gated[at, :] = gated[at, :] * value

    smooth_into(padded, own1, recv1, taps, 1, first)
    smooth_into(padded, own2, recv2, taps, 2, second)
    ahead_into(gated, ahead, waves)
    if padded_rows > rows:
        sums[rows * two :, :] = jnp.zeros(((padded_rows - rows) * two, width), jnp.float32)

    def one(k, _):
        at = pl.ds(pl.multiple_of(k * two, two), two)
        wave = waves[at, :].astype(jnp.bfloat16)
        data = jnp.dot(middle[k], wave, preferred_element_type=jnp.float32)
        filters = freq_ref[at, :]
        data_real, filter_real = data[:inner_len], filters[:inner_len]
        data_imag, filter_imag = data[inner_len:], filters[inner_len:]
        product = jnp.concatenate(
            [
                data_real * filter_real - data_imag * filter_imag,
                data_real * filter_imag + data_imag * filter_real,
            ],
            0,
        ).astype(jnp.bfloat16)
        sums[at, :] = jnp.dot(middle_back[k], product, preferred_element_type=jnp.float32)
        return 0

    lax.fori_loop(0, rows, one, 0, unroll=unroll_of(rows))
    for n in range(0, inner_len, 2):
        pieces = [
            jnp.concatenate(
                [
                    sums[pl.ds(n + i, padded_rows, stride=two), :],
                    sums[pl.ds(inner_len + n + i, padded_rows, stride=two), :],
                ],
                0,
            )
            for i in range(2)
        ]
        wave = jnp.dot(
            back[...],
            jnp.concatenate(pieces, 1).astype(jnp.bfloat16),
            preferred_element_type=jnp.float32,
        )
        for i in range(2):
            at = pl.ds(n + i, used, stride=inner_len)
            mixed_ref[at, :] = wave[:, i * width : (i + 1) * width] + skip * gated[at, :]
    loading.wait()


def mix(where, own1, recv1, own2, recv2, taps, skip, tables, freq, weight, after):
    length, width = own1.shape
    two = tables[1].shape[1]
    padded_rows = tables[0].shape[0] // 2
    vmem = pl.BlockSpec(memory_space=pltpu.VMEM)
    return pl.pallas_call(
        functools.partial(mix_kernel, after=len(after)),
        out_shape=(
            jax.ShapeDtypeStruct((length, width), jnp.float32),
            jax.ShapeDtypeStruct(weight.shape, weight.dtype),
        ),
        in_specs=[pl.BlockSpec(memory_space=pltpu.SMEM)]
        + [vmem] * 11
        + [pl.BlockSpec(memory_space=pl.ANY)] * (1 + len(after)),
        out_specs=(vmem, vmem),
        scratch_shapes=[
            pltpu.VMEM((length + 8, width), jnp.float32),
            pltpu.VMEM((length, width), jnp.float32),
            pltpu.VMEM((padded_rows * two, width), jnp.float32),
            pltpu.VMEM((padded_rows * two, width), jnp.float32),
            pltpu.SemaphoreType.DMA,
        ],
        compiler_params=pltpu.CompilerParams(vmem_limit_bytes=16 * 2**20),
        cost_estimate=pl.CostEstimate(
            flops=2 * 6 * length * inner_len * width, bytes_accessed=6 * 2**20, transcendentals=0
        ),
        name="mix",
    )(where, own1, recv1, own2, recv2, taps, skip, *tables, freq, weight, *after)


def gate_kernel(where_ref, own0, recv0, mixed_ref, taps_ref, *refs):
    outs, padded, product = refs[:8], refs[8], refs[9]
    place = where_ref[0]
    block, width = own0.shape[0] // 8, own0.shape[1]
    taps = taps_ref[:, :, pl.ds(pl.multiple_of(place * width, width), width)]

    def store(at, value):
        product[at, :] = (mixed_ref[at, :] * value).astype(jnp.bfloat16)

    smooth_into(padded, own0, recv0, taps, 0, store)
    for i in range(8):
        start = pl.multiple_of(jnp.bitwise_xor(place, i) * block, block)
        outs[i][...] = product[pl.ds(start, block), :]


def gate(where, own0, recv0, mixed, taps):
    length, width = own0.shape
    vmem = pl.BlockSpec(memory_space=pltpu.VMEM)
    return pl.pallas_call(
        gate_kernel,
        out_shape=(jax.ShapeDtypeStruct((length // 8, width), jnp.bfloat16),) * 8,
        in_specs=[pl.BlockSpec(memory_space=pltpu.SMEM)] + [vmem] * 4,
        out_specs=(vmem,) * 8,
        scratch_shapes=[
            pltpu.VMEM((length + 8, width), jnp.float32),
            pltpu.VMEM((length, width), jnp.bfloat16),
        ],
        compiler_params=pltpu.CompilerParams(vmem_limit_bytes=8 * 2**20),
        cost_estimate=pl.CostEstimate(
            flops=8 * length * width, bytes_accessed=12 * length * width, transcendentals=0
        ),
        name="gate",
    )(where, own0, recv0, mixed, taps)


def emit_kernel(where_ref, weight, *refs, turns, added):
    parts, extra = refs[:8], refs[8 : 8 + added]
    outs, joined = refs[8 + added : -1], refs[-1]
    place, chan = where_ref[0], where_ref[1]
    width = parts[0].shape[1]
    columns = outs[0].shape[1]
    tile = 256
    for i in range(8):
        start = pl.multiple_of(jnp.bitwise_xor(place, i) * width, width)
        joined[:, pl.ds(start, width)] = parts[i][...]
    for i, turn in enumerate(turns):
        for low in range(0, columns, tile):
            start = pl.multiple_of(jnp.bitwise_xor(chan, turn) * columns + low, tile)
            total = jnp.dot(
                joined[...], weight[:, pl.ds(start, tile)], preferred_element_type=jnp.float32
            )
            if added:
                total = total + extra[i][:, low : low + tile].astype(jnp.float32)
            outs[i][:, low : low + tile] = total.astype(outs[i].dtype)


def emit(where, parts, weight, turns, extra, out_dtype):
    rows, width = parts[0].shape
    columns = weight.shape[1] // 4
    vmem = pl.BlockSpec(memory_space=pltpu.VMEM)
    shape = jax.ShapeDtypeStruct((rows, columns), out_dtype)
    return pl.pallas_call(
        functools.partial(emit_kernel, turns=turns, added=len(extra)),
        out_shape=(shape,) * len(turns),
        in_specs=[pl.BlockSpec(memory_space=pltpu.SMEM)] + [vmem] * (9 + len(extra)),
        out_specs=(vmem,) * len(turns),
        scratch_shapes=[pltpu.VMEM((rows, 8 * width), jnp.bfloat16)],
        compiler_params=pltpu.CompilerParams(vmem_limit_bytes=8 * 2**20),
        cost_estimate=pl.CostEstimate(
            flops=2 * rows * weight.shape[0] * columns * len(turns),
            bytes_accessed=2 * weight.shape[0] * columns * len(turns),
            transcendentals=0,
        ),
        name="emit",
    )(where, weight, *parts, *extra)


def swap(value, axis, count, turn):
    return lax.ppermute(value, axis, [(i, i ^ turn) for i in range(count)])


def fast_body(tokens, in_weight, short_taps, skip_gain, long_filter, out_weight):
    seq, chans = lax.axis_size("seq"), lax.axis_size("chan")
    place, chan = lax.axis_index("seq"), lax.axis_index("chan")
    rows, width = tokens.shape
    length = rows * seq
    part = width // seq
    where = jnp.stack([place, chan]).astype(jnp.int32)

    weight = jnp.transpose(in_weight, (1, 0, 2))

    lags = tokens.shape[0]
    rows = in_weight.shape[0]

    ours, theirs, cut_2, cut_1 = halve(where, tokens, long_filter, weight, (2, 1), (1, 2))
    beside = swap(theirs, "seq", seq, 1)
    w_2, w_1 = swap(cut_2, "seq", seq, 4), swap(cut_1, "seq", seq, 2)
    whole = [(0, 0, lags), (1, 0, lags)]
    (pair,) = join([ours, beside], [whole], [])
    far = swap(pair, "seq", seq, 4)
    near = swap(pair, "seq", seq, 2)
    pair_across = swap(pair, "chan", chans, 2)
    inputs = (where, weight, long_filter, beside)
    plan = [(0, (1, 2, 0, "f")), (3, (1, 2, "f"))]
    plan += [(2, (0, "f")), (3, (0,)), (1, (0, "f"))]
    w_0, cut_3, cut0_2, cut0_3, cut0_1 = cut(*inputs, plan, [pair])
    (far_and_near,) = join(
        [far, near],
        [[(0, 0, 2 * lags), (1, 0, 2 * lags)]],
        [pair_across, cut_3, w_2, w_1],
    )
    w_3 = swap(cut_3, "seq", seq, 6)
    far_near = swap(far, "seq", seq, 2)
    across = swap(far_and_near, "chan", chans, 2)
    every = [(0, 0, 2 * lags), (1, 0, 2 * lags)]
    (first,) = join(
        [pair, pair_across, near, across],
        [every + [(2, 0, 2 * lags), (3, 2 * lags, 2 * lags)]],
        [w_3],
    )
    core_a = swap(first, "chan", chans, 1)
    far_near_across = swap(far_near, "chan", chans, 2)
    (second,) = join(
        [far, across, far_near, far_near_across],
        [every + [(2, 0, 2 * lags), (3, 0, 2 * lags)]],
        [],
    )
    core_b = swap(second, "chan", chans, 1)
    line, across = [pair, near, far, far_near], [pair_across, across, far_near_across]
    cores = [core_a, core_b]
    shared = (where, line, across, cores)
    parts = [w_0, w_1, w_2, w_3]
    own1, send1 = project(*shared, parts, (0,) * 4, length, [])
    recv1 = swap(send1, "seq", seq, 1)
    w0_2, w0_3 = swap(cut0_2, "seq", seq, 4), swap(cut0_3, "seq", seq, 6)
    w0_1 = swap(cut0_1, "seq", seq, 2)
    tables = wave_tables(length)
    parts0 = [w_0, w0_1, w0_2, w0_3]
    freq = spectrum(
        where, tables, [w_0, w0_1, w0_2, w_3], (3 * rows, rows, rows, 2 * rows), length
    )
    own2, send2 = project(*shared, parts, (rows,) * 4, length, [])
    recv2 = swap(send2, "seq", seq, 1)
    own0, send0 = project(*shared, parts0, (2 * rows, 0, 0, 0), length, [])
    recv0 = swap(send0, "seq", seq, 1)
    mixed, held = mix(
        where,
        own1,
        recv1,
        own2,
        recv2,
        short_taps,
        skip_gain[None],
        tables,
        freq,
        out_weight,
        [send0],
    )
    pieces = gate(where, own0, recv0, mixed, short_taps)
    joined = [
        piece if turn == 0 else swap(piece, "seq", seq, turn) for turn, piece in enumerate(pieces)
    ]

    (across_out,) = emit(where, joined, held, (3,), [], jnp.bfloat16)
    from_core = swap(across_out, "chan", chans, 1)
    (beside_out,) = emit(where, joined, held, (1,), [], jnp.bfloat16)
    near_sum = swap(beside_out, "chan", chans, 1)
    (chip_out,) = emit(where, joined, held, (2,), [from_core], jnp.bfloat16)
    from_chip = swap(chip_out, "chan", chans, 2)
    (own,) = emit(where, joined, held, (0,), [near_sum], jnp.float32)
    return (own + from_chip.astype(jnp.float32)).astype(jnp.bfloat16)


def solution(mesh):
    in_specs = (
        P("seq", "chan"),
        P("seq", None, "chan"),
        P(None, None, "chan"),
        P("chan"),
        P("seq", "chan"),
        P("chan", None),
    )
    out_specs = P("seq", "chan")
    seq, chans = mesh.shape["seq"], mesh.shape["chan"]
    chosen = fast_body if seq == 8 and chans == 4 else body
    return jax.shard_map(chosen, mesh=mesh, in_specs=in_specs, out_specs=out_specs, check_vma=False)
```

```python
import functools
import math

import jax
import jax.numpy as jnp
import numpy as np
from jax import lax
from jax.experimental import pallas as pl
from jax.experimental.pallas import tpu as pltpu
from jax.sharding import PartitionSpec as P

exact_prec = lax.Precision.HIGHEST
inner_len = 64


def dft_tables(half_len, blocks):
    full_len = 2 * half_len
    full_size = full_len * blocks
    half_index = jnp.arange(half_len, dtype=jnp.int32)
    full_index = jnp.arange(full_len, dtype=jnp.int32)
    block_index = jnp.arange(blocks, dtype=jnp.int32)
    outer_angle = (half_index[:, None] * full_index[None, :] % full_len).astype(jnp.float32) * (
        2.0 * math.pi / full_len
    )
    inner_angle = (block_index[:, None] * block_index[None, :] % blocks).astype(jnp.float32) * (
        2.0 * math.pi / blocks
    )
    twist_angle = (full_index[:, None] * block_index[None, :] % full_size).astype(jnp.float32) * (
        2.0 * math.pi / full_size
    )
    return (
        jnp.cos(outer_angle),
        jnp.sin(outer_angle),
        jnp.cos(inner_angle),
        jnp.sin(inner_angle),
        jnp.cos(twist_angle),
        jnp.sin(twist_angle),
    )


def forward_dft(signal, tables):
    outer_cos, outer_sin, inner_cos, inner_sin, twist_cos, twist_sin = tables
    real_section = jnp.einsum("cmn,mk->ckn", signal, outer_cos, precision=exact_prec)
    imag_section = -jnp.einsum("cmn,mk->ckn", signal, outer_sin, precision=exact_prec)
    real_twist = real_section * twist_cos + imag_section * twist_sin
    imag_twist = imag_section * twist_cos - real_section * twist_sin
    real_freq = jnp.einsum("ckn,nj->ckj", real_twist, inner_cos, precision=exact_prec) + jnp.einsum(
        "ckn,nj->ckj", imag_twist, inner_sin, precision=exact_prec
    )
    imag_freq = jnp.einsum("ckn,nj->ckj", imag_twist, inner_cos, precision=exact_prec) - jnp.einsum(
        "ckn,nj->ckj", real_twist, inner_sin, precision=exact_prec
    )
    return (real_freq, imag_freq)


def inverse_real(spectrum_real, spectrum_imag, tables):
    outer_cos, outer_sin, inner_cos, inner_sin, twist_cos, twist_sin = tables
    full_size = outer_cos.shape[1] * inner_cos.shape[0]
    back_real = jnp.einsum(
        "ckj,jn->ckn", spectrum_real, inner_cos, precision=exact_prec
    ) - jnp.einsum("ckj,jn->ckn", spectrum_imag, inner_sin, precision=exact_prec)
    back_imag = jnp.einsum(
        "ckj,jn->ckn", spectrum_imag, inner_cos, precision=exact_prec
    ) + jnp.einsum("ckj,jn->ckn", spectrum_real, inner_sin, precision=exact_prec)
    turn_real = back_real * twist_cos - back_imag * twist_sin
    turn_imag = back_imag * twist_cos + back_real * twist_sin
    summed_real = jnp.einsum(
        "ckn,mk->cmn", turn_real, outer_cos, precision=exact_prec
    ) - jnp.einsum("ckn,mk->cmn", turn_imag, outer_sin, precision=exact_prec)
    return summed_real / full_size


def causal_conv(signal, kernel, blocks):
    channels, length = signal.shape
    half_len = length // blocks
    tables = dft_tables(half_len, blocks)
    stacked = jnp.concatenate([signal, kernel], 0).reshape(2 * channels, half_len, blocks)
    real_freq, imag_freq = forward_dft(stacked, tables)
    data_real, filter_real = (real_freq[:channels], real_freq[channels:])
    data_imag, filter_imag = (imag_freq[:channels], imag_freq[channels:])
    spectrum_real = data_real * filter_real - data_imag * filter_imag
    spectrum_imag = data_real * filter_imag + data_imag * filter_real
    return inverse_real(spectrum_real, spectrum_imag, tables).reshape(channels, length)


def body(tokens, in_weight, short_taps, skip_gain, long_filter, out_weight):
    row_count, chan_width = tokens.shape
    blocks = lax.axis_size("seq")
    part_width = chan_width // blocks
    flat_weight = in_weight.reshape(in_weight.shape[0], 3 * chan_width)
    whole = lax.all_gather(tokens, "chan", axis=1, tiled=True)
    projected = jnp.dot(
        whole,
        lax.all_gather(flat_weight, "seq", axis=0, tiled=True),
        preferred_element_type=jnp.float32,
    )
    projected = projected.astype(jnp.bfloat16).reshape(row_count, 3, chan_width)
    outgoing = jnp.transpose(projected, (1, 2, 0))
    filter_rows = jnp.transpose(long_filter)[None]
    channel_major, filter_major = (
        lax.all_to_all(outgoing, "seq", split_axis=1, concat_axis=2, tiled=True),
        lax.all_to_all(filter_rows, "seq", split_axis=1, concat_axis=2, tiled=True),
    )
    offset = lax.axis_index("seq") * part_width
    local_taps = lax.dynamic_slice_in_dim(short_taps, offset, part_width, 2)
    local_skip = lax.dynamic_slice_in_dim(skip_gain, offset, part_width, 0)
    values = channel_major.astype(jnp.float32)
    tap_count = short_taps.shape[1]
    length = values.shape[2]
    padded = jnp.pad(values, ((0, 0), (0, 0), (tap_count - 1, 0)))
    smoothed = jnp.zeros_like(values)
    for tap_index in range(tap_count):
        lag_start = tap_count - 1 - tap_index
        smoothed = (
            smoothed
            + local_taps[:, tap_index, :, None] * padded[:, :, lag_start : lag_start + length]
        )
    gate_query = smoothed[0]
    gated = smoothed[1] * smoothed[2]
    mixed_seq = (
        causal_conv(gated, filter_major[0].astype(jnp.float32), blocks)
        + local_skip[:, None] * gated
    )
    product = (mixed_seq * gate_query).astype(jnp.bfloat16)
    returned = lax.all_to_all(product, "seq", split_axis=1, concat_axis=0, tiled=True)
    summed = lax.psum_scatter(
        lax.dot_general(
            out_weight, returned, (((0,), (0,)), ((), ())), preferred_element_type=jnp.float32
        ).astype(jnp.bfloat16),
        "chan",
        scatter_dimension=0,
        tiled=True,
    ).astype(jnp.float32)
    return jnp.transpose(summed).astype(jnp.bfloat16)


def wave_tables(length):
    span = 2 * length
    outer = span // inner_len
    used, rows = outer // 2, outer // 2 + 1
    padded_rows = -(-rows // 8) * 8
    m, k = np.arange(used), np.arange(rows)
    n, j = np.arange(inner_len), np.arange(inner_len)
    angle = (2.0 * math.pi / outer) * (np.outer(k, m) % outer)
    ahead = np.zeros((2, padded_rows, used))
    ahead[0, :rows], ahead[1, :rows] = np.cos(angle), -np.sin(angle)
    weight = np.where((k == 0) | (k == used), 1.0, 2.0) / span
    back = np.zeros((used, 2, padded_rows))
    back[:, 0, :rows] = (np.cos(angle) * weight[:, None]).T
    back[:, 1, :rows] = (-np.sin(angle) * weight[:, None]).T
    turn = n[None, None, :] * (k[:, None, None] + outer * j[None, :, None]) % span
    cos, sin = np.cos(turn * (2.0 * math.pi / span)), np.sin(turn * (2.0 * math.pi / span))
    middle = np.concatenate(
        [np.concatenate([cos, sin], 2), np.concatenate([-sin, cos], 2)], 1
    )
    return tuple(
        jnp.asarray(table, jnp.bfloat16)
        for table in (
            ahead.reshape(2 * padded_rows, used),
            middle,
            np.swapaxes(middle, 1, 2),
            back.reshape(used, 2 * padded_rows),
        )
    )


def halve_kernel(where_ref, tokens, filters, weight, ours, theirs, *refs, plan):
    pieces, sems = refs[:-1], refs[-1]
    depth, side = where_ref[0] // 2, where_ref[0] % 2
    rows, half = ours.shape
    part = half // 4
    copies = []

    def copy(source, block, width, target):
        columns = pl.ds(pl.multiple_of(block * width, width), width)
        copies.append(
            pltpu.make_async_copy(source.at[:, columns], target, sems.at[len(copies)])
        )

    copy(tokens, side, half, ours)
    copy(tokens, 1 - side, half, theirs.at[pl.ds(0, rows), :])
    for i in range(4):
        target = theirs.at[pl.ds(rows, filters.shape[0]), pl.ds(i * part, part)]
        copy(filters, 2 * i + 1 - side, part, target)
    depth_rows = weight.shape[1]
    for piece, (turn, names) in zip(pieces, plan, strict=True):
        for i, name in enumerate(names):
            target = piece.at[pl.ds(i * depth_rows, depth_rows), :]
            copy(weight.at[name], jnp.bitwise_xor(depth, turn), piece.shape[1], target)
    for one in copies:
        one.start()
    for one in copies:
        one.wait()


def halve(where, tokens, filters, weight, plan):
    rows, half = tokens.shape[0], tokens.shape[1] // 2
    pieces = tuple(
        jax.ShapeDtypeStruct((len(names) * weight.shape[1], weight.shape[2] // 4), weight.dtype)
        for _, names in plan
    )
    vmem = pl.BlockSpec(memory_space=pltpu.VMEM)
    return pl.pallas_call(
        functools.partial(halve_kernel, plan=plan),
        out_shape=(
            jax.ShapeDtypeStruct((rows, half), tokens.dtype),
            jax.ShapeDtypeStruct((rows + filters.shape[0], half), tokens.dtype),
        )
        + pieces,
        in_specs=[pl.BlockSpec(memory_space=pltpu.SMEM)]
        + [pl.BlockSpec(memory_space=pl.ANY)] * 3,
        out_specs=(vmem,) * (2 + len(plan)),
        scratch_shapes=[
            pltpu.SemaphoreType.DMA((6 + sum(len(names) for _, names in plan),))
        ],
        compiler_params=pltpu.CompilerParams(vmem_limit_bytes=61 * 2**20),
        name="halve",
    )(where, tokens, filters, weight)


def cut_kernel(where_ref, weight, filters, filter_beside, *refs, plan, after):
    place = where_ref[0]
    depth, side = place // 2, place % 2
    outs, sems = refs[after:-1], refs[-1]
    copies = []

    def copy(source, target):
        copies.append(pltpu.make_async_copy(source, target, sems.at[len(copies)]))

    def columns_of(block, width):
        return pl.ds(pl.multiple_of(block * width, width), width)

    rows, width = weight.shape[1], outs[0].shape[1]
    half = width // 2
    for out, (turn, names) in zip(outs, plan, strict=True):
        block = jnp.bitwise_xor(depth, turn)
        low = 0
        for name in names:
            if name == "f":
                at = pl.ds(low, filters.shape[0])
                here = columns_of(2 * block + side, half)
                copy(filters.at[:, here], out.at[at, pl.ds(0, half)])
                there = columns_of(block, half)
                below = pl.ds(filter_beside.shape[0] - filters.shape[0], filters.shape[0])
                copy(filter_beside.at[below, there], out.at[at, pl.ds(half, half)])
                low += filters.shape[0]
            else:
                source = weight.at[name, :, columns_of(block, width)]
                copy(source, out.at[pl.ds(low, rows), :])
                low += rows
    for one in copies:
        one.start()
    for one in copies:
        one.wait()


def cut(where, weight, filters, filter_beside, plan, after):
    count_of = {"f": filters.shape[0]}
    shapes = []
    for _, names in plan:
        rows = sum(count_of.get(name, weight.shape[1]) for name in names)
        shapes.append(jax.ShapeDtypeStruct((rows, weight.shape[2] // 4), weight.dtype))
    return pl.pallas_call(
        functools.partial(cut_kernel, plan=plan, after=len(after)),
        out_shape=tuple(shapes),
        in_specs=[pl.BlockSpec(memory_space=pltpu.SMEM)]
        + [pl.BlockSpec(memory_space=pl.ANY)] * (3 + len(after)),
        out_specs=(pl.BlockSpec(memory_space=pltpu.VMEM),) * len(shapes),
        scratch_shapes=[pltpu.SemaphoreType.DMA((24,))],
        compiler_params=pltpu.CompilerParams(vmem_limit_bytes=8 * 2**20),
        name="cut",
    )(where, weight, filters, filter_beside, *after)


def join_kernel(*refs, pieces, outs):
    for out_ref, group in zip(refs[len(refs) - outs :], pieces, strict=True):
        start = 0
        for at, low, count in group:
            out_ref[start : start + count, :] = refs[at][low : low + count, :]
            start += count


def join(values, pieces, after):
    shapes = []
    for group in pieces:
        rows = sum(count for _, _, count in group)
        shapes.append(jax.ShapeDtypeStruct((rows, values[0].shape[1]), values[0].dtype))
    vmem = pl.BlockSpec(memory_space=pltpu.VMEM)
    return pl.pallas_call(
        functools.partial(join_kernel, pieces=pieces, outs=len(pieces)),
        out_shape=tuple(shapes),
        in_specs=[vmem] * len(values) + [pl.BlockSpec(memory_space=pl.ANY)] * len(after),
        out_specs=(vmem,) * len(shapes),
        compiler_params=pltpu.CompilerParams(vmem_limit_bytes=8 * 2**20),
        name="join",
    )(*values, *after)


def project_kernel(where_ref, *refs, lows, after):
    line, across, cores, parts = refs[:4], refs[4:7], refs[7:9], refs[9:13]
    own_ref, send_ref, weights = refs[13 + after :]
    place, chan = where_ref[0], where_ref[1]
    depth, side = place // 2, place % 2
    rows = line[0].shape[1]
    for i in range(4):
        slot = jnp.bitwise_xor(depth, jnp.bitwise_xor(chan, i))
        start = pl.multiple_of(slot * rows, rows)
        weights[pl.ds(start, rows), :] = parts[i][lows[i] : lows[i] + rows, :]
    length, half = own_ref.shape
    block = length // 8
    for step in range(4):
        low = 4 * block * (step % 2)
        both = cores[step // 2]
        beside = across[(0, 1, 1, 2)[step]]
        at = 2 * block if step == 1 else 0
        joined = jnp.concatenate(
            [
                line[step][...],
                both[low : low + 2 * block, :],
                beside[at : at + 2 * block, :],
                both[low + 2 * block : low + 4 * block, :],
            ],
            1,
        )
        total = jnp.dot(joined, weights[...], preferred_element_type=jnp.float32)
        left, right = total[:, :half], total[:, half:]
        own = jnp.where(side == 0, left, right)
        send = jnp.where(side == 0, right, left).astype(jnp.bfloat16)
        for pair in range(2):
            start = pl.multiple_of(jnp.bitwise_xor(place, 2 * step + pair) * block, block)
            own_ref[pl.ds(start, block), :] = own[pair * block : (pair + 1) * block]
            send_ref[pl.ds(start, block), :] = send[pair * block : (pair + 1) * block]


def project(where, line, across, cores, parts, lows, length, after):
    depth, width = line[0].shape[1], parts[0].shape[1]
    vmem = pl.BlockSpec(memory_space=pltpu.VMEM)
    return pl.pallas_call(
        functools.partial(project_kernel, lows=lows, after=len(after)),
        out_shape=(
            jax.ShapeDtypeStruct((length, width // 2), jnp.float32),
            jax.ShapeDtypeStruct((length, width // 2), jnp.bfloat16),
        ),
        in_specs=[pl.BlockSpec(memory_space=pltpu.SMEM)]
        + [vmem] * 13
        + [pl.BlockSpec(memory_space=pl.ANY)] * len(after),
        out_specs=(vmem, vmem),
        scratch_shapes=[pltpu.VMEM((4 * depth, width), jnp.bfloat16)],
        compiler_params=pltpu.CompilerParams(vmem_limit_bytes=12 * 2**20),
        cost_estimate=pl.CostEstimate(
            flops=2 * length * 4 * depth * 2 * width,
            bytes_accessed=2 * length * 4 * depth,
            transcendentals=0,
        ),
        name="project",
    )(where, *line, *across, *cores, *parts, *after)


def smooth_into(padded, own_ref, recv_ref, taps, branch, store):
    length = own_ref.shape[0]
    tap_count = taps.shape[1]
    block = length // 8
    padded[0:8, :] = jnp.zeros((8, padded.shape[1]), jnp.float32)
    for i in range(8):
        rows = slice(i * block, (i + 1) * block)
        padded[8 + i * block : 8 + (i + 1) * block, :] = own_ref[rows, :] + recv_ref[
            rows, :
        ].astype(jnp.float32)
    for i in range(8):
        total = None
        for tap in range(tap_count):
            start = 8 + i * block - tap
            term = taps[branch, tap : tap + 1, :] * padded[start : start + block, :]
            total = term if total is None else total + term
        store(slice(i * block, (i + 1) * block), total)


def ahead_into(signal, table, waves):
    padded_rows, used = table.shape[0] // 2, table.shape[1]
    two = 2 * inner_len
    for n in range(0, inner_len, 2):
        both = jnp.concatenate(
            [signal[pl.ds(n + i, used, stride=inner_len), :] for i in range(2)], 1
        ).astype(jnp.bfloat16)
        wave = jnp.dot(table[...], both, preferred_element_type=jnp.float32)
        width = wave.shape[1] // 2
        for i in range(2):
            part = wave[:, i * width : (i + 1) * width]
            for half in range(2):
                at = pl.ds(half * inner_len + n + i, padded_rows, stride=two)
                waves[at, :] = part[half * padded_rows : (half + 1) * padded_rows]


def unroll_of(rows):
    return 11 if rows % 11 == 0 else 1


def spectrum_kernel(where_ref, ahead, middle, *refs, lows):
    filters = refs[:4]
    freq_ref, lags, waves = refs[len(refs) - 3 :]
    place = where_ref[0]
    length, width = lags.shape
    block = length // 8
    rows, two = middle.shape[:2]
    for i in range(4):
        at = slice(lows[i], lows[i] + block)
        for pair in range(2):
            start = pl.multiple_of(jnp.bitwise_xor(place, 2 * i + pair) * block, block)
            piece = filters[i][at, pair * width : (pair + 1) * width]
            lags[pl.ds(start, block), :] = piece.astype(jnp.float32)
    ahead_into(lags, ahead, waves)

    def one(k, _):
        at = pl.ds(pl.multiple_of(k * two, two), two)
        wave = waves[at, :].astype(jnp.bfloat16)
        freq_ref[at, :] = jnp.dot(middle[k], wave, preferred_element_type=jnp.float32)
        return 0

    lax.fori_loop(0, rows, one, 0, unroll=unroll_of(rows))


def spectrum(where, tables, filters, lows, length, after):
    ahead, middle = tables[:2]
    rows, two = middle.shape[:2]
    width = filters[0].shape[1] // 2
    vmem = pl.BlockSpec(memory_space=pltpu.VMEM)
    return pl.pallas_call(
        functools.partial(spectrum_kernel, lows=lows),
        out_shape=jax.ShapeDtypeStruct((rows * two, width), jnp.float32),
        in_specs=[pl.BlockSpec(memory_space=pltpu.SMEM)]
        + [vmem] * 6
        + [pl.BlockSpec(memory_space=pl.ANY)] * len(after),
        out_specs=vmem,
        scratch_shapes=[
            pltpu.VMEM((length, width), jnp.float32),
            pltpu.VMEM((ahead.shape[0] // 2 * two, width), jnp.float32),
        ],
        compiler_params=pltpu.CompilerParams(vmem_limit_bytes=8 * 2**20),
        cost_estimate=pl.CostEstimate(
            flops=2 * 2 * length * inner_len * width, bytes_accessed=2**20, transcendentals=0
        ),
        name="spectrum",
    )(where, ahead, middle, *filters, *after)


def mix_kernel(
    where_ref,
    own1,
    recv1,
    own2,
    recv2,
    taps_ref,
    skip_ref,
    ahead,
    middle,
    middle_back,
    back,
    freq_ref,
    weight,
    *refs,
    after,
):
    mixed_ref, held_ref, padded, gated, waves, sums, sem = refs[after:]
    loading = pltpu.make_async_copy(weight, held_ref, sem)
    loading.start()
    place = where_ref[0]
    width = own1.shape[1]
    ours = pl.ds(pl.multiple_of(place * width, width), width)
    taps, skip = taps_ref[:, :, ours], skip_ref[:, ours]
    rows, two = middle.shape[0], middle.shape[1]
    padded_rows = ahead.shape[0] // 2
    used = ahead.shape[1]

    def first(at, value):
        gated[at, :] = value

    def second(at, value):
        gated[at, :] = gated[at, :] * value

    smooth_into(padded, own1, recv1, taps, 1, first)
    smooth_into(padded, own2, recv2, taps, 2, second)
    ahead_into(gated, ahead, waves)
    if padded_rows > rows:
        sums[rows * two :, :] = jnp.zeros(((padded_rows - rows) * two, width), jnp.float32)

    def one(k, _):
        at = pl.ds(pl.multiple_of(k * two, two), two)
        wave = waves[at, :].astype(jnp.bfloat16)
        data = jnp.dot(middle[k], wave, preferred_element_type=jnp.float32)
        filters = freq_ref[at, :]
        data_real, filter_real = data[:inner_len], filters[:inner_len]
        data_imag, filter_imag = data[inner_len:], filters[inner_len:]
        product = jnp.concatenate(
            [
                data_real * filter_real - data_imag * filter_imag,
                data_real * filter_imag + data_imag * filter_real,
            ],
            0,
        ).astype(jnp.bfloat16)
        sums[at, :] = jnp.dot(middle_back[k], product, preferred_element_type=jnp.float32)
        return 0

    lax.fori_loop(0, rows, one, 0, unroll=unroll_of(rows))
    for n in range(0, inner_len, 2):
        pieces = [
            jnp.concatenate(
                [
                    sums[pl.ds(n + i, padded_rows, stride=two), :],
                    sums[pl.ds(inner_len + n + i, padded_rows, stride=two), :],
                ],
                0,
            )
            for i in range(2)
        ]
        wave = jnp.dot(
            back[...],
            jnp.concatenate(pieces, 1).astype(jnp.bfloat16),
            preferred_element_type=jnp.float32,
        )
        for i in range(2):
            at = pl.ds(n + i, used, stride=inner_len)
            mixed_ref[at, :] = wave[:, i * width : (i + 1) * width] + skip * gated[at, :]
    loading.wait()


def mix(where, own1, recv1, own2, recv2, taps, skip, tables, freq, weight, after):
    length, width = own1.shape
    two = tables[1].shape[1]
    padded_rows = tables[0].shape[0] // 2
    vmem = pl.BlockSpec(memory_space=pltpu.VMEM)
    return pl.pallas_call(
        functools.partial(mix_kernel, after=len(after)),
        out_shape=(
            jax.ShapeDtypeStruct((length, width), jnp.float32),
            jax.ShapeDtypeStruct(weight.shape, weight.dtype),
        ),
        in_specs=[pl.BlockSpec(memory_space=pltpu.SMEM)]
        + [vmem] * 11
        + [pl.BlockSpec(memory_space=pl.ANY)] * (1 + len(after)),
        out_specs=(vmem, vmem),
        scratch_shapes=[
            pltpu.VMEM((length + 8, width), jnp.float32),
            pltpu.VMEM((length, width), jnp.float32),
            pltpu.VMEM((padded_rows * two, width), jnp.float32),
            pltpu.VMEM((padded_rows * two, width), jnp.float32),
            pltpu.SemaphoreType.DMA,
        ],
        compiler_params=pltpu.CompilerParams(vmem_limit_bytes=16 * 2**20),
        cost_estimate=pl.CostEstimate(
            flops=2 * 6 * length * inner_len * width, bytes_accessed=6 * 2**20, transcendentals=0
        ),
        name="mix",
    )(where, own1, recv1, own2, recv2, taps, skip, *tables, freq, weight, *after)


def gate_kernel(where_ref, own0, recv0, mixed_ref, taps_ref, *refs):
    outs, padded, product = refs[:8], refs[8], refs[9]
    place = where_ref[0]
    block, width = own0.shape[0] // 8, own0.shape[1]
    taps = taps_ref[:, :, pl.ds(pl.multiple_of(place * width, width), width)]

    def store(at, value):
        product[at, :] = (mixed_ref[at, :] * value).astype(jnp.bfloat16)

    smooth_into(padded, own0, recv0, taps, 0, store)
    for i in range(8):
        start = pl.multiple_of(jnp.bitwise_xor(place, i) * block, block)
        outs[i][...] = product[pl.ds(start, block), :]


def gate(where, own0, recv0, mixed, taps):
    length, width = own0.shape
    vmem = pl.BlockSpec(memory_space=pltpu.VMEM)
    return pl.pallas_call(
        gate_kernel,
        out_shape=(jax.ShapeDtypeStruct((length // 8, width), jnp.bfloat16),) * 8,
        in_specs=[pl.BlockSpec(memory_space=pltpu.SMEM)] + [vmem] * 4,
        out_specs=(vmem,) * 8,
        scratch_shapes=[
            pltpu.VMEM((length + 8, width), jnp.float32),
            pltpu.VMEM((length, width), jnp.bfloat16),
        ],
        compiler_params=pltpu.CompilerParams(vmem_limit_bytes=8 * 2**20),
        cost_estimate=pl.CostEstimate(
            flops=8 * length * width, bytes_accessed=12 * length * width, transcendentals=0
        ),
        name="gate",
    )(where, own0, recv0, mixed, taps)


def emit_kernel(where_ref, weight, *refs, order, turns, added):
    parts, extra = refs[:8], refs[8 : 8 + added]
    outs, joined = refs[8 + added : -1], refs[-1]
    place, chan = where_ref[0], where_ref[1]
    width = parts[0].shape[1]
    columns = outs[0].shape[1]
    tile = 256
    for part, source in zip(parts, order, strict=True):
        start = pl.multiple_of(jnp.bitwise_xor(place, source) * width, width)
        joined[:, pl.ds(start, width)] = part[...]
    for i, turn in enumerate(turns):
        for low in range(0, columns, tile):
            start = pl.multiple_of(jnp.bitwise_xor(chan, turn) * columns + low, tile)
            total = jnp.dot(
                joined[...], weight[:, pl.ds(start, tile)], preferred_element_type=jnp.float32
            )
            if added:
                total = total + extra[i][:, low : low + tile].astype(jnp.float32)
            outs[i][:, low : low + tile] = total.astype(outs[i].dtype)


def emit(where, parts, order, weight, turns, extra, out_dtype):
    rows, width = parts[0].shape
    columns = weight.shape[1] // 4
    vmem = pl.BlockSpec(memory_space=pltpu.VMEM)
    shape = jax.ShapeDtypeStruct((rows, columns), out_dtype)
    return pl.pallas_call(
        functools.partial(emit_kernel, order=order, turns=turns, added=len(extra)),
        out_shape=(shape,) * len(turns),
        in_specs=[pl.BlockSpec(memory_space=pltpu.SMEM)] + [vmem] * (9 + len(extra)),
        out_specs=(vmem,) * len(turns),
        scratch_shapes=[pltpu.VMEM((rows, 8 * width), jnp.bfloat16)],
        compiler_params=pltpu.CompilerParams(vmem_limit_bytes=8 * 2**20),
        cost_estimate=pl.CostEstimate(
            flops=2 * rows * weight.shape[0] * columns * len(turns),
            bytes_accessed=2 * weight.shape[0] * columns * len(turns),
            transcendentals=0,
        ),
        name="emit",
    )(where, weight, *parts, *extra)


def swap(value, axis, count, turn):
    return lax.ppermute(value, axis, [(i, i ^ turn) for i in range(count)])


def fast_body(tokens, in_weight, short_taps, skip_gain, long_filter, out_weight):
    seq, chans = lax.axis_size("seq"), lax.axis_size("chan")
    place, chan = lax.axis_index("seq"), lax.axis_index("chan")
    rows, width = tokens.shape
    length = rows * seq
    part = width // seq
    where = jnp.stack([place, chan]).astype(jnp.int32)

    weight = jnp.transpose(in_weight, (1, 0, 2))

    lags = tokens.shape[0]
    rows = in_weight.shape[0]

    ours, theirs, cut1_2, cut_1 = halve(
        where, tokens, long_filter, weight, [(2, (1,)), (1, (1, 2))]
    )
    beside = swap(theirs, "seq", seq, 1)
    w1_2, w_1 = swap(cut1_2, "seq", seq, 4), swap(cut_1, "seq", seq, 2)
    whole = [(0, 0, lags), (1, 0, lags)]
    (pair,) = join([ours, beside], [whole], [w1_2])
    far = swap(pair, "seq", seq, 4)
    near = swap(pair, "seq", seq, 2)
    pair_across = swap(pair, "chan", chans, 2)
    inputs = (where, weight, long_filter, beside)
    plan = [(0, (1, 2, 0, "f")), (3, (1, 2, "f"))]
    plan += [(2, (0, "f")), (3, (0,)), (1, (0, "f")), (2, (2,))]
    w_0, cut_3, cut0_2, cut0_3, cut0_1, cut2_2 = cut(*inputs, plan, [pair])
    (far_and_near,) = join(
        [far, near],
        [[(0, 0, 2 * lags), (1, 0, 2 * lags)]],
        [pair_across, cut_3, w_1],
    )
    w_3 = swap(cut_3, "seq", seq, 6)
    w2_2 = swap(cut2_2, "seq", seq, 4)
    far_near = swap(far, "seq", seq, 2)
    across = swap(far_and_near, "chan", chans, 2)
    every = [(0, 0, 2 * lags), (1, 0, 2 * lags)]
    (first,) = join(
        [pair, pair_across, near, across],
        [every + [(2, 0, 2 * lags), (3, 2 * lags, 2 * lags)]],
        [w_3, w2_2],
    )
    core_a = swap(first, "chan", chans, 1)
    far_near_across = swap(far_near, "chan", chans, 2)
    (second,) = join(
        [far, across, far_near, far_near_across],
        [every + [(2, 0, 2 * lags), (3, 0, 2 * lags)]],
        [],
    )
    core_b = swap(second, "chan", chans, 1)
    line, across = [pair, near, far, far_near], [pair_across, across, far_near_across]
    cores = [core_a, core_b]
    shared = (where, line, across, cores)
    own1, send1 = project(*shared, [w_0, w_1, w1_2, w_3], (0,) * 4, length, [])
    recv1 = swap(send1, "seq", seq, 1)
    w0_2, w0_3 = swap(cut0_2, "seq", seq, 4), swap(cut0_3, "seq", seq, 6)
    w0_1 = swap(cut0_1, "seq", seq, 2)
    tables = wave_tables(length)
    own2, send2 = project(*shared, [w_0, w_1, w2_2, w_3], (rows, rows, 0, rows), length, [])
    recv2 = swap(send2, "seq", seq, 1)
    freq = spectrum(
        where, tables, [w_0, w0_1, w0_2, w_3], (3 * rows, rows, rows, 2 * rows), length, [send2]
    )
    parts0 = [w_0, w0_1, w0_2, w0_3]
    own0, send0 = project(*shared, parts0, (2 * rows, 0, 0, 0), length, [])
    recv0 = swap(send0, "seq", seq, 1)
    mixed, held = mix(
        where,
        own1,
        recv1,
        own2,
        recv2,
        short_taps,
        skip_gain[None],
        tables,
        freq,
        out_weight,
        [send0],
    )
    pieces = gate(where, own0, recv0, mixed, short_taps)
    order = (6, 7, 4, 5, 2, 3, 1, 0)
    joined = [swap(pieces[turn], "seq", seq, turn) if turn else pieces[0] for turn in order]

    (across_out,) = emit(where, joined, order, held, (3,), [], jnp.bfloat16)
    from_core = swap(across_out, "chan", chans, 1)
    (beside_out,) = emit(where, joined, order, held, (1,), [], jnp.bfloat16)
    near_sum = swap(beside_out, "chan", chans, 1)
    (chip_out,) = emit(where, joined, order, held, (2,), [from_core], jnp.bfloat16)
    from_chip = swap(chip_out, "chan", chans, 2)
    (own,) = emit(where, joined, order, held, (0,), [near_sum], jnp.float32)
    return (own + from_chip.astype(jnp.float32)).astype(jnp.bfloat16)


def solution(mesh):
    in_specs = (
        P("seq", "chan"),
        P("seq", None, "chan"),
        P(None, None, "chan"),
        P("chan"),
        P("seq", "chan"),
        P("chan", None),
    )
    out_specs = P("seq", "chan")
    seq, chans = mesh.shape["seq"], mesh.shape["chan"]
    chosen = fast_body if seq == 8 and chans == 4 else body
    return jax.shard_map(chosen, mesh=mesh, in_specs=in_specs, out_specs=out_specs, check_vma=False)
```

```python
import functools
import math

import jax
import jax.numpy as jnp
import numpy as np
from jax import lax
from jax.experimental import pallas as pl
from jax.experimental.pallas import tpu as pltpu
from jax.sharding import PartitionSpec as P

exact_prec = lax.Precision.HIGHEST
inner_len = 64


def dft_tables(half_len, blocks):
    full_len = 2 * half_len
    full_size = full_len * blocks
    half_index = jnp.arange(half_len, dtype=jnp.int32)
    full_index = jnp.arange(full_len, dtype=jnp.int32)
    block_index = jnp.arange(blocks, dtype=jnp.int32)
    outer_angle = (half_index[:, None] * full_index[None, :] % full_len).astype(jnp.float32) * (
        2.0 * math.pi / full_len
    )
    inner_angle = (block_index[:, None] * block_index[None, :] % blocks).astype(jnp.float32) * (
        2.0 * math.pi / blocks
    )
    twist_angle = (full_index[:, None] * block_index[None, :] % full_size).astype(jnp.float32) * (
        2.0 * math.pi / full_size
    )
    return (
        jnp.cos(outer_angle),
        jnp.sin(outer_angle),
        jnp.cos(inner_angle),
        jnp.sin(inner_angle),
        jnp.cos(twist_angle),
        jnp.sin(twist_angle),
    )


def forward_dft(signal, tables):
    outer_cos, outer_sin, inner_cos, inner_sin, twist_cos, twist_sin = tables
    real_section = jnp.einsum("cmn,mk->ckn", signal, outer_cos, precision=exact_prec)
    imag_section = -jnp.einsum("cmn,mk->ckn", signal, outer_sin, precision=exact_prec)
    real_twist = real_section * twist_cos + imag_section * twist_sin
    imag_twist = imag_section * twist_cos - real_section * twist_sin
    real_freq = jnp.einsum("ckn,nj->ckj", real_twist, inner_cos, precision=exact_prec) + jnp.einsum(
        "ckn,nj->ckj", imag_twist, inner_sin, precision=exact_prec
    )
    imag_freq = jnp.einsum("ckn,nj->ckj", imag_twist, inner_cos, precision=exact_prec) - jnp.einsum(
        "ckn,nj->ckj", real_twist, inner_sin, precision=exact_prec
    )
    return (real_freq, imag_freq)


def inverse_real(spectrum_real, spectrum_imag, tables):
    outer_cos, outer_sin, inner_cos, inner_sin, twist_cos, twist_sin = tables
    full_size = outer_cos.shape[1] * inner_cos.shape[0]
    back_real = jnp.einsum(
        "ckj,jn->ckn", spectrum_real, inner_cos, precision=exact_prec
    ) - jnp.einsum("ckj,jn->ckn", spectrum_imag, inner_sin, precision=exact_prec)
    back_imag = jnp.einsum(
        "ckj,jn->ckn", spectrum_imag, inner_cos, precision=exact_prec
    ) + jnp.einsum("ckj,jn->ckn", spectrum_real, inner_sin, precision=exact_prec)
    turn_real = back_real * twist_cos - back_imag * twist_sin
    turn_imag = back_imag * twist_cos + back_real * twist_sin
    summed_real = jnp.einsum(
        "ckn,mk->cmn", turn_real, outer_cos, precision=exact_prec
    ) - jnp.einsum("ckn,mk->cmn", turn_imag, outer_sin, precision=exact_prec)
    return summed_real / full_size


def causal_conv(signal, kernel, blocks):
    channels, length = signal.shape
    half_len = length // blocks
    tables = dft_tables(half_len, blocks)
    stacked = jnp.concatenate([signal, kernel], 0).reshape(2 * channels, half_len, blocks)
    real_freq, imag_freq = forward_dft(stacked, tables)
    data_real, filter_real = (real_freq[:channels], real_freq[channels:])
    data_imag, filter_imag = (imag_freq[:channels], imag_freq[channels:])
    spectrum_real = data_real * filter_real - data_imag * filter_imag
    spectrum_imag = data_real * filter_imag + data_imag * filter_real
    return inverse_real(spectrum_real, spectrum_imag, tables).reshape(channels, length)


def body(tokens, in_weight, short_taps, skip_gain, long_filter, out_weight):
    row_count, chan_width = tokens.shape
    blocks = lax.axis_size("seq")
    part_width = chan_width // blocks
    flat_weight = in_weight.reshape(in_weight.shape[0], 3 * chan_width)
    whole = lax.all_gather(tokens, "chan", axis=1, tiled=True)
    projected = jnp.dot(
        whole,
        lax.all_gather(flat_weight, "seq", axis=0, tiled=True),
        preferred_element_type=jnp.float32,
    )
    projected = projected.astype(jnp.bfloat16).reshape(row_count, 3, chan_width)
    outgoing = jnp.transpose(projected, (1, 2, 0))
    filter_rows = jnp.transpose(long_filter)[None]
    channel_major, filter_major = (
        lax.all_to_all(outgoing, "seq", split_axis=1, concat_axis=2, tiled=True),
        lax.all_to_all(filter_rows, "seq", split_axis=1, concat_axis=2, tiled=True),
    )
    offset = lax.axis_index("seq") * part_width
    local_taps = lax.dynamic_slice_in_dim(short_taps, offset, part_width, 2)
    local_skip = lax.dynamic_slice_in_dim(skip_gain, offset, part_width, 0)
    values = channel_major.astype(jnp.float32)
    tap_count = short_taps.shape[1]
    length = values.shape[2]
    padded = jnp.pad(values, ((0, 0), (0, 0), (tap_count - 1, 0)))
    smoothed = jnp.zeros_like(values)
    for tap_index in range(tap_count):
        lag_start = tap_count - 1 - tap_index
        smoothed = (
            smoothed
            + local_taps[:, tap_index, :, None] * padded[:, :, lag_start : lag_start + length]
        )
    gate_query = smoothed[0]
    gated = smoothed[1] * smoothed[2]
    mixed_seq = (
        causal_conv(gated, filter_major[0].astype(jnp.float32), blocks)
        + local_skip[:, None] * gated
    )
    product = (mixed_seq * gate_query).astype(jnp.bfloat16)
    returned = lax.all_to_all(product, "seq", split_axis=1, concat_axis=0, tiled=True)
    summed = lax.psum_scatter(
        lax.dot_general(
            out_weight, returned, (((0,), (0,)), ((), ())), preferred_element_type=jnp.float32
        ).astype(jnp.bfloat16),
        "chan",
        scatter_dimension=0,
        tiled=True,
    ).astype(jnp.float32)
    return jnp.transpose(summed).astype(jnp.bfloat16)


def wave_tables(length):
    span = 2 * length
    outer = span // inner_len
    used, rows = outer // 2, outer // 2 + 1
    padded_rows = -(-rows // 8) * 8
    m, k = np.arange(used), np.arange(rows)
    n, j = np.arange(inner_len), np.arange(inner_len)
    angle = (2.0 * math.pi / outer) * (np.outer(k, m) % outer)
    ahead = np.zeros((2, padded_rows, used))
    ahead[0, :rows], ahead[1, :rows] = np.cos(angle), -np.sin(angle)
    weight = np.where((k == 0) | (k == used), 1.0, 2.0) / span
    back = np.zeros((used, 2, padded_rows))
    back[:, 0, :rows] = (np.cos(angle) * weight[:, None]).T
    back[:, 1, :rows] = (-np.sin(angle) * weight[:, None]).T
    turn = n[None, None, :] * (k[:, None, None] + outer * j[None, :, None]) % span
    cos, sin = np.cos(turn * (2.0 * math.pi / span)), np.sin(turn * (2.0 * math.pi / span))
    middle = np.concatenate(
        [np.concatenate([cos, sin], 2), np.concatenate([-sin, cos], 2)], 1
    )
    return tuple(
        jnp.asarray(table, jnp.bfloat16)
        for table in (
            ahead.reshape(2 * padded_rows, used),
            middle,
            np.swapaxes(middle, 1, 2),
            back.reshape(used, 2 * padded_rows),
        )
    )


def halve_kernel(tokens, filters, weight, ours, theirs, *refs, plan):
    pieces, sems = refs[:-1], refs[-1]
    place = lax.axis_index("seq")
    depth, side = place // 2, place % 2
    rows, half = ours.shape
    part = half // 4
    copies = []

    def copy(source, block, width, target):
        columns = pl.ds(pl.multiple_of(block * width, width), width)
        copies.append(
            pltpu.make_async_copy(source.at[:, columns], target, sems.at[len(copies)])
        )

    copy(tokens, side, half, ours)
    copy(tokens, 1 - side, half, theirs.at[pl.ds(0, rows), :])
    for i in range(4):
        target = theirs.at[pl.ds(rows, filters.shape[0]), pl.ds(i * part, part)]
        copy(filters, 2 * i + 1 - side, part, target)
    depth_rows = weight.shape[1]
    for piece, (turn, names) in zip(pieces, plan, strict=True):
        for i, name in enumerate(names):
            target = piece.at[pl.ds(i * depth_rows, depth_rows), :]
            copy(weight.at[name], jnp.bitwise_xor(depth, turn), piece.shape[1], target)
    for one in copies:
        one.start()
    for one in copies:
        one.wait()


def halve(tokens, filters, weight, plan):
    rows, half = tokens.shape[0], tokens.shape[1] // 2
    pieces = tuple(
        jax.ShapeDtypeStruct((len(names) * weight.shape[1], weight.shape[2] // 4), weight.dtype)
        for _, names in plan
    )
    vmem = pl.BlockSpec(memory_space=pltpu.VMEM)
    return pl.pallas_call(
        functools.partial(halve_kernel, plan=plan),
        out_shape=(
            jax.ShapeDtypeStruct((rows, half), tokens.dtype),
            jax.ShapeDtypeStruct((rows + filters.shape[0], half), tokens.dtype),
        )
        + pieces,
        in_specs=[pl.BlockSpec(memory_space=pl.ANY)] * 3,
        out_specs=(vmem,) * (2 + len(plan)),
        scratch_shapes=[
            pltpu.SemaphoreType.DMA((6 + sum(len(names) for _, names in plan),))
        ],
        compiler_params=pltpu.CompilerParams(vmem_limit_bytes=60 * 2**20),
        name="halve",
    )(tokens, filters, weight)


def cut_kernel(weight, filters, filter_beside, *refs, plan, after):
    place = lax.axis_index("seq")
    depth, side = place // 2, place % 2
    outs, sems = refs[after:-1], refs[-1]
    copies = []

    def copy(source, target):
        copies.append(pltpu.make_async_copy(source, target, sems.at[len(copies)]))

    def columns_of(block, width):
        return pl.ds(pl.multiple_of(block * width, width), width)

    rows, width = weight.shape[1], outs[0].shape[1]
    half = width // 2
    for out, (turn, names) in zip(outs, plan, strict=True):
        block = jnp.bitwise_xor(depth, turn)
        low = 0
        for name in names:
            if name == "f":
                at = pl.ds(low, filters.shape[0])
                here = columns_of(2 * block + side, half)
                copy(filters.at[:, here], out.at[at, pl.ds(0, half)])
                there = columns_of(block, half)
                below = pl.ds(filter_beside.shape[0] - filters.shape[0], filters.shape[0])
                copy(filter_beside.at[below, there], out.at[at, pl.ds(half, half)])
                low += filters.shape[0]
            else:
                source = weight.at[name, :, columns_of(block, width)]
                copy(source, out.at[pl.ds(low, rows), :])
                low += rows
    for one in copies:
        one.start()
    for one in copies:
        one.wait()


def cut(weight, filters, filter_beside, plan, after):
    count_of = {"f": filters.shape[0]}
    shapes = []
    for _, names in plan:
        rows = sum(count_of.get(name, weight.shape[1]) for name in names)
        shapes.append(jax.ShapeDtypeStruct((rows, weight.shape[2] // 4), weight.dtype))
    return pl.pallas_call(
        functools.partial(cut_kernel, plan=plan, after=len(after)),
        out_shape=tuple(shapes),
        in_specs=[pl.BlockSpec(memory_space=pl.ANY)] * (3 + len(after)),
        out_specs=(pl.BlockSpec(memory_space=pltpu.VMEM),) * len(shapes),
        scratch_shapes=[pltpu.SemaphoreType.DMA((24,))],
        compiler_params=pltpu.CompilerParams(vmem_limit_bytes=8 * 2**20),
        name="cut",
    )(weight, filters, filter_beside, *after)


def join_kernel(*refs, pieces, outs):
    for out_ref, group in zip(refs[len(refs) - outs :], pieces, strict=True):
        start = 0
        for at, low, count in group:
            out_ref[start : start + count, :] = refs[at][low : low + count, :]
            start += count


def join(values, pieces, after):
    shapes = []
    for group in pieces:
        rows = sum(count for _, _, count in group)
        shapes.append(jax.ShapeDtypeStruct((rows, values[0].shape[1]), values[0].dtype))
    vmem = pl.BlockSpec(memory_space=pltpu.VMEM)
    return pl.pallas_call(
        functools.partial(join_kernel, pieces=pieces, outs=len(pieces)),
        out_shape=tuple(shapes),
        in_specs=[vmem] * len(values) + [pl.BlockSpec(memory_space=pl.ANY)] * len(after),
        out_specs=(vmem,) * len(shapes),
        compiler_params=pltpu.CompilerParams(vmem_limit_bytes=8 * 2**20),
        name="join",
    )(*values, *after)


def project_kernel(*refs, lows, after):
    line, across, cores, parts = refs[:4], refs[4:7], refs[7:9], refs[9:13]
    own_ref, send_ref, weights = refs[13 + after :]
    place, chan = lax.axis_index("seq"), lax.axis_index("chan")
    depth, side = place // 2, place % 2
    rows = line[0].shape[1]
    for i in range(4):
        slot = jnp.bitwise_xor(depth, jnp.bitwise_xor(chan, i))
        start = pl.multiple_of(slot * rows, rows)
        weights[pl.ds(start, rows), :] = parts[i][lows[i] : lows[i] + rows, :]
    length, half = own_ref.shape
    block = length // 8
    for step in range(4):
        low = 4 * block * (step % 2)
        both = cores[step // 2]
        beside = across[(0, 1, 1, 2)[step]]
        at = 2 * block if step == 1 else 0
        joined = jnp.concatenate(
            [
                line[step][...],
                both[low : low + 2 * block, :],
                beside[at : at + 2 * block, :],
                both[low + 2 * block : low + 4 * block, :],
            ],
            1,
        )
        total = jnp.dot(joined, weights[...], preferred_element_type=jnp.float32)
        left, right = total[:, :half], total[:, half:]
        own = jnp.where(side == 0, left, right)
        send = jnp.where(side == 0, right, left).astype(jnp.bfloat16)
        for pair in range(2):
            start = pl.multiple_of(jnp.bitwise_xor(place, 2 * step + pair) * block, block)
            own_ref[pl.ds(start, block), :] = own[pair * block : (pair + 1) * block]
            send_ref[pl.ds(start, block), :] = send[pair * block : (pair + 1) * block]


def project(line, across, cores, parts, lows, length, after):
    depth, width = line[0].shape[1], parts[0].shape[1]
    vmem = pl.BlockSpec(memory_space=pltpu.VMEM)
    return pl.pallas_call(
        functools.partial(project_kernel, lows=lows, after=len(after)),
        out_shape=(
            jax.ShapeDtypeStruct((length, width // 2), jnp.float32),
            jax.ShapeDtypeStruct((length, width // 2), jnp.bfloat16),
        ),
        in_specs=[vmem] * 13
        + [pl.BlockSpec(memory_space=pl.ANY)] * len(after),
        out_specs=(vmem, vmem),
        scratch_shapes=[pltpu.VMEM((4 * depth, width), jnp.bfloat16)],
        compiler_params=pltpu.CompilerParams(vmem_limit_bytes=12 * 2**20),
        cost_estimate=pl.CostEstimate(
            flops=2 * length * 4 * depth * 2 * width,
            bytes_accessed=2 * length * 4 * depth,
            transcendentals=0,
        ),
        name="project",
    )(*line, *across, *cores, *parts, *after)


def smooth_into(padded, own_ref, recv_ref, taps, branch, store):
    length = own_ref.shape[0]
    tap_count = taps.shape[1]
    block = length // 8
    padded[0:8, :] = jnp.zeros((8, padded.shape[1]), jnp.float32)
    for i in range(8):
        rows = slice(i * block, (i + 1) * block)
        padded[8 + i * block : 8 + (i + 1) * block, :] = own_ref[rows, :] + recv_ref[
            rows, :
        ].astype(jnp.float32)
    for i in range(8):
        total = None
        for tap in range(tap_count):
            start = 8 + i * block - tap
            term = taps[branch, tap : tap + 1, :] * padded[start : start + block, :]
            total = term if total is None else total + term
        store(slice(i * block, (i + 1) * block), total)


def ahead_into(signal, table, waves):
    padded_rows, used = table.shape[0] // 2, table.shape[1]
    two = 2 * inner_len
    for n in range(0, inner_len, 2):
        both = jnp.concatenate(
            [signal[pl.ds(n + i, used, stride=inner_len), :] for i in range(2)], 1
        ).astype(jnp.bfloat16)
        wave = jnp.dot(table[...], both, preferred_element_type=jnp.float32)
        width = wave.shape[1] // 2
        for i in range(2):
            part = wave[:, i * width : (i + 1) * width]
            for half in range(2):
                at = pl.ds(half * inner_len + n + i, padded_rows, stride=two)
                waves[at, :] = part[half * padded_rows : (half + 1) * padded_rows]


def unroll_of(rows):
    return 11 if rows % 11 == 0 else 1


def spectrum_kernel(ahead, middle, *refs, lows):
    filters = refs[:4]
    freq_ref, lags, waves = refs[len(refs) - 3 :]
    place = lax.axis_index("seq")
    length, width = lags.shape
    block = length // 8
    rows, two = middle.shape[:2]
    for i in range(4):
        at = slice(lows[i], lows[i] + block)
        for pair in range(2):
            start = pl.multiple_of(jnp.bitwise_xor(place, 2 * i + pair) * block, block)
            piece = filters[i][at, pair * width : (pair + 1) * width]
            lags[pl.ds(start, block), :] = piece.astype(jnp.float32)
    ahead_into(lags, ahead, waves)

    def one(k, _):
        at = pl.ds(pl.multiple_of(k * two, two), two)
        wave = waves[at, :].astype(jnp.bfloat16)
        freq_ref[at, :] = jnp.dot(middle[k], wave, preferred_element_type=jnp.float32)
        return 0

    lax.fori_loop(0, rows, one, 0, unroll=unroll_of(rows))


def spectrum(tables, filters, lows, length, after):
    ahead, middle = tables[:2]
    rows, two = middle.shape[:2]
    width = filters[0].shape[1] // 2
    vmem = pl.BlockSpec(memory_space=pltpu.VMEM)
    return pl.pallas_call(
        functools.partial(spectrum_kernel, lows=lows),
        out_shape=jax.ShapeDtypeStruct((rows * two, width), jnp.float32),
        in_specs=[vmem] * 6
        + [pl.BlockSpec(memory_space=pl.ANY)] * len(after),
        out_specs=vmem,
        scratch_shapes=[
            pltpu.VMEM((length, width), jnp.float32),
            pltpu.VMEM((ahead.shape[0] // 2 * two, width), jnp.float32),
        ],
        compiler_params=pltpu.CompilerParams(vmem_limit_bytes=8 * 2**20),
        cost_estimate=pl.CostEstimate(
            flops=2 * 2 * length * inner_len * width, bytes_accessed=2**20, transcendentals=0
        ),
        name="spectrum",
    )(ahead, middle, *filters, *after)


def mix_kernel(
    own1,
    recv1,
    own2,
    recv2,
    taps_ref,
    skip_ref,
    ahead,
    middle,
    middle_back,
    back,
    freq_ref,
    weight,
    *refs,
    after,
):
    mixed_ref, held_ref, padded, gated, waves, sums, sem = refs[after:]
    loading = pltpu.make_async_copy(weight, held_ref, sem)
    loading.start()
    place = lax.axis_index("seq")
    width = own1.shape[1]
    ours = pl.ds(pl.multiple_of(place * width, width), width)
    taps, skip = taps_ref[:, :, ours], skip_ref[:, ours]
    rows, two = middle.shape[0], middle.shape[1]
    padded_rows = ahead.shape[0] // 2
    used = ahead.shape[1]

    def first(at, value):
        gated[at, :] = value

    def second(at, value):
        gated[at, :] = gated[at, :] * value

    smooth_into(padded, own1, recv1, taps, 1, first)
    smooth_into(padded, own2, recv2, taps, 2, second)
    ahead_into(gated, ahead, waves)
    if padded_rows > rows:
        sums[rows * two :, :] = jnp.zeros(((padded_rows - rows) * two, width), jnp.float32)

    def one(k, _):
        at = pl.ds(pl.multiple_of(k * two, two), two)
        wave = waves[at, :].astype(jnp.bfloat16)
        data = jnp.dot(middle[k], wave, preferred_element_type=jnp.float32)
        filters = freq_ref[at, :]
        data_real, filter_real = data[:inner_len], filters[:inner_len]
        data_imag, filter_imag = data[inner_len:], filters[inner_len:]
        product = jnp.concatenate(
            [
                data_real * filter_real - data_imag * filter_imag,
                data_real * filter_imag + data_imag * filter_real,
            ],
            0,
        ).astype(jnp.bfloat16)
        sums[at, :] = jnp.dot(middle_back[k], product, preferred_element_type=jnp.float32)
        return 0

    lax.fori_loop(0, rows, one, 0, unroll=unroll_of(rows))
    for n in range(0, inner_len, 2):
        pieces = [
            jnp.concatenate(
                [
                    sums[pl.ds(n + i, padded_rows, stride=two), :],
                    sums[pl.ds(inner_len + n + i, padded_rows, stride=two), :],
                ],
                0,
            )
            for i in range(2)
        ]
        wave = jnp.dot(
            back[...],
            jnp.concatenate(pieces, 1).astype(jnp.bfloat16),
            preferred_element_type=jnp.float32,
        )
        for i in range(2):
            at = pl.ds(n + i, used, stride=inner_len)
            mixed_ref[at, :] = wave[:, i * width : (i + 1) * width] + skip * gated[at, :]
    loading.wait()


def mix(own1, recv1, own2, recv2, taps, skip, tables, freq, weight, after):
    length, width = own1.shape
    two = tables[1].shape[1]
    padded_rows = tables[0].shape[0] // 2
    vmem = pl.BlockSpec(memory_space=pltpu.VMEM)
    return pl.pallas_call(
        functools.partial(mix_kernel, after=len(after)),
        out_shape=(
            jax.ShapeDtypeStruct((length, width), jnp.float32),
            jax.ShapeDtypeStruct(weight.shape, weight.dtype),
        ),
        in_specs=[vmem] * 11
        + [pl.BlockSpec(memory_space=pl.ANY)] * (1 + len(after)),
        out_specs=(vmem, vmem),
        scratch_shapes=[
            pltpu.VMEM((length + 8, width), jnp.float32),
            pltpu.VMEM((length, width), jnp.float32),
            pltpu.VMEM((padded_rows * two, width), jnp.float32),
            pltpu.VMEM((padded_rows * two, width), jnp.float32),
            pltpu.SemaphoreType.DMA,
        ],
        compiler_params=pltpu.CompilerParams(vmem_limit_bytes=16 * 2**20),
        cost_estimate=pl.CostEstimate(
            flops=2 * 6 * length * inner_len * width, bytes_accessed=6 * 2**20, transcendentals=0
        ),
        name="mix",
    )(own1, recv1, own2, recv2, taps, skip, *tables, freq, weight, *after)


def gate_kernel(own0, recv0, mixed_ref, taps_ref, *refs):
    outs, padded, product = refs[:8], refs[8], refs[9]
    place = lax.axis_index("seq")
    block, width = own0.shape[0] // 8, own0.shape[1]
    taps = taps_ref[:, :, pl.ds(pl.multiple_of(place * width, width), width)]

    def store(at, value):
        product[at, :] = (mixed_ref[at, :] * value).astype(jnp.bfloat16)

    smooth_into(padded, own0, recv0, taps, 0, store)
    for i in range(8):
        start = pl.multiple_of(jnp.bitwise_xor(place, i) * block, block)
        outs[i][...] = product[pl.ds(start, block), :]


def gate(own0, recv0, mixed, taps):
    length, width = own0.shape
    vmem = pl.BlockSpec(memory_space=pltpu.VMEM)
    return pl.pallas_call(
        gate_kernel,
        out_shape=(jax.ShapeDtypeStruct((length // 8, width), jnp.bfloat16),) * 8,
        in_specs=[vmem] * 4,
        out_specs=(vmem,) * 8,
        scratch_shapes=[
            pltpu.VMEM((length + 8, width), jnp.float32),
            pltpu.VMEM((length, width), jnp.bfloat16),
        ],
        compiler_params=pltpu.CompilerParams(vmem_limit_bytes=8 * 2**20),
        cost_estimate=pl.CostEstimate(
            flops=8 * length * width, bytes_accessed=12 * length * width, transcendentals=0
        ),
        name="gate",
    )(own0, recv0, mixed, taps)


def emit_kernel(weight, *refs, order, turn, added):
    parts, extra = refs[: len(order)], refs[len(order) : len(order) + added]
    out_ref = refs[len(order) + added]
    place, chan = lax.axis_index("seq"), lax.axis_index("chan")
    columns = out_ref.shape[1]
    tile = 256
    if len(order) == 1:
        joined = parts[0]
    else:
        joined = refs[-1]
        width = parts[0].shape[1]
        for part, source in zip(parts, order, strict=True):
            start = pl.multiple_of(jnp.bitwise_xor(place, source) * width, width)
            joined[:, pl.ds(start, width)] = part[...]
    for low in range(0, columns, tile):
        start = pl.multiple_of(jnp.bitwise_xor(chan, turn) * columns + low, tile)
        total = jnp.dot(
            joined[...], weight[:, pl.ds(start, tile)], preferred_element_type=jnp.float32
        )
        for term in extra:
            total = total + term[:, low : low + tile].astype(jnp.float32)
        out_ref[:, low : low + tile] = total.astype(out_ref.dtype)


def emit(parts, order, weight, turn, extra, out_dtype):
    rows = parts[0].shape[0]
    depth, columns = weight.shape[0], weight.shape[1] // 4
    vmem = pl.BlockSpec(memory_space=pltpu.VMEM)
    shapes = [jax.ShapeDtypeStruct((rows, columns), out_dtype)]
    if len(order) > 1:
        shapes.append(jax.ShapeDtypeStruct((rows, depth), parts[0].dtype))
    return pl.pallas_call(
        functools.partial(emit_kernel, order=order, turn=turn, added=len(extra)),
        out_shape=tuple(shapes),
        in_specs=[vmem] * (1 + len(parts) + len(extra)),
        out_specs=(vmem,) * len(shapes),
        compiler_params=pltpu.CompilerParams(vmem_limit_bytes=8 * 2**20),
        cost_estimate=pl.CostEstimate(
            flops=2 * rows * depth * columns,
            bytes_accessed=2 * depth * columns,
            transcendentals=0,
        ),
        name="emit",
    )(weight, *parts, *extra)


def swap(value, axis, count, turn):
    return lax.ppermute(value, axis, [(i, i ^ turn) for i in range(count)])


def fast_body(tokens, in_weight, short_taps, skip_gain, long_filter, out_weight):
    seq, chans = lax.axis_size("seq"), lax.axis_size("chan")
    rows, width = tokens.shape
    length = rows * seq
    part = width // seq

    weight = jnp.transpose(in_weight, (1, 0, 2))

    lags = tokens.shape[0]
    rows = in_weight.shape[0]

    ours, theirs, cut1_2, cut_1 = halve(
        tokens, long_filter, weight, [(2, (1,)), (1, (1, 2))]
    )
    beside = swap(theirs, "seq", seq, 1)
    w1_2, w_1 = swap(cut1_2, "seq", seq, 4), swap(cut_1, "seq", seq, 2)
    whole = [(0, 0, lags), (1, 0, lags)]
    (pair,) = join([ours, beside], [whole], [w1_2])
    far = swap(pair, "seq", seq, 4)
    near = swap(pair, "seq", seq, 2)
    pair_across = swap(pair, "chan", chans, 2)
    inputs = (weight, long_filter, beside)
    plan = [(0, (1, 2, 0, "f")), (3, (1, 2, "f"))]
    plan += [(2, (0, "f")), (3, (0,)), (1, (0, "f")), (2, (2,))]
    w_0, cut_3, cut0_2, cut0_3, cut0_1, cut2_2 = cut(*inputs, plan, [pair])
    (far_and_near,) = join(
        [far, near],
        [[(0, 0, 2 * lags), (1, 0, 2 * lags)]],
        [pair_across, cut_3, w_1],
    )
    w_3 = swap(cut_3, "seq", seq, 6)
    w2_2 = swap(cut2_2, "seq", seq, 4)
    far_near = swap(far, "seq", seq, 2)
    across = swap(far_and_near, "chan", chans, 2)
    every = [(0, 0, 2 * lags), (1, 0, 2 * lags)]
    (first,) = join(
        [pair, pair_across, near, across],
        [every + [(2, 0, 2 * lags), (3, 2 * lags, 2 * lags)]],
        [w_3, w2_2],
    )
    core_a = swap(first, "chan", chans, 1)
    far_near_across = swap(far_near, "chan", chans, 2)
    (second,) = join(
        [far, across, far_near, far_near_across],
        [every + [(2, 0, 2 * lags), (3, 0, 2 * lags)]],
        [],
    )
    core_b = swap(second, "chan", chans, 1)
    line, across = [pair, near, far, far_near], [pair_across, across, far_near_across]
    cores = [core_a, core_b]
    shared = (line, across, cores)
    own1, send1 = project(*shared, [w_0, w_1, w1_2, w_3], (0,) * 4, length, [])
    recv1 = swap(send1, "seq", seq, 1)
    w0_2, w0_3 = swap(cut0_2, "seq", seq, 4), swap(cut0_3, "seq", seq, 6)
    w0_1 = swap(cut0_1, "seq", seq, 2)
    tables = wave_tables(length)
    own2, send2 = project(*shared, [w_0, w_1, w2_2, w_3], (rows, rows, 0, rows), length, [])
    recv2 = swap(send2, "seq", seq, 1)
    freq = spectrum(
        tables, [w_0, w0_1, w0_2, w_3], (3 * rows, rows, rows, 2 * rows), length, [send2]
    )
    parts0 = [w_0, w0_1, w0_2, w0_3]
    own0, send0 = project(*shared, parts0, (2 * rows, 0, 0, 0), length, [])
    recv0 = swap(send0, "seq", seq, 1)
    mixed, held = mix(
        own1,
        recv1,
        own2,
        recv2,
        short_taps,
        skip_gain[None],
        tables,
        freq,
        out_weight,
        [send0],
    )
    pieces = gate(own0, recv0, mixed, short_taps)
    order = (6, 7, 4, 5, 2, 3, 1, 0)
    joined = [swap(pieces[turn], "seq", seq, turn) if turn else pieces[0] for turn in order]

    across_out, rows_here = emit(joined, order, held, 3, [], jnp.bfloat16)
    from_core = swap(across_out, "chan", chans, 1)
    (beside_out,) = emit([rows_here], (0,), held, 1, [], jnp.bfloat16)
    near_sum = swap(beside_out, "chan", chans, 1)
    (chip_out,) = emit([rows_here], (0,), held, 2, [from_core], jnp.bfloat16)
    from_chip = swap(chip_out, "chan", chans, 2)
    (own,) = emit([rows_here], (0,), held, 0, [near_sum], jnp.float32)
    return (own + from_chip.astype(jnp.float32)).astype(jnp.bfloat16)


def solution(mesh):
    in_specs = (
        P("seq", "chan"),
        P("seq", None, "chan"),
        P(None, None, "chan"),
        P("chan"),
        P("seq", "chan"),
        P("chan", None),
    )
    out_specs = P("seq", "chan")
    seq, chans = mesh.shape["seq"], mesh.shape["chan"]
    chosen = fast_body if seq == 8 and chans == 4 else body
    return jax.shard_map(chosen, mesh=mesh, in_specs=in_specs, out_specs=out_specs, check_vma=False)
```

```python
import functools
import math

import jax
import jax.numpy as jnp
import numpy as np
from jax import lax
from jax.experimental import pallas as pl
from jax.experimental.pallas import tpu as pltpu
from jax.sharding import PartitionSpec as P

exact_prec = lax.Precision.HIGHEST
inner_len = 64


def dft_tables(half_len, blocks):
    full_len = 2 * half_len
    full_size = full_len * blocks
    half_index = jnp.arange(half_len, dtype=jnp.int32)
    full_index = jnp.arange(full_len, dtype=jnp.int32)
    block_index = jnp.arange(blocks, dtype=jnp.int32)
    outer_angle = (half_index[:, None] * full_index[None, :] % full_len).astype(jnp.float32) * (
        2.0 * math.pi / full_len
    )
    inner_angle = (block_index[:, None] * block_index[None, :] % blocks).astype(jnp.float32) * (
        2.0 * math.pi / blocks
    )
    twist_angle = (full_index[:, None] * block_index[None, :] % full_size).astype(jnp.float32) * (
        2.0 * math.pi / full_size
    )
    return (
        jnp.cos(outer_angle),
        jnp.sin(outer_angle),
        jnp.cos(inner_angle),
        jnp.sin(inner_angle),
        jnp.cos(twist_angle),
        jnp.sin(twist_angle),
    )


def forward_dft(signal, tables):
    outer_cos, outer_sin, inner_cos, inner_sin, twist_cos, twist_sin = tables
    real_section = jnp.einsum("cmn,mk->ckn", signal, outer_cos, precision=exact_prec)
    imag_section = -jnp.einsum("cmn,mk->ckn", signal, outer_sin, precision=exact_prec)
    real_twist = real_section * twist_cos + imag_section * twist_sin
    imag_twist = imag_section * twist_cos - real_section * twist_sin
    real_freq = jnp.einsum("ckn,nj->ckj", real_twist, inner_cos, precision=exact_prec) + jnp.einsum(
        "ckn,nj->ckj", imag_twist, inner_sin, precision=exact_prec
    )
    imag_freq = jnp.einsum("ckn,nj->ckj", imag_twist, inner_cos, precision=exact_prec) - jnp.einsum(
        "ckn,nj->ckj", real_twist, inner_sin, precision=exact_prec
    )
    return (real_freq, imag_freq)


def inverse_real(spectrum_real, spectrum_imag, tables):
    outer_cos, outer_sin, inner_cos, inner_sin, twist_cos, twist_sin = tables
    full_size = outer_cos.shape[1] * inner_cos.shape[0]
    back_real = jnp.einsum(
        "ckj,jn->ckn", spectrum_real, inner_cos, precision=exact_prec
    ) - jnp.einsum("ckj,jn->ckn", spectrum_imag, inner_sin, precision=exact_prec)
    back_imag = jnp.einsum(
        "ckj,jn->ckn", spectrum_imag, inner_cos, precision=exact_prec
    ) + jnp.einsum("ckj,jn->ckn", spectrum_real, inner_sin, precision=exact_prec)
    turn_real = back_real * twist_cos - back_imag * twist_sin
    turn_imag = back_imag * twist_cos + back_real * twist_sin
    summed_real = jnp.einsum(
        "ckn,mk->cmn", turn_real, outer_cos, precision=exact_prec
    ) - jnp.einsum("ckn,mk->cmn", turn_imag, outer_sin, precision=exact_prec)
    return summed_real / full_size


def causal_conv(signal, kernel, blocks):
    channels, length = signal.shape
    half_len = length // blocks
    tables = dft_tables(half_len, blocks)
    stacked = jnp.concatenate([signal, kernel], 0).reshape(2 * channels, half_len, blocks)
    real_freq, imag_freq = forward_dft(stacked, tables)
    data_real, filter_real = (real_freq[:channels], real_freq[channels:])
    data_imag, filter_imag = (imag_freq[:channels], imag_freq[channels:])
    spectrum_real = data_real * filter_real - data_imag * filter_imag
    spectrum_imag = data_real * filter_imag + data_imag * filter_real
    return inverse_real(spectrum_real, spectrum_imag, tables).reshape(channels, length)


def body(tokens, in_weight, short_taps, skip_gain, long_filter, out_weight):
    row_count, chan_width = tokens.shape
    blocks = lax.axis_size("seq")
    part_width = chan_width // blocks
    flat_weight = in_weight.reshape(in_weight.shape[0], 3 * chan_width)
    whole = lax.all_gather(tokens, "chan", axis=1, tiled=True)
    projected = jnp.dot(
        whole,
        lax.all_gather(flat_weight, "seq", axis=0, tiled=True),
        preferred_element_type=jnp.float32,
    )
    projected = projected.astype(jnp.bfloat16).reshape(row_count, 3, chan_width)
    outgoing = jnp.transpose(projected, (1, 2, 0))
    filter_rows = jnp.transpose(long_filter)[None]
    channel_major, filter_major = (
        lax.all_to_all(outgoing, "seq", split_axis=1, concat_axis=2, tiled=True),
        lax.all_to_all(filter_rows, "seq", split_axis=1, concat_axis=2, tiled=True),
    )
    offset = lax.axis_index("seq") * part_width
    local_taps = lax.dynamic_slice_in_dim(short_taps, offset, part_width, 2)
    local_skip = lax.dynamic_slice_in_dim(skip_gain, offset, part_width, 0)
    values = channel_major.astype(jnp.float32)
    tap_count = short_taps.shape[1]
    length = values.shape[2]
    padded = jnp.pad(values, ((0, 0), (0, 0), (tap_count - 1, 0)))
    smoothed = jnp.zeros_like(values)
    for tap_index in range(tap_count):
        lag_start = tap_count - 1 - tap_index
        smoothed = (
            smoothed
            + local_taps[:, tap_index, :, None] * padded[:, :, lag_start : lag_start + length]
        )
    gate_query = smoothed[0]
    gated = smoothed[1] * smoothed[2]
    mixed_seq = (
        causal_conv(gated, filter_major[0].astype(jnp.float32), blocks)
        + local_skip[:, None] * gated
    )
    product = (mixed_seq * gate_query).astype(jnp.bfloat16)
    returned = lax.all_to_all(product, "seq", split_axis=1, concat_axis=0, tiled=True)
    summed = lax.psum_scatter(
        lax.dot_general(
            out_weight, returned, (((0,), (0,)), ((), ())), preferred_element_type=jnp.float32
        ).astype(jnp.bfloat16),
        "chan",
        scatter_dimension=0,
        tiled=True,
    ).astype(jnp.float32)
    return jnp.transpose(summed).astype(jnp.bfloat16)


def wave_tables(length):
    span = 2 * length
    outer = span // inner_len
    used, rows = outer // 2, outer // 2 + 1
    padded_rows = -(-rows // 8) * 8
    m, k = np.arange(used), np.arange(rows)
    n, j = np.arange(inner_len), np.arange(inner_len)
    angle = (2.0 * math.pi / outer) * (np.outer(k, m) % outer)
    ahead = np.zeros((2, padded_rows, used))
    ahead[0, :rows], ahead[1, :rows] = np.cos(angle), -np.sin(angle)
    weight = np.where((k == 0) | (k == used), 1.0, 2.0) / span
    back = np.zeros((used, 2, padded_rows))
    back[:, 0, :rows] = (np.cos(angle) * weight[:, None]).T
    back[:, 1, :rows] = (-np.sin(angle) * weight[:, None]).T
    turn = n[None, None, :] * (k[:, None, None] + outer * j[None, :, None]) % span
    cos, sin = np.cos(turn * (2.0 * math.pi / span)), np.sin(turn * (2.0 * math.pi / span))
    middle = np.concatenate(
        [np.concatenate([cos, sin], 2), np.concatenate([-sin, cos], 2)], 1
    )
    return tuple(
        jnp.asarray(table, jnp.bfloat16)
        for table in (
            ahead.reshape(2 * padded_rows, used),
            middle,
            np.swapaxes(middle, 1, 2),
            back.reshape(used, 2 * padded_rows),
        )
    )


def halve_kernel(tokens, filters, weight, theirs, *refs, plan):
    pieces, sems = refs[:-1], refs[-1]
    place = lax.axis_index("seq")
    depth, side = place // 2, place % 2
    rows, half = tokens.shape[0], theirs.shape[1]
    part = half // 4
    copies = []

    def copy(source, block, width, target):
        columns = pl.ds(pl.multiple_of(block * width, width), width)
        copies.append(
            pltpu.make_async_copy(source.at[:, columns], target, sems.at[len(copies)])
        )

    copy(tokens, 1 - side, half, theirs.at[pl.ds(0, rows), :])
    for i in range(4):
        target = theirs.at[pl.ds(rows, filters.shape[0]), pl.ds(i * part, part)]
        copy(filters, 2 * i + 1 - side, part, target)
    depth_rows = weight.shape[1]
    for piece, (turn, names) in zip(pieces, plan, strict=True):
        for i, name in enumerate(names):
            target = piece.at[pl.ds(i * depth_rows, depth_rows), :]
            copy(weight.at[name], jnp.bitwise_xor(depth, turn), piece.shape[1], target)
    for one in copies:
        one.start()
    for one in copies:
        one.wait()


def halve(tokens, filters, weight, plan):
    rows, half = tokens.shape[0], tokens.shape[1] // 2
    pieces = tuple(
        jax.ShapeDtypeStruct((len(names) * weight.shape[1], weight.shape[2] // 4), weight.dtype)
        for _, names in plan
    )
    vmem = pl.BlockSpec(memory_space=pltpu.VMEM)
    return pl.pallas_call(
        functools.partial(halve_kernel, plan=plan),
        out_shape=(
            jax.ShapeDtypeStruct((rows + filters.shape[0], half), tokens.dtype),
        )
        + pieces,
        in_specs=[pl.BlockSpec(memory_space=pl.ANY)] * 3,
        out_specs=(vmem,) * (1 + len(plan)),
        scratch_shapes=[
            pltpu.SemaphoreType.DMA((5 + sum(len(names) for _, names in plan),))
        ],
        compiler_params=pltpu.CompilerParams(vmem_limit_bytes=60 * 2**20),
        name="halve",
    )(tokens, filters, weight)


def own_half_kernel(tokens, ours, sem):
    half = ours.shape[1]
    start = pl.multiple_of(lax.axis_index("seq") % 2 * half, half)
    copy = pltpu.make_async_copy(tokens.at[:, pl.ds(start, half)], ours, sem)
    copy.start()
    copy.wait()


def own_half(tokens, after):
    rows, half = tokens.shape[0], tokens.shape[1] // 2
    return pl.pallas_call(
        lambda *refs: own_half_kernel(refs[0], refs[-2], refs[-1]),
        out_shape=jax.ShapeDtypeStruct((rows, half), tokens.dtype),
        in_specs=[pl.BlockSpec(memory_space=pl.ANY)] * (1 + len(after)),
        out_specs=pl.BlockSpec(memory_space=pltpu.VMEM),
        scratch_shapes=[pltpu.SemaphoreType.DMA],
        compiler_params=pltpu.CompilerParams(vmem_limit_bytes=8 * 2**20),
        name="own_half",
    )(tokens, *after)


def cut_kernel(weight, filters, filter_beside, *refs, plan, after):
    place = lax.axis_index("seq")
    depth, side = place // 2, place % 2
    outs, sems = refs[after:-1], refs[-1]
    copies = []

    def copy(source, target):
        copies.append(pltpu.make_async_copy(source, target, sems.at[len(copies)]))

    def columns_of(block, width):
        return pl.ds(pl.multiple_of(block * width, width), width)

    rows, width = weight.shape[1], outs[0].shape[1]
    half = width // 2
    for out, (turn, names) in zip(outs, plan, strict=True):
        block = jnp.bitwise_xor(depth, turn)
        low = 0
        for name in names:
            if name == "f":
                at = pl.ds(low, filters.shape[0])
                here = columns_of(2 * block + side, half)
                copy(filters.at[:, here], out.at[at, pl.ds(0, half)])
                there = columns_of(block, half)
                below = pl.ds(filter_beside.shape[0] - filters.shape[0], filters.shape[0])
                copy(filter_beside.at[below, there], out.at[at, pl.ds(half, half)])
                low += filters.shape[0]
            else:
                source = weight.at[name, :, columns_of(block, width)]
                copy(source, out.at[pl.ds(low, rows), :])
                low += rows
    for one in copies:
        one.start()
    for one in copies:
        one.wait()


def cut(weight, filters, filter_beside, plan, after):
    count_of = {"f": filters.shape[0]}
    shapes = []
    for _, names in plan:
        rows = sum(count_of.get(name, weight.shape[1]) for name in names)
        shapes.append(jax.ShapeDtypeStruct((rows, weight.shape[2] // 4), weight.dtype))
    return pl.pallas_call(
        functools.partial(cut_kernel, plan=plan, after=len(after)),
        out_shape=tuple(shapes),
        in_specs=[pl.BlockSpec(memory_space=pl.ANY)] * (3 + len(after)),
        out_specs=(pl.BlockSpec(memory_space=pltpu.VMEM),) * len(shapes),
        scratch_shapes=[pltpu.SemaphoreType.DMA((24,))],
        compiler_params=pltpu.CompilerParams(vmem_limit_bytes=8 * 2**20),
        name="cut",
    )(weight, filters, filter_beside, *after)


def join_kernel(*refs, pieces, outs):
    for out_ref, group in zip(refs[len(refs) - outs :], pieces, strict=True):
        start = 0
        for at, low, count in group:
            out_ref[start : start + count, :] = refs[at][low : low + count, :]
            start += count


def join(values, pieces, after):
    shapes = []
    for group in pieces:
        rows = sum(count for _, _, count in group)
        shapes.append(jax.ShapeDtypeStruct((rows, values[0].shape[1]), values[0].dtype))
    vmem = pl.BlockSpec(memory_space=pltpu.VMEM)
    return pl.pallas_call(
        functools.partial(join_kernel, pieces=pieces, outs=len(pieces)),
        out_shape=tuple(shapes),
        in_specs=[vmem] * len(values) + [pl.BlockSpec(memory_space=pl.ANY)] * len(after),
        out_specs=(vmem,) * len(shapes),
        compiler_params=pltpu.CompilerParams(vmem_limit_bytes=8 * 2**20),
        name="join",
    )(*values, *after)


def project_kernel(*refs, lows, after):
    line, across, cores, parts = refs[:4], refs[4:7], refs[7:9], refs[9:13]
    own_ref, send_ref, weights = refs[13 + after :]
    place, chan = lax.axis_index("seq"), lax.axis_index("chan")
    depth, side = place // 2, place % 2
    rows = line[0].shape[1]
    for i in range(4):
        slot = jnp.bitwise_xor(depth, jnp.bitwise_xor(chan, i))
        start = pl.multiple_of(slot * rows, rows)
        weights[pl.ds(start, rows), :] = parts[i][lows[i] : lows[i] + rows, :]
    length, half = own_ref.shape
    block = length // 8
    for step in range(4):
        low = 4 * block * (step % 2)
        both = cores[step // 2]
        beside = across[(0, 1, 1, 2)[step]]
        at = 2 * block if step == 1 else 0
        joined = jnp.concatenate(
            [
                line[step][...],
                both[low : low + 2 * block, :],
                beside[at : at + 2 * block, :],
                both[low + 2 * block : low + 4 * block, :],
            ],
            1,
        )
        total = jnp.dot(joined, weights[...], preferred_element_type=jnp.float32)
        left, right = total[:, :half], total[:, half:]
        own = jnp.where(side == 0, left, right)
        send = jnp.where(side == 0, right, left).astype(jnp.bfloat16)
        for pair in range(2):
            start = pl.multiple_of(jnp.bitwise_xor(place, 2 * step + pair) * block, block)
            own_ref[pl.ds(start, block), :] = own[pair * block : (pair + 1) * block]
            send_ref[pl.ds(start, block), :] = send[pair * block : (pair + 1) * block]


def project(line, across, cores, parts, lows, length, after):
    depth, width = line[0].shape[1], parts[0].shape[1]
    vmem = pl.BlockSpec(memory_space=pltpu.VMEM)
    return pl.pallas_call(
        functools.partial(project_kernel, lows=lows, after=len(after)),
        out_shape=(
            jax.ShapeDtypeStruct((length, width // 2), jnp.float32),
            jax.ShapeDtypeStruct((length, width // 2), jnp.bfloat16),
        ),
        in_specs=[vmem] * 13
        + [pl.BlockSpec(memory_space=pl.ANY)] * len(after),
        out_specs=(vmem, vmem),
        scratch_shapes=[pltpu.VMEM((4 * depth, width), jnp.bfloat16)],
        compiler_params=pltpu.CompilerParams(vmem_limit_bytes=12 * 2**20),
        cost_estimate=pl.CostEstimate(
            flops=2 * length * 4 * depth * 2 * width,
            bytes_accessed=2 * length * 4 * depth,
            transcendentals=0,
        ),
        name="project",
    )(*line, *across, *cores, *parts, *after)


def smooth_into(padded, own_ref, recv_ref, taps, branch, store):
    length = own_ref.shape[0]
    tap_count = taps.shape[1]
    block = length // 8
    padded[0:8, :] = jnp.zeros((8, padded.shape[1]), jnp.float32)
    for i in range(8):
        rows = slice(i * block, (i + 1) * block)
        padded[8 + i * block : 8 + (i + 1) * block, :] = own_ref[rows, :] + recv_ref[
            rows, :
        ].astype(jnp.float32)
    for i in range(8):
        total = None
        for tap in range(tap_count):
            start = 8 + i * block - tap
            term = taps[branch, tap : tap + 1, :] * padded[start : start + block, :]
            total = term if total is None else total + term
        store(slice(i * block, (i + 1) * block), total)


def ahead_into(signal, table, waves):
    padded_rows, used = table.shape[0] // 2, table.shape[1]
    two = 2 * inner_len
    for n in range(0, inner_len, 2):
        both = jnp.concatenate(
            [signal[pl.ds(n + i, used, stride=inner_len), :] for i in range(2)], 1
        ).astype(jnp.bfloat16)
        wave = jnp.dot(table[...], both, preferred_element_type=jnp.float32)
        width = wave.shape[1] // 2
        for i in range(2):
            part = wave[:, i * width : (i + 1) * width]
            for half in range(2):
                at = pl.ds(half * inner_len + n + i, padded_rows, stride=two)
                waves[at, :] = part[half * padded_rows : (half + 1) * padded_rows]


def unroll_of(rows):
    return 11 if rows % 11 == 0 else 1


def spectrum_kernel(ahead, middle, *refs, lows):
    filters = refs[:4]
    freq_ref, lags, waves = refs[len(refs) - 3 :]
    place = lax.axis_index("seq")
    length, width = lags.shape
    block = length // 8
    rows, two = middle.shape[:2]
    for i in range(4):
        at = slice(lows[i], lows[i] + block)
        for pair in range(2):
            start = pl.multiple_of(jnp.bitwise_xor(place, 2 * i + pair) * block, block)
            piece = filters[i][at, pair * width : (pair + 1) * width]
            lags[pl.ds(start, block), :] = piece.astype(jnp.float32)
    ahead_into(lags, ahead, waves)

    def one(k, _):
        at = pl.ds(pl.multiple_of(k * two, two), two)
        wave = waves[at, :].astype(jnp.bfloat16)
        freq_ref[at, :] = jnp.dot(middle[k], wave, preferred_element_type=jnp.float32)
        return 0

    lax.fori_loop(0, rows, one, 0, unroll=unroll_of(rows))


def spectrum(tables, filters, lows, length, after):
    ahead, middle = tables[:2]
    rows, two = middle.shape[:2]
    width = filters[0].shape[1] // 2
    vmem = pl.BlockSpec(memory_space=pltpu.VMEM)
    return pl.pallas_call(
        functools.partial(spectrum_kernel, lows=lows),
        out_shape=jax.ShapeDtypeStruct((rows * two, width), jnp.float32),
        in_specs=[vmem] * 6
        + [pl.BlockSpec(memory_space=pl.ANY)] * len(after),
        out_specs=vmem,
        scratch_shapes=[
            pltpu.VMEM((length, width), jnp.float32),
            pltpu.VMEM((ahead.shape[0] // 2 * two, width), jnp.float32),
        ],
        compiler_params=pltpu.CompilerParams(vmem_limit_bytes=8 * 2**20),
        cost_estimate=pl.CostEstimate(
            flops=2 * 2 * length * inner_len * width, bytes_accessed=2**20, transcendentals=0
        ),
        name="spectrum",
    )(ahead, middle, *filters, *after)


def mix_kernel(
    own1,
    recv1,
    own2,
    recv2,
    taps_ref,
    skip_ref,
    ahead,
    middle,
    middle_back,
    back,
    freq_ref,
    weight,
    *refs,
    after,
):
    mixed_ref, held_ref, padded, gated, waves, sums, sem = refs[after:]
    loading = pltpu.make_async_copy(weight, held_ref, sem)
    loading.start()
    place = lax.axis_index("seq")
    width = own1.shape[1]
    ours = pl.ds(pl.multiple_of(place * width, width), width)
    taps, skip = taps_ref[:, :, ours], skip_ref[:, ours]
    rows, two = middle.shape[0], middle.shape[1]
    padded_rows = ahead.shape[0] // 2
    used = ahead.shape[1]

    def first(at, value):
        gated[at, :] = value

    def second(at, value):
        gated[at, :] = gated[at, :] * value

    smooth_into(padded, own1, recv1, taps, 1, first)
    smooth_into(padded, own2, recv2, taps, 2, second)
    ahead_into(gated, ahead, waves)
    if padded_rows > rows:
        sums[rows * two :, :] = jnp.zeros(((padded_rows - rows) * two, width), jnp.float32)

    def one(k, _):
        at = pl.ds(pl.multiple_of(k * two, two), two)
        wave = waves[at, :].astype(jnp.bfloat16)
        data = jnp.dot(middle[k], wave, preferred_element_type=jnp.float32)
        filters = freq_ref[at, :]
        data_real, filter_real = data[:inner_len], filters[:inner_len]
        data_imag, filter_imag = data[inner_len:], filters[inner_len:]
        product = jnp.concatenate(
            [
                data_real * filter_real - data_imag * filter_imag,
                data_real * filter_imag + data_imag * filter_real,
            ],
            0,
        ).astype(jnp.bfloat16)
        sums[at, :] = jnp.dot(middle_back[k], product, preferred_element_type=jnp.float32)
        return 0

    lax.fori_loop(0, rows, one, 0, unroll=unroll_of(rows))
    for n in range(0, inner_len, 2):
        pieces = [
            jnp.concatenate(
                [
                    sums[pl.ds(n + i, padded_rows, stride=two), :],
                    sums[pl.ds(inner_len + n + i, padded_rows, stride=two), :],
                ],
                0,
            )
            for i in range(2)
        ]
        wave = jnp.dot(
            back[...],
            jnp.concatenate(pieces, 1).astype(jnp.bfloat16),
            preferred_element_type=jnp.float32,
        )
        for i in range(2):
            at = pl.ds(n + i, used, stride=inner_len)
            mixed_ref[at, :] = wave[:, i * width : (i + 1) * width] + skip * gated[at, :]
    loading.wait()


def mix(own1, recv1, own2, recv2, taps, skip, tables, freq, weight, after):
    length, width = own1.shape
    two = tables[1].shape[1]
    padded_rows = tables[0].shape[0] // 2
    vmem = pl.BlockSpec(memory_space=pltpu.VMEM)
    return pl.pallas_call(
        functools.partial(mix_kernel, after=len(after)),
        out_shape=(
            jax.ShapeDtypeStruct((length, width), jnp.float32),
            jax.ShapeDtypeStruct(weight.shape, weight.dtype),
        ),
        in_specs=[vmem] * 11
        + [pl.BlockSpec(memory_space=pl.ANY)] * (1 + len(after)),
        out_specs=(vmem, vmem),
        scratch_shapes=[
            pltpu.VMEM((length + 8, width), jnp.float32),
            pltpu.VMEM((length, width), jnp.float32),
            pltpu.VMEM((padded_rows * two, width), jnp.float32),
            pltpu.VMEM((padded_rows * two, width), jnp.float32),
            pltpu.SemaphoreType.DMA,
        ],
        compiler_params=pltpu.CompilerParams(vmem_limit_bytes=16 * 2**20),
        cost_estimate=pl.CostEstimate(
            flops=2 * 6 * length * inner_len * width, bytes_accessed=6 * 2**20, transcendentals=0
        ),
        name="mix",
    )(own1, recv1, own2, recv2, taps, skip, *tables, freq, weight, *after)


def gate_kernel(own0, recv0, mixed_ref, taps_ref, *refs):
    outs, padded, product = refs[:8], refs[8], refs[9]
    place = lax.axis_index("seq")
    block, width = own0.shape[0] // 8, own0.shape[1]
    taps = taps_ref[:, :, pl.ds(pl.multiple_of(place * width, width), width)]

    def store(at, value):
        product[at, :] = (mixed_ref[at, :] * value).astype(jnp.bfloat16)

    smooth_into(padded, own0, recv0, taps, 0, store)
    for i in range(8):
        start = pl.multiple_of(jnp.bitwise_xor(place, i) * block, block)
        outs[i][...] = product[pl.ds(start, block), :]


def gate(own0, recv0, mixed, taps):
    length, width = own0.shape
    vmem = pl.BlockSpec(memory_space=pltpu.VMEM)
    return pl.pallas_call(
        gate_kernel,
        out_shape=(jax.ShapeDtypeStruct((length // 8, width), jnp.bfloat16),) * 8,
        in_specs=[vmem] * 4,
        out_specs=(vmem,) * 8,
        scratch_shapes=[
            pltpu.VMEM((length + 8, width), jnp.float32),
            pltpu.VMEM((length, width), jnp.bfloat16),
        ],
        compiler_params=pltpu.CompilerParams(vmem_limit_bytes=8 * 2**20),
        cost_estimate=pl.CostEstimate(
            flops=8 * length * width, bytes_accessed=12 * length * width, transcendentals=0
        ),
        name="gate",
    )(own0, recv0, mixed, taps)


def emit_kernel(weight, *refs, order, turn, added):
    parts, extra = refs[: len(order)], refs[len(order) : len(order) + added]
    out_ref = refs[len(order) + added]
    place, chan = lax.axis_index("seq"), lax.axis_index("chan")
    columns = out_ref.shape[1]
    tile = 256
    if len(order) == 1:
        joined = parts[0]
    else:
        joined = refs[-1]
        width = parts[0].shape[1]
        for part, source in zip(parts, order, strict=True):
            start = pl.multiple_of(jnp.bitwise_xor(place, source) * width, width)
            joined[:, pl.ds(start, width)] = part[...]
    for low in range(0, columns, tile):
        start = pl.multiple_of(jnp.bitwise_xor(chan, turn) * columns + low, tile)
        total = jnp.dot(
            joined[...], weight[:, pl.ds(start, tile)], preferred_element_type=jnp.float32
        )
        for term in extra:
            total = total + term[:, low : low + tile].astype(jnp.float32)
        out_ref[:, low : low + tile] = total.astype(out_ref.dtype)


def emit(parts, order, weight, turn, extra, out_dtype):
    rows = parts[0].shape[0]
    depth, columns = weight.shape[0], weight.shape[1] // 4
    vmem = pl.BlockSpec(memory_space=pltpu.VMEM)
    shapes = [jax.ShapeDtypeStruct((rows, columns), out_dtype)]
    if len(order) > 1:
        shapes.append(jax.ShapeDtypeStruct((rows, depth), parts[0].dtype))
    return pl.pallas_call(
        functools.partial(emit_kernel, order=order, turn=turn, added=len(extra)),
        out_shape=tuple(shapes),
        in_specs=[vmem] * (1 + len(parts) + len(extra)),
        out_specs=(vmem,) * len(shapes),
        compiler_params=pltpu.CompilerParams(vmem_limit_bytes=8 * 2**20),
        cost_estimate=pl.CostEstimate(
            flops=2 * rows * depth * columns,
            bytes_accessed=2 * depth * columns,
            transcendentals=0,
        ),
        name="emit",
    )(weight, *parts, *extra)


def swap(value, axis, count, turn):
    return lax.ppermute(value, axis, [(i, i ^ turn) for i in range(count)])


def fast_body(tokens, in_weight, short_taps, skip_gain, long_filter, out_weight):
    seq, chans = lax.axis_size("seq"), lax.axis_size("chan")
    rows, width = tokens.shape
    length = rows * seq
    part = width // seq

    weight = jnp.transpose(in_weight, (1, 0, 2))

    lags = tokens.shape[0]
    rows = in_weight.shape[0]

    theirs, cut1_2, cut_1 = halve(
        tokens, long_filter, weight, [(2, (1,)), (1, (1, 2))]
    )
    ours = own_half(tokens, [theirs])
    beside = swap(theirs, "seq", seq, 1)
    w1_2, w_1 = swap(cut1_2, "seq", seq, 4), swap(cut_1, "seq", seq, 2)
    whole = [(0, 0, lags), (1, 0, lags)]
    (pair,) = join([ours, beside], [whole], [w1_2])
    far = swap(pair, "seq", seq, 4)
    near = swap(pair, "seq", seq, 2)
    pair_across = swap(pair, "chan", chans, 2)
    inputs = (weight, long_filter, beside)
    plan = [(0, (1, 2, 0, "f")), (3, (1, 2, "f"))]
    plan += [(2, (0, "f")), (3, (0,)), (1, (0, "f")), (2, (2,))]
    w_0, cut_3, cut0_2, cut0_3, cut0_1, cut2_2 = cut(*inputs, plan, [pair])
    (far_and_near,) = join(
        [far, near],
        [[(0, 0, 2 * lags), (1, 0, 2 * lags)]],
        [pair_across, cut_3, w_1],
    )
    w_3 = swap(cut_3, "seq", seq, 6)
    w2_2 = swap(cut2_2, "seq", seq, 4)
    far_near = swap(far, "seq", seq, 2)
    across = swap(far_and_near, "chan", chans, 2)
    every = [(0, 0, 2 * lags), (1, 0, 2 * lags)]
    (first,) = join(
        [pair, pair_across, near, across],
        [every + [(2, 0, 2 * lags), (3, 2 * lags, 2 * lags)]],
        [w_3, w2_2],
    )
    core_a = swap(first, "chan", chans, 1)
    far_near_across = swap(far_near, "chan", chans, 2)
    (second,) = join(
        [far, across, far_near, far_near_across],
        [every + [(2, 0, 2 * lags), (3, 0, 2 * lags)]],
        [],
    )
    core_b = swap(second, "chan", chans, 1)
    line, across = [pair, near, far, far_near], [pair_across, across, far_near_across]
    cores = [core_a, core_b]
    shared = (line, across, cores)
    own1, send1 = project(*shared, [w_0, w_1, w1_2, w_3], (0,) * 4, length, [])
    recv1 = swap(send1, "seq", seq, 1)
    w0_2, w0_3 = swap(cut0_2, "seq", seq, 4), swap(cut0_3, "seq", seq, 6)
    w0_1 = swap(cut0_1, "seq", seq, 2)
    tables = wave_tables(length)
    own2, send2 = project(*shared, [w_0, w_1, w2_2, w_3], (rows, rows, 0, rows), length, [])
    recv2 = swap(send2, "seq", seq, 1)
    freq = spectrum(
        tables, [w_0, w0_1, w0_2, w_3], (3 * rows, rows, rows, 2 * rows), length, [send2]
    )
    parts0 = [w_0, w0_1, w0_2, w0_3]
    own0, send0 = project(*shared, parts0, (2 * rows, 0, 0, 0), length, [])
    recv0 = swap(send0, "seq", seq, 1)
    mixed, held = mix(
        own1,
        recv1,
        own2,
        recv2,
        short_taps,
        skip_gain[None],
        tables,
        freq,
        out_weight,
        [send0],
    )
    pieces = gate(own0, recv0, mixed, short_taps)
    order = (6, 7, 4, 5, 2, 3, 1, 0)
    joined = [swap(pieces[turn], "seq", seq, turn) if turn else pieces[0] for turn in order]

    across_out, rows_here = emit(joined, order, held, 3, [], jnp.bfloat16)
    from_core = swap(across_out, "chan", chans, 1)
    (beside_out,) = emit([rows_here], (0,), held, 1, [], jnp.bfloat16)
    near_sum = swap(beside_out, "chan", chans, 1)
    (chip_out,) = emit([rows_here], (0,), held, 2, [from_core], jnp.bfloat16)
    from_chip = swap(chip_out, "chan", chans, 2)
    (own,) = emit([rows_here], (0,), held, 0, [near_sum], jnp.float32)
    return (own + from_chip.astype(jnp.float32)).astype(jnp.bfloat16)


def solution(mesh):
    in_specs = (
        P("seq", "chan"),
        P("seq", None, "chan"),
        P(None, None, "chan"),
        P("chan"),
        P("seq", "chan"),
        P("chan", None),
    )
    out_specs = P("seq", "chan")
    seq, chans = mesh.shape["seq"], mesh.shape["chan"]
    chosen = fast_body if seq == 8 and chans == 4 else body
    return jax.shard_map(chosen, mesh=mesh, in_specs=in_specs, out_specs=out_specs, check_vma=False)
```

```python
import functools
import math

import jax
import jax.numpy as jnp
import numpy as np
from jax import lax
from jax.experimental import pallas as pl
from jax.experimental.pallas import tpu as pltpu
from jax.sharding import PartitionSpec as P

exact_prec = lax.Precision.HIGHEST
inner_len = 64


def dft_tables(half_len, blocks):
    full_len = 2 * half_len
    full_size = full_len * blocks
    half_index = jnp.arange(half_len, dtype=jnp.int32)
    full_index = jnp.arange(full_len, dtype=jnp.int32)
    block_index = jnp.arange(blocks, dtype=jnp.int32)
    outer_angle = (half_index[:, None] * full_index[None, :] % full_len).astype(jnp.float32) * (
        2.0 * math.pi / full_len
    )
    inner_angle = (block_index[:, None] * block_index[None, :] % blocks).astype(jnp.float32) * (
        2.0 * math.pi / blocks
    )
    twist_angle = (full_index[:, None] * block_index[None, :] % full_size).astype(jnp.float32) * (
        2.0 * math.pi / full_size
    )
    return (
        jnp.cos(outer_angle),
        jnp.sin(outer_angle),
        jnp.cos(inner_angle),
        jnp.sin(inner_angle),
        jnp.cos(twist_angle),
        jnp.sin(twist_angle),
    )


def forward_dft(signal, tables):
    outer_cos, outer_sin, inner_cos, inner_sin, twist_cos, twist_sin = tables
    real_section = jnp.einsum("cmn,mk->ckn", signal, outer_cos, precision=exact_prec)
    imag_section = -jnp.einsum("cmn,mk->ckn", signal, outer_sin, precision=exact_prec)
    real_twist = real_section * twist_cos + imag_section * twist_sin
    imag_twist = imag_section * twist_cos - real_section * twist_sin
    real_freq = jnp.einsum("ckn,nj->ckj", real_twist, inner_cos, precision=exact_prec) + jnp.einsum(
        "ckn,nj->ckj", imag_twist, inner_sin, precision=exact_prec
    )
    imag_freq = jnp.einsum("ckn,nj->ckj", imag_twist, inner_cos, precision=exact_prec) - jnp.einsum(
        "ckn,nj->ckj", real_twist, inner_sin, precision=exact_prec
    )
    return (real_freq, imag_freq)


def inverse_real(spectrum_real, spectrum_imag, tables):
    outer_cos, outer_sin, inner_cos, inner_sin, twist_cos, twist_sin = tables
    full_size = outer_cos.shape[1] * inner_cos.shape[0]
    back_real = jnp.einsum(
        "ckj,jn->ckn", spectrum_real, inner_cos, precision=exact_prec
    ) - jnp.einsum("ckj,jn->ckn", spectrum_imag, inner_sin, precision=exact_prec)
    back_imag = jnp.einsum(
        "ckj,jn->ckn", spectrum_imag, inner_cos, precision=exact_prec
    ) + jnp.einsum("ckj,jn->ckn", spectrum_real, inner_sin, precision=exact_prec)
    turn_real = back_real * twist_cos - back_imag * twist_sin
    turn_imag = back_imag * twist_cos + back_real * twist_sin
    summed_real = jnp.einsum(
        "ckn,mk->cmn", turn_real, outer_cos, precision=exact_prec
    ) - jnp.einsum("ckn,mk->cmn", turn_imag, outer_sin, precision=exact_prec)
    return summed_real / full_size


def causal_conv(signal, kernel, blocks):
    channels, length = signal.shape
    half_len = length // blocks
    tables = dft_tables(half_len, blocks)
    stacked = jnp.concatenate([signal, kernel], 0).reshape(2 * channels, half_len, blocks)
    real_freq, imag_freq = forward_dft(stacked, tables)
    data_real, filter_real = (real_freq[:channels], real_freq[channels:])
    data_imag, filter_imag = (imag_freq[:channels], imag_freq[channels:])
    spectrum_real = data_real * filter_real - data_imag * filter_imag
    spectrum_imag = data_real * filter_imag + data_imag * filter_real
    return inverse_real(spectrum_real, spectrum_imag, tables).reshape(channels, length)


def body(tokens, in_weight, short_taps, skip_gain, long_filter, out_weight):
    row_count, chan_width = tokens.shape
    blocks = lax.axis_size("seq")
    part_width = chan_width // blocks
    flat_weight = in_weight.reshape(in_weight.shape[0], 3 * chan_width)
    whole = lax.all_gather(tokens, "chan", axis=1, tiled=True)
    projected = jnp.dot(
        whole,
        lax.all_gather(flat_weight, "seq", axis=0, tiled=True),
        preferred_element_type=jnp.float32,
    )
    projected = projected.astype(jnp.bfloat16).reshape(row_count, 3, chan_width)
    outgoing = jnp.transpose(projected, (1, 2, 0))
    filter_rows = jnp.transpose(long_filter)[None]
    channel_major, filter_major = (
        lax.all_to_all(outgoing, "seq", split_axis=1, concat_axis=2, tiled=True),
        lax.all_to_all(filter_rows, "seq", split_axis=1, concat_axis=2, tiled=True),
    )
    offset = lax.axis_index("seq") * part_width
    local_taps = lax.dynamic_slice_in_dim(short_taps, offset, part_width, 2)
    local_skip = lax.dynamic_slice_in_dim(skip_gain, offset, part_width, 0)
    values = channel_major.astype(jnp.float32)
    tap_count = short_taps.shape[1]
    length = values.shape[2]
    padded = jnp.pad(values, ((0, 0), (0, 0), (tap_count - 1, 0)))
    smoothed = jnp.zeros_like(values)
    for tap_index in range(tap_count):
        lag_start = tap_count - 1 - tap_index
        smoothed = (
            smoothed
            + local_taps[:, tap_index, :, None] * padded[:, :, lag_start : lag_start + length]
        )
    gate_query = smoothed[0]
    gated = smoothed[1] * smoothed[2]
    mixed_seq = (
        causal_conv(gated, filter_major[0].astype(jnp.float32), blocks)
        + local_skip[:, None] * gated
    )
    product = (mixed_seq * gate_query).astype(jnp.bfloat16)
    returned = lax.all_to_all(product, "seq", split_axis=1, concat_axis=0, tiled=True)
    summed = lax.psum_scatter(
        lax.dot_general(
            out_weight, returned, (((0,), (0,)), ((), ())), preferred_element_type=jnp.float32
        ).astype(jnp.bfloat16),
        "chan",
        scatter_dimension=0,
        tiled=True,
    ).astype(jnp.float32)
    return jnp.transpose(summed).astype(jnp.bfloat16)


def wave_tables(length):
    span = 2 * length
    outer = span // inner_len
    used, rows = outer // 2, outer // 2 + 1
    padded_rows = -(-rows // 8) * 8
    m, k = np.arange(used), np.arange(rows)
    n, j = np.arange(inner_len), np.arange(inner_len)
    angle = (2.0 * math.pi / outer) * (np.outer(k, m) % outer)
    ahead = np.zeros((2, padded_rows, used))
    ahead[0, :rows], ahead[1, :rows] = np.cos(angle), -np.sin(angle)
    weight = np.where((k == 0) | (k == used), 1.0, 2.0) / span
    back = np.zeros((used, 2, padded_rows))
    back[:, 0, :rows] = (np.cos(angle) * weight[:, None]).T
    back[:, 1, :rows] = (-np.sin(angle) * weight[:, None]).T
    turn = n[None, None, :] * (k[:, None, None] + outer * j[None, :, None]) % span
    cos, sin = np.cos(turn * (2.0 * math.pi / span)), np.sin(turn * (2.0 * math.pi / span))
    middle = np.concatenate(
        [np.concatenate([cos, sin], 2), np.concatenate([-sin, cos], 2)], 1
    )
    return tuple(
        jnp.asarray(table, jnp.bfloat16)
        for table in (
            ahead.reshape(2 * padded_rows, used),
            middle,
            np.swapaxes(middle, 1, 2),
            back.reshape(used, 2 * padded_rows),
        )
    )


def halve_kernel(tokens, filters, weight, theirs, *refs, plan):
    pieces, sems = refs[:-1], refs[-1]
    place = lax.axis_index("seq")
    depth, side = place // 2, place % 2
    rows, half = tokens.shape[0], theirs.shape[1]
    part = half // 4
    copies = []

    def copy(source, block, width, target):
        columns = pl.ds(pl.multiple_of(block * width, width), width)
        copies.append(
            pltpu.make_async_copy(source.at[:, columns], target, sems.at[len(copies)])
        )

    copy(tokens, 1 - side, half, theirs.at[pl.ds(0, rows), :])
    for i in range(4):
        target = theirs.at[pl.ds(rows, filters.shape[0]), pl.ds(i * part, part)]
        copy(filters, 2 * i + 1 - side, part, target)
    depth_rows = weight.shape[1]
    for piece, (turn, names) in zip(pieces, plan, strict=True):
        for i, name in enumerate(names):
            target = piece.at[pl.ds(i * depth_rows, depth_rows), :]
            copy(weight.at[name], jnp.bitwise_xor(depth, turn), piece.shape[1], target)
    for one in copies:
        one.start()
    for one in copies:
        one.wait()


def halve(tokens, filters, weight, plan):
    rows, half = tokens.shape[0], tokens.shape[1] // 2
    pieces = tuple(
        jax.ShapeDtypeStruct((len(names) * weight.shape[1], weight.shape[2] // 4), weight.dtype)
        for _, names in plan
    )
    vmem = pl.BlockSpec(memory_space=pltpu.VMEM)
    return pl.pallas_call(
        functools.partial(halve_kernel, plan=plan),
        out_shape=(
            jax.ShapeDtypeStruct((rows + filters.shape[0], half), tokens.dtype),
        )
        + pieces,
        in_specs=[pl.BlockSpec(memory_space=pl.ANY)] * 3,
        out_specs=(vmem,) * (1 + len(plan)),
        scratch_shapes=[
            pltpu.SemaphoreType.DMA((5 + sum(len(names) for _, names in plan),))
        ],
        compiler_params=pltpu.CompilerParams(vmem_limit_bytes=60 * 2**20),
        name="halve",
    )(tokens, filters, weight)


def own_half_kernel(tokens, ours, sem):
    half = ours.shape[1]
    start = pl.multiple_of(lax.axis_index("seq") % 2 * half, half)
    copy = pltpu.make_async_copy(tokens.at[:, pl.ds(start, half)], ours, sem)
    copy.start()
    copy.wait()


def own_half(tokens, after):
    rows, half = tokens.shape[0], tokens.shape[1] // 2
    return pl.pallas_call(
        lambda *refs: own_half_kernel(refs[0], refs[-2], refs[-1]),
        out_shape=jax.ShapeDtypeStruct((rows, half), tokens.dtype),
        in_specs=[pl.BlockSpec(memory_space=pl.ANY)] * (1 + len(after)),
        out_specs=pl.BlockSpec(memory_space=pltpu.VMEM),
        scratch_shapes=[pltpu.SemaphoreType.DMA],
        compiler_params=pltpu.CompilerParams(vmem_limit_bytes=8 * 2**20),
        name="own_half",
    )(tokens, *after)


def cut_kernel(weight, filters, filter_beside, *refs, plan, after):
    place = lax.axis_index("seq")
    depth, side = place // 2, place % 2
    outs, sems = refs[after:-1], refs[-1]
    copies = []

    def copy(source, target):
        copies.append(pltpu.make_async_copy(source, target, sems.at[len(copies)]))

    def columns_of(block, width):
        return pl.ds(pl.multiple_of(block * width, width), width)

    rows, width = weight.shape[1], outs[0].shape[1]
    half = width // 2
    for out, (turn, names) in zip(outs, plan, strict=True):
        block = jnp.bitwise_xor(depth, turn)
        low = 0
        for name in names:
            if name == "f":
                at = pl.ds(low, filters.shape[0])
                here = columns_of(2 * block + side, half)
                copy(filters.at[:, here], out.at[at, pl.ds(0, half)])
                there = columns_of(block, half)
                below = pl.ds(filter_beside.shape[0] - filters.shape[0], filters.shape[0])
                copy(filter_beside.at[below, there], out.at[at, pl.ds(half, half)])
                low += filters.shape[0]
            else:
                source = weight.at[name, :, columns_of(block, width)]
                copy(source, out.at[pl.ds(low, rows), :])
                low += rows
    for one in copies:
        one.start()
    for one in copies:
        one.wait()


def cut(weight, filters, filter_beside, plan, after):
    count_of = {"f": filters.shape[0]}
    shapes = []
    for _, names in plan:
        rows = sum(count_of.get(name, weight.shape[1]) for name in names)
        shapes.append(jax.ShapeDtypeStruct((rows, weight.shape[2] // 4), weight.dtype))
    return pl.pallas_call(
        functools.partial(cut_kernel, plan=plan, after=len(after)),
        out_shape=tuple(shapes),
        in_specs=[pl.BlockSpec(memory_space=pl.ANY)] * (3 + len(after)),
        out_specs=(pl.BlockSpec(memory_space=pltpu.VMEM),) * len(shapes),
        scratch_shapes=[pltpu.SemaphoreType.DMA((24,))],
        compiler_params=pltpu.CompilerParams(vmem_limit_bytes=8 * 2**20),
        name="cut",
    )(weight, filters, filter_beside, *after)


def join_kernel(*refs, pieces, outs):
    for out_ref, group in zip(refs[len(refs) - outs :], pieces, strict=True):
        start = 0
        for at, low, count in group:
            out_ref[start : start + count, :] = refs[at][low : low + count, :]
            start += count


def join(values, pieces, after):
    shapes = []
    for group in pieces:
        rows = sum(count for _, _, count in group)
        shapes.append(jax.ShapeDtypeStruct((rows, values[0].shape[1]), values[0].dtype))
    vmem = pl.BlockSpec(memory_space=pltpu.VMEM)
    return pl.pallas_call(
        functools.partial(join_kernel, pieces=pieces, outs=len(pieces)),
        out_shape=tuple(shapes),
        in_specs=[vmem] * len(values) + [pl.BlockSpec(memory_space=pl.ANY)] * len(after),
        out_specs=(vmem,) * len(shapes),
        compiler_params=pltpu.CompilerParams(vmem_limit_bytes=8 * 2**20),
        name="join",
    )(*values, *after)


def project_kernel(*refs, lows, after):
    line, across, cores, parts = refs[:4], refs[4:7], refs[7:9], refs[9:13]
    own_ref, send_ref, weights = refs[13 + after :]
    place, chan = lax.axis_index("seq"), lax.axis_index("chan")
    depth, side = place // 2, place % 2
    rows = line[0].shape[1]
    for i in range(4):
        slot = jnp.bitwise_xor(depth, jnp.bitwise_xor(chan, i))
        start = pl.multiple_of(slot * rows, rows)
        weights[pl.ds(start, rows), :] = parts[i][lows[i] : lows[i] + rows, :]
    length, half = own_ref.shape
    block = length // 8
    for step in range(4):
        low = 4 * block * (step % 2)
        both = cores[step // 2]
        beside = across[(0, 1, 1, 2)[step]]
        at = 2 * block if step == 1 else 0
        joined = jnp.concatenate(
            [
                line[step][...],
                both[low : low + 2 * block, :],
                beside[at : at + 2 * block, :],
                both[low + 2 * block : low + 4 * block, :],
            ],
            1,
        )
        total = jnp.dot(joined, weights[...], preferred_element_type=jnp.float32)
        left, right = total[:, :half], total[:, half:]
        own = jnp.where(side == 0, left, right)
        send = jnp.where(side == 0, right, left).astype(jnp.bfloat16)
        for pair in range(2):
            start = pl.multiple_of(jnp.bitwise_xor(place, 2 * step + pair) * block, block)
            own_ref[pl.ds(start, block), :] = own[pair * block : (pair + 1) * block]
            send_ref[pl.ds(start, block), :] = send[pair * block : (pair + 1) * block]


def project(line, across, cores, parts, lows, length, after):
    depth, width = line[0].shape[1], parts[0].shape[1]
    vmem = pl.BlockSpec(memory_space=pltpu.VMEM)
    return pl.pallas_call(
        functools.partial(project_kernel, lows=lows, after=len(after)),
        out_shape=(
            jax.ShapeDtypeStruct((length, width // 2), jnp.float32),
            jax.ShapeDtypeStruct((length, width // 2), jnp.bfloat16),
        ),
        in_specs=[vmem] * 13
        + [pl.BlockSpec(memory_space=pl.ANY)] * len(after),
        out_specs=(vmem, vmem),
        scratch_shapes=[pltpu.VMEM((4 * depth, width), jnp.bfloat16)],
        compiler_params=pltpu.CompilerParams(vmem_limit_bytes=12 * 2**20),
        cost_estimate=pl.CostEstimate(
            flops=2 * length * 4 * depth * 2 * width,
            bytes_accessed=2 * length * 4 * depth,
            transcendentals=0,
        ),
        name="project",
    )(*line, *across, *cores, *parts, *after)


def project_part_kernel(*refs, lows, far):
    line, across, cores, parts = refs[:4], refs[4:7], refs[7:9], refs[9:11]
    weights = refs[-1]
    place, chan = lax.axis_index("seq"), lax.axis_index("chan")
    depth, side = place // 2, place % 2
    rows = line[0].shape[1]
    turned = jnp.bitwise_xor(depth, chan)
    for i in range(2):
        slot = jnp.bitwise_xor(turned % 2, i)
        start = pl.multiple_of(slot * rows, rows)
        weights[pl.ds(start, rows), :] = parts[i][lows[i] : lows[i] + rows, :]
    block = line[0].shape[0] // 2
    half = weights.shape[1] // 2

    def run(second):
        for step in range(4):
            low = 4 * block * (step % 2)
            both = cores[step // 2]
            if second:
                beside = across[(0, 1, 1, 2)[step]]
                at = 2 * block if step == 1 else 0
                first = beside[at : at + 2 * block, :]
                low += 2 * block
            else:
                first = line[step][...]
            joined = jnp.concatenate([first, both[low : low + 2 * block, :]], 1)
            total = jnp.dot(joined, weights[...], preferred_element_type=jnp.float32)
            rows_here = slice(2 * step * block, 2 * (step + 1) * block)
            if not far:
                refs[11][rows_here, :] = total
                continue
            total = total + refs[11][rows_here, :]
            left, right = total[:, :half], total[:, half:]
            own = jnp.where(side == 0, left, right)
            send = jnp.where(side == 0, right, left).astype(jnp.bfloat16)
            for pair in range(2):
                start = pl.multiple_of(jnp.bitwise_xor(place, 2 * step + pair) * block, block)
                refs[12][pl.ds(start, block), :] = own[pair * block : (pair + 1) * block]
                refs[13][pl.ds(start, block), :] = send[pair * block : (pair + 1) * block]

    pair_of = turned // 2
    pl.when(pair_of == (1 if far else 0))(lambda: run(False))
    pl.when(pair_of == (0 if far else 1))(lambda: run(True))


def project_part(line, across, cores, parts, lows, length, begun):
    depth, width = line[0].shape[1], parts[0].shape[1]
    vmem = pl.BlockSpec(memory_space=pltpu.VMEM)
    shapes = (jax.ShapeDtypeStruct((length, width), jnp.float32),)
    if begun:
        shapes = (
            jax.ShapeDtypeStruct((length, width // 2), jnp.float32),
            jax.ShapeDtypeStruct((length, width // 2), jnp.bfloat16),
        )
    return pl.pallas_call(
        functools.partial(project_part_kernel, lows=lows, far=len(begun) > 0),
        out_shape=shapes,
        in_specs=[vmem] * (11 + len(begun)),
        out_specs=(vmem,) * len(shapes),
        scratch_shapes=[pltpu.VMEM((2 * depth, width), jnp.bfloat16)],
        compiler_params=pltpu.CompilerParams(vmem_limit_bytes=12 * 2**20),
        cost_estimate=pl.CostEstimate(
            flops=2 * length * 2 * depth * width,
            bytes_accessed=2 * length * 2 * depth,
            transcendentals=0,
        ),
        name="project_part",
    )(*line, *across, *cores, *parts, *begun)


def smooth_into(padded, own_ref, recv_ref, taps, branch, store):
    length = own_ref.shape[0]
    tap_count = taps.shape[1]
    block = length // 8
    padded[0:8, :] = jnp.zeros((8, padded.shape[1]), jnp.float32)
    for i in range(8):
        rows = slice(i * block, (i + 1) * block)
        padded[8 + i * block : 8 + (i + 1) * block, :] = own_ref[rows, :] + recv_ref[
            rows, :
        ].astype(jnp.float32)
    for i in range(8):
        total = None
        for tap in range(tap_count):
            start = 8 + i * block - tap
            term = taps[branch, tap : tap + 1, :] * padded[start : start + block, :]
            total = term if total is None else total + term
        store(slice(i * block, (i + 1) * block), total)


def ahead_into(signal, table, waves):
    padded_rows, used = table.shape[0] // 2, table.shape[1]
    two = 2 * inner_len
    for n in range(0, inner_len, 2):
        both = jnp.concatenate(
            [signal[pl.ds(n + i, used, stride=inner_len), :] for i in range(2)], 1
        ).astype(jnp.bfloat16)
        wave = jnp.dot(table[...], both, preferred_element_type=jnp.float32)
        width = wave.shape[1] // 2
        for i in range(2):
            part = wave[:, i * width : (i + 1) * width]
            for half in range(2):
                at = pl.ds(half * inner_len + n + i, padded_rows, stride=two)
                waves[at, :] = part[half * padded_rows : (half + 1) * padded_rows]


def unroll_of(rows):
    return rows


def spectrum_kernel(ahead, middle, *refs, lows):
    filters = refs[:4]
    freq_ref, lags, waves = refs[len(refs) - 3 :]
    place = lax.axis_index("seq")
    length, width = lags.shape
    block = length // 8
    rows, two = middle.shape[:2]
    for i in range(4):
        at = slice(lows[i], lows[i] + block)
        for pair in range(2):
            start = pl.multiple_of(jnp.bitwise_xor(place, 2 * i + pair) * block, block)
            piece = filters[i][at, pair * width : (pair + 1) * width]
            lags[pl.ds(start, block), :] = piece.astype(jnp.float32)
    ahead_into(lags, ahead, waves)

    def one(k, _):
        at = pl.ds(pl.multiple_of(k * two, two), two)
        wave = waves[at, :].astype(jnp.bfloat16)
        freq_ref[at, :] = jnp.dot(middle[k], wave, preferred_element_type=jnp.float32)
        return 0

    lax.fori_loop(0, rows, one, 0, unroll=unroll_of(rows))


def spectrum(tables, filters, lows, length, after):
    ahead, middle = tables[:2]
    rows, two = middle.shape[:2]
    width = filters[0].shape[1] // 2
    vmem = pl.BlockSpec(memory_space=pltpu.VMEM)
    return pl.pallas_call(
        functools.partial(spectrum_kernel, lows=lows),
        out_shape=jax.ShapeDtypeStruct((rows * two, width), jnp.float32),
        in_specs=[vmem] * 6
        + [pl.BlockSpec(memory_space=pl.ANY)] * len(after),
        out_specs=vmem,
        scratch_shapes=[
            pltpu.VMEM((length, width), jnp.float32),
            pltpu.VMEM((ahead.shape[0] // 2 * two, width), jnp.float32),
        ],
        compiler_params=pltpu.CompilerParams(vmem_limit_bytes=8 * 2**20),
        cost_estimate=pl.CostEstimate(
            flops=2 * 2 * length * inner_len * width, bytes_accessed=2**20, transcendentals=0
        ),
        name="spectrum",
    )(ahead, middle, *filters, *after)


def mix_kernel(
    own1,
    recv1,
    own2,
    recv2,
    taps_ref,
    skip_ref,
    ahead,
    middle,
    middle_back,
    back,
    freq_ref,
    weight,
    *refs,
    after,
):
    mixed_ref, held_ref, padded, gated, waves, sums, sem = refs[after:]
    loading = pltpu.make_async_copy(weight, held_ref, sem)
    loading.start()
    place = lax.axis_index("seq")
    width = own1.shape[1]
    ours = pl.ds(pl.multiple_of(place * width, width), width)
    taps, skip = taps_ref[:, :, ours], skip_ref[:, ours]
    rows, two = middle.shape[0], middle.shape[1]
    padded_rows = ahead.shape[0] // 2
    used = ahead.shape[1]

    def first(at, value):
        gated[at, :] = value

    def second(at, value):
        gated[at, :] = gated[at, :] * value

    smooth_into(padded, own1, recv1, taps, 1, first)
    smooth_into(padded, own2, recv2, taps, 2, second)
    ahead_into(gated, ahead, waves)
    if padded_rows > rows:
        sums[rows * two :, :] = jnp.zeros(((padded_rows - rows) * two, width), jnp.float32)

    def one(k, _):
        at = pl.ds(pl.multiple_of(k * two, two), two)
        wave = waves[at, :].astype(jnp.bfloat16)
        data = jnp.dot(middle[k], wave, preferred_element_type=jnp.float32)
        filters = freq_ref[at, :]
        data_real, filter_real = data[:inner_len], filters[:inner_len]
        data_imag, filter_imag = data[inner_len:], filters[inner_len:]
        product = jnp.concatenate(
            [
                data_real * filter_real - data_imag * filter_imag,
                data_real * filter_imag + data_imag * filter_real,
            ],
            0,
        ).astype(jnp.bfloat16)
        sums[at, :] = jnp.dot(middle_back[k], product, preferred_element_type=jnp.float32)
        return 0

    lax.fori_loop(0, rows, one, 0, unroll=unroll_of(rows))
    for n in range(0, inner_len, 2):
        pieces = [
            jnp.concatenate(
                [
                    sums[pl.ds(n + i, padded_rows, stride=two), :],
                    sums[pl.ds(inner_len + n + i, padded_rows, stride=two), :],
                ],
                0,
            )
            for i in range(2)
        ]
        wave = jnp.dot(
            back[...],
            jnp.concatenate(pieces, 1).astype(jnp.bfloat16),
            preferred_element_type=jnp.float32,
        )
        for i in range(2):
            at = pl.ds(n + i, used, stride=inner_len)
            mixed_ref[at, :] = wave[:, i * width : (i + 1) * width] + skip * gated[at, :]
    loading.wait()


def mix(own1, recv1, own2, recv2, taps, skip, tables, freq, weight, after):
    length, width = own1.shape
    two = tables[1].shape[1]
    padded_rows = tables[0].shape[0] // 2
    vmem = pl.BlockSpec(memory_space=pltpu.VMEM)
    return pl.pallas_call(
        functools.partial(mix_kernel, after=len(after)),
        out_shape=(
            jax.ShapeDtypeStruct((length, width), jnp.float32),
            jax.ShapeDtypeStruct(weight.shape, weight.dtype),
        ),
        in_specs=[vmem] * 11
        + [pl.BlockSpec(memory_space=pl.ANY)] * (1 + len(after)),
        out_specs=(vmem, vmem),
        scratch_shapes=[
            pltpu.VMEM((length + 8, width), jnp.float32),
            pltpu.VMEM((length, width), jnp.float32),
            pltpu.VMEM((padded_rows * two, width), jnp.float32),
            pltpu.VMEM((padded_rows * two, width), jnp.float32),
            pltpu.SemaphoreType.DMA,
        ],
        compiler_params=pltpu.CompilerParams(vmem_limit_bytes=16 * 2**20),
        cost_estimate=pl.CostEstimate(
            flops=2 * 6 * length * inner_len * width, bytes_accessed=6 * 2**20, transcendentals=0
        ),
        name="mix",
    )(own1, recv1, own2, recv2, taps, skip, *tables, freq, weight, *after)


def gate_kernel(own0, recv0, mixed_ref, taps_ref, *refs):
    outs, padded, product = refs[:8], refs[8], refs[9]
    place = lax.axis_index("seq")
    block, width = own0.shape[0] // 8, own0.shape[1]
    taps = taps_ref[:, :, pl.ds(pl.multiple_of(place * width, width), width)]

    def store(at, value):
        product[at, :] = (mixed_ref[at, :] * value).astype(jnp.bfloat16)

    smooth_into(padded, own0, recv0, taps, 0, store)
    for i in range(8):
        start = pl.multiple_of(jnp.bitwise_xor(place, i) * block, block)
        outs[i][...] = product[pl.ds(start, block), :]


def gate(own0, recv0, mixed, taps):
    length, width = own0.shape
    vmem = pl.BlockSpec(memory_space=pltpu.VMEM)
    return pl.pallas_call(
        gate_kernel,
        out_shape=(jax.ShapeDtypeStruct((length // 8, width), jnp.bfloat16),) * 8,
        in_specs=[vmem] * 4,
        out_specs=(vmem,) * 8,
        scratch_shapes=[
            pltpu.VMEM((length + 8, width), jnp.float32),
            pltpu.VMEM((length, width), jnp.bfloat16),
        ],
        compiler_params=pltpu.CompilerParams(vmem_limit_bytes=8 * 2**20),
        cost_estimate=pl.CostEstimate(
            flops=8 * length * width, bytes_accessed=12 * length * width, transcendentals=0
        ),
        name="gate",
    )(own0, recv0, mixed, taps)


def emit_kernel(weight, *refs, order, turn, added):
    parts, extra = refs[: len(order)], refs[len(order) : len(order) + added]
    out_ref = refs[len(order) + added]
    place, chan = lax.axis_index("seq"), lax.axis_index("chan")
    columns = out_ref.shape[1]
    tile = columns // 2
    if len(order) == 1:
        joined = parts[0]
    else:
        joined = refs[-1]
        width = parts[0].shape[1]
        for part, source in zip(parts, order, strict=True):
            start = pl.multiple_of(jnp.bitwise_xor(place, source) * width, width)
            joined[:, pl.ds(start, width)] = part[...]
    for low in range(0, columns, tile):
        start = pl.multiple_of(jnp.bitwise_xor(chan, turn) * columns + low, tile)
        total = jnp.dot(
            joined[...], weight[:, pl.ds(start, tile)], preferred_element_type=jnp.float32
        )
        for term in extra:
            total = total + term[:, low : low + tile].astype(jnp.float32)
        out_ref[:, low : low + tile] = total.astype(out_ref.dtype)


def emit(parts, order, weight, turn, extra, out_dtype):
    rows = parts[0].shape[0]
    depth, columns = weight.shape[0], weight.shape[1] // 4
    vmem = pl.BlockSpec(memory_space=pltpu.VMEM)
    shapes = [jax.ShapeDtypeStruct((rows, columns), out_dtype)]
    if len(order) > 1:
        shapes.append(jax.ShapeDtypeStruct((rows, depth), parts[0].dtype))
    return pl.pallas_call(
        functools.partial(emit_kernel, order=order, turn=turn, added=len(extra)),
        out_shape=tuple(shapes),
        in_specs=[vmem] * (1 + len(parts) + len(extra)),
        out_specs=(vmem,) * len(shapes),
        compiler_params=pltpu.CompilerParams(vmem_limit_bytes=8 * 2**20),
        cost_estimate=pl.CostEstimate(
            flops=2 * rows * depth * columns,
            bytes_accessed=2 * depth * columns,
            transcendentals=0,
        ),
        name="emit",
    )(weight, *parts, *extra)


def swap(value, axis, count, turn):
    return lax.ppermute(value, axis, [(i, i ^ turn) for i in range(count)])


def fast_body(tokens, in_weight, short_taps, skip_gain, long_filter, out_weight):
    seq, chans = lax.axis_size("seq"), lax.axis_size("chan")
    rows, width = tokens.shape
    length = rows * seq
    part = width // seq

    weight = jnp.transpose(in_weight, (1, 0, 2))

    lags = tokens.shape[0]
    rows = in_weight.shape[0]

    theirs, cut1_2, cut_1 = halve(
        tokens, long_filter, weight, [(2, (1,)), (1, (1, 2))]
    )
    ours = own_half(tokens, [theirs])
    beside = swap(theirs, "seq", seq, 1)
    w1_2, w_1 = swap(cut1_2, "seq", seq, 4), swap(cut_1, "seq", seq, 2)
    whole = [(0, 0, lags), (1, 0, lags)]
    (pair,) = join([ours, beside], [whole], [w1_2])
    far = swap(pair, "seq", seq, 4)
    near = swap(pair, "seq", seq, 2)
    pair_across = swap(pair, "chan", chans, 2)
    inputs = (weight, long_filter, beside)
    plan = [(0, (1, 2, 0, "f")), (3, (1, 2, "f"))]
    plan += [(2, (0, "f")), (3, (0,)), (1, (0, "f")), (2, (2,))]
    w_0, cut_3, cut0_2, cut0_3, cut0_1, cut2_2 = cut(*inputs, plan, [pair])
    (far_and_near,) = join(
        [far, near],
        [[(0, 0, 2 * lags), (1, 0, 2 * lags)]],
        [pair_across, cut_3, w_1],
    )
    w_3 = swap(cut_3, "seq", seq, 6)
    w2_2 = swap(cut2_2, "seq", seq, 4)
    far_near = swap(far, "seq", seq, 2)
    across = swap(far_and_near, "chan", chans, 2)
    every = [(0, 0, 2 * lags), (1, 0, 2 * lags)]
    (first,) = join(
        [pair, pair_across, near, across],
        [every + [(2, 0, 2 * lags), (3, 2 * lags, 2 * lags)]],
        [w_3, w2_2],
    )
    core_a = swap(first, "chan", chans, 1)
    far_near_across = swap(far_near, "chan", chans, 2)
    (second,) = join(
        [far, across, far_near, far_near_across],
        [every + [(2, 0, 2 * lags), (3, 0, 2 * lags)]],
        [],
    )
    core_b = swap(second, "chan", chans, 1)
    line, across = [pair, near, far, far_near], [pair_across, across, far_near_across]
    cores = [core_a, core_b]
    shared = (line, across, cores)
    own1, send1 = project(*shared, [w_0, w_1, w1_2, w_3], (0,) * 4, length, [])
    recv1 = swap(send1, "seq", seq, 1)
    w0_2, w0_3 = swap(cut0_2, "seq", seq, 4), swap(cut0_3, "seq", seq, 6)
    w0_1 = swap(cut0_1, "seq", seq, 2)
    tables = wave_tables(length)
    own2, send2 = project(*shared, [w_0, w_1, w2_2, w_3], (rows, rows, 0, rows), length, [])
    recv2 = swap(send2, "seq", seq, 1)
    freq = spectrum(
        tables, [w_0, w0_1, w0_2, w_3], (3 * rows, rows, rows, 2 * rows), length, [send2]
    )
    begun = project_part(*shared, [w_0, w0_1], (2 * rows, 0), length, [])
    own0, send0 = project_part(*shared, [w0_2, w0_3], (0, 0), length, begun)
    recv0 = swap(send0, "seq", seq, 1)
    mixed, held = mix(
        own1,
        recv1,
        own2,
        recv2,
        short_taps,
        skip_gain[None],
        tables,
        freq,
        out_weight,
        [send0],
    )
    pieces = gate(own0, recv0, mixed, short_taps)
    order = (6, 7, 4, 5, 2, 3, 1, 0)
    joined = [swap(pieces[turn], "seq", seq, turn) if turn else pieces[0] for turn in order]

    across_out, rows_here = emit(joined, order, held, 3, [], jnp.bfloat16)
    from_core = swap(across_out, "chan", chans, 1)
    (beside_out,) = emit([rows_here], (0,), held, 1, [], jnp.bfloat16)
    near_sum = swap(beside_out, "chan", chans, 1)
    (chip_out,) = emit([rows_here], (0,), held, 2, [from_core], jnp.bfloat16)
    from_chip = swap(chip_out, "chan", chans, 2)
    (own,) = emit([rows_here], (0,), held, 0, [near_sum], jnp.float32)
    return (own + from_chip.astype(jnp.float32)).astype(jnp.bfloat16)


def solution(mesh):
    in_specs = (
        P("seq", "chan"),
        P("seq", None, "chan"),
        P(None, None, "chan"),
        P("chan"),
        P("seq", "chan"),
        P("chan", None),
    )
    out_specs = P("seq", "chan")
    seq, chans = mesh.shape["seq"], mesh.shape["chan"]
    chosen = fast_body if seq == 8 and chans == 4 else body
    return jax.shard_map(chosen, mesh=mesh, in_specs=in_specs, out_specs=out_specs, check_vma=False)
```
